32 devices in a mesh: grp: 8 (over z, y), tok: 4 (over x, core).
Axes of the slice: x: 2, y: 2, z: 4, core: 2. Of those that a mesh axis runs over, the one named last changes fastest.
Arguments:
- queries: bfloat16 [4096, 5120], P(('grp', 'tok')), may hold values from -6 to 6
- rotated_keys_values: bfloat16 [4096, 2048], P(('grp', 'tok')), may hold values from -6 to 6
- prompt_window_index: int32 [8, 512], P('grp', 'tok'), may hold values from 0 to 1, never falling along the last dimension, each value on 1 to 384 neighbouring positions
- residual: bfloat16 [4096, 5120], P(('grp', 'tok')), may hold values from -8 to 8
- ffn_gain: float32 [5120], replicated, may hold values from 0.1 to 1.9
- gate_weight: bfloat16 [5120, 8192], P(None, 'grp'), may hold values from -0.078125 to 0.078125
- up_weight: bfloat16 [5120, 8192], P(None, 'grp'), may hold values from -0.078125 to 0.078125
- paged_cache: bfloat16 [512, 16, 2048], P(('grp', 'tok')), may hold values from -6 to 6
- page_table: int32 [8, 64], P('grp'), may hold values from 0 to 63, each once within a row
Outputs:
- attended: bfloat16 [4096, 5120], P(('grp', 'tok'))
- hidden: bfloat16 [4096, 8192], P(('grp', 'tok'))
- cache_out: bfloat16 [512, 16, 2048], P(('grp', 'tok'))
The draws below stay inside these ranges and needn't reach their ends.
All inputs are finite; a program needn't handle non-finite values.
Results may differ from the reference program's by a relative error of at most 0.012.
Values may be sent and summed in bfloat16 or wider, within the bound.
No kernel may reach another device: no remote copies, remote signals or barrier semaphores. Data moves between devices by JAX's collectives and lax.ppermute only.
A program may use at most 128 MiB of HBM per device.

```python
import math
import jax
import jax.numpy as jnp
import numpy as np
from jax import lax

MODEL_WIDTH = 5120
QUERY_HEADS = 40
KEY_VALUE_HEADS = 8
HEAD_SIZE = 128
GATED_UNITS = 8192
TOK_DEV = 128
PAGE_TOKENS = 16
PROMPTS = 2
GT = 512
TOTAL_TOKENS = 4096
MOST = 384
GROUP_SLOTS = 64
N_GRP = 8
N_TOK = 4


def draw_queries(key, part):
    unrotated = jnp.clip(jax.random.normal(jax.random.fold_in(key, 1), (TOTAL_TOKENS, QUERY_HEADS * HEAD_SIZE), jnp.float32), -6.0, 6.0)
    return unrotated.astype(jnp.bfloat16)


def draw_rotated_keys_values(key, part):
    unrotated = jnp.clip(jax.random.normal(jax.random.fold_in(key, 2), (TOTAL_TOKENS, 2 * KEY_VALUE_HEADS * HEAD_SIZE), jnp.float32), -6.0, 6.0)
    return unrotated.astype(jnp.bfloat16)


def draw_residual(key, part):
    noise = jnp.clip(jax.random.normal(jax.random.fold_in(key, 3), (TOTAL_TOKENS, MODEL_WIDTH), jnp.float32), -6.0, 6.0)
    column_scale = jnp.exp(jax.random.uniform(jax.random.fold_in(key, 4), (MODEL_WIDTH,), jnp.float32, math.log(0.3), math.log(3.0)))
    spread = 0.7
    row_scale = jnp.exp(jax.random.uniform(jax.random.fold_in(key, 5), (TOTAL_TOKENS, 1), jnp.float32, -spread, spread))
    value = 0.25 * noise * column_scale * row_scale
    return jnp.clip(value, -8.0, 8.0).astype(jnp.bfloat16)


def levels(key, dims, cuts, least, top_value):
    factor_of = 1.0
    for dim, parts in cuts:
        heights = jax.random.uniform(jax.random.fold_in(jax.random.fold_in(key, 6), dim), (parts,), jnp.float32, least / len(cuts), top_value / len(cuts))
        factor_of = factor_of * jnp.repeat(jnp.exp(heights), dims[dim] // parts).reshape((-1,) + (1,) * (len(dims) - 1 - dim))
    return factor_of


def length_profile(number_of, total, bound, slope):
    portions = [(1 << 20) // math.isqrt(rank ** slope) + 1 for rank in range(2, number_of + 1)]
    surplus, holding = total - bound - (number_of - 1), [1] * (number_of - 1)
    while surplus > 0:
        movable = [i for i in range(number_of - 1) if holding[i] < bound]
        whole, left = sum([portions[i] for i in movable]), surplus
        for i in movable:
            extra = min(bound - holding[i], max(1, left * portions[i] // whole), surplus)
            holding[i] = holding[i] + extra
            surplus = surplus - extra
    return np.array([bound] + holding)


def uneven(rng, amount, total, most, lean):
    if amount == 2:
        one = jax.random.randint(rng, (), max(1, total - most), min(most, total - 1) + 1)
        return jnp.stack([one, total - one])
    sizes = jnp.asarray(length_profile(amount, total, most, lean), jnp.int32)
    twos = (amount - 1) // 2
    giver, sink = sizes[1:1 + 2 * twos:2], sizes[2:2 + 2 * twos:2]
    slack = jnp.minimum(giver - 1, most - sink)
    moved = jax.random.randint(jax.random.fold_in(rng, 1), (twos,), 0, 1 << 20) % (slack + 1)
    sizes = sizes.at[1:1 + 2 * twos:2].set(giver - moved).at[2:2 + 2 * twos:2].set(sink + moved)
    return sizes[jax.random.permutation(jax.random.fold_in(rng, 2), amount)]


def centred(key, shape, width, reach, cuts=(), held_as=jnp.bfloat16):
    level = levels(key, shape, cuts, -0.22, 0.18) if cuts else 1.0
    entries = jax.random.normal(key, shape, jnp.float32) * width * level
    return jnp.minimum(jnp.maximum(entries, -reach), reach).astype(held_as)


def setup_inputs(seed: int = 0) -> dict:
    keys = jax.random.split(jax.random.key(seed), 10)
    return {
        "queries": draw_queries(jax.random.fold_in(keys[9], 71), 0),
        "rotated_keys_values": draw_rotated_keys_values(jax.random.fold_in(keys[9], 71), 0),
        "prompt_window_index": jax.vmap(lambda own: jnp.searchsorted(jnp.cumsum(uneven(own, PROMPTS, GT, MOST, 2)), jnp.arange(GT), side="right"))(jax.random.split(keys[2], N_GRP)).reshape((N_GRP, GT)).astype(jnp.int32),
        "residual": draw_residual(jax.random.fold_in(keys[9], 71), 0),
        "ffn_gain": jnp.clip(1.0 + 0.18 * jax.random.normal(keys[4], (MODEL_WIDTH,), jnp.float32), 0.1, 1.9),
        "gate_weight": centred(keys[5], (MODEL_WIDTH, GATED_UNITS), MODEL_WIDTH ** -0.5, 0.078125, ((1, 8),)),
        "up_weight": centred(keys[6], (MODEL_WIDTH, GATED_UNITS), MODEL_WIDTH ** -0.5, 0.078125, ((1, 8),)),
        "paged_cache": centred(keys[7], (N_GRP * GROUP_SLOTS, PAGE_TOKENS, 2 * KEY_VALUE_HEADS * HEAD_SIZE), 1.0, 6.0, ((0, 32),)),
        "page_table": jax.vmap(lambda own: jax.random.permutation(own, GROUP_SLOTS))(jax.random.split(keys[8], N_GRP)).reshape((N_GRP, GROUP_SLOTS)).astype(jnp.int32),
    }


MASK_FILLER = -1e+30

def attend_group(group_query, group_key_value, group_seg):
    count_of_rows = group_query.shape[0]
    grouped_rows = group_query.reshape(count_of_rows, KEY_VALUE_HEADS, QUERY_HEADS // KEY_VALUE_HEADS, HEAD_SIZE).astype(jnp.float32)
    rows_of_keys = group_key_value[:, :KEY_VALUE_HEADS * HEAD_SIZE].reshape(count_of_rows, KEY_VALUE_HEADS, HEAD_SIZE).astype(jnp.float32)
    rows_of_values = group_key_value[:, KEY_VALUE_HEADS * HEAD_SIZE:].reshape(count_of_rows, KEY_VALUE_HEADS, HEAD_SIZE).astype(jnp.float32)
    scores = jnp.einsum('qgrd,kgd->qgrk', grouped_rows, rows_of_keys) * (1.0 / math.sqrt(HEAD_SIZE))
    position = jnp.arange(count_of_rows)
    live_mask = (group_seg[:, None] == group_seg[None, :]) & (position[None, :] <= position[:, None])
    live_mask = live_mask[:, None, None, :]
    scores = jnp.where(live_mask, scores, MASK_FILLER)
    row_max = lax.optimization_barrier(jnp.max(scores, axis=-1, keepdims=True))
    weights = jnp.where(live_mask, jnp.exp(scores - row_max), 0.0)
    denominator = lax.optimization_barrier(jnp.sum(weights, axis=-1))
    rounded = lax.optimization_barrier(weights.astype(jnp.bfloat16)).astype(jnp.float32)
    summed = jnp.einsum('qgrk,kgd->qgrd', rounded, rows_of_values) / denominator[..., None]
    return summed.reshape(count_of_rows, QUERY_HEADS * HEAD_SIZE).astype(jnp.bfloat16)

def reference(queries, rotated_keys_values, prompt_window_index, residual, ffn_gain, gate_weight, up_weight, paged_cache, page_table):
    rows_of_group = TOK_DEV * N_TOK

    def single_group(group_items):
        group_query, group_key_value, group_seg, group_res = group_items
        attention = attend_group(group_query, group_key_value, group_seg)
        attended = (group_res.astype(jnp.float32) + attention.astype(jnp.float32)).astype(jnp.bfloat16)
        widened = attended.astype(jnp.float32)
        normed = (widened * lax.rsqrt(lax.optimization_barrier(jnp.mean(widened * widened, axis=-1, keepdims=True)) + 1e-06) * ffn_gain).astype(jnp.bfloat16)
        gate_sum = jnp.dot(normed, gate_weight, preferred_element_type=jnp.float32)
        up_sum = jnp.dot(normed, up_weight, preferred_element_type=jnp.float32)
        hidden = (jax.nn.silu(gate_sum) * up_sum).astype(jnp.bfloat16)
        return (attended, hidden)
    attended, hidden = lax.map(single_group, (queries.reshape(N_GRP, rows_of_group, QUERY_HEADS * HEAD_SIZE), rotated_keys_values.reshape(N_GRP, rows_of_group, 2 * KEY_VALUE_HEADS * HEAD_SIZE), prompt_window_index, residual.reshape(N_GRP, rows_of_group, MODEL_WIDTH)))
    cache_slot_index = paged_cache.reshape(N_GRP, GROUP_SLOTS, PAGE_TOKENS, 2 * KEY_VALUE_HEADS * HEAD_SIZE)
    newly_written_pages = rotated_keys_values.reshape(N_GRP, rows_of_group // PAGE_TOKENS, PAGE_TOKENS, 2 * KEY_VALUE_HEADS * HEAD_SIZE)
    used_pages = rows_of_group // PAGE_TOKENS

    def write_pages(slots_of_group, table_row, pages_of_group):
        return slots_of_group.at[table_row[:used_pages]].set(pages_of_group)
    cache_slot_index = jax.vmap(write_pages)(cache_slot_index, page_table, newly_written_pages)
    return (attended.reshape(TOTAL_TOKENS, MODEL_WIDTH), hidden.reshape(TOTAL_TOKENS, GATED_UNITS), cache_slot_index.reshape(N_GRP * GROUP_SLOTS, PAGE_TOKENS, 2 * KEY_VALUE_HEADS * HEAD_SIZE))
```

```python
import math

import jax
import jax.numpy as jnp
from jax import lax
from jax.sharding import PartitionSpec as P

QUERY_HEADS = 40
KEY_VALUE_HEADS = 8
HEAD_SIZE = 128
PAGE_TOKENS = 16


MASK_FILLER = -1e30


def on_device(
    queries,
    rotated_keys_values,
    prompt_window_index,
    residual,
    ffn_gain,
    gate_weight,
    up_weight,
    paged_cache,
    page_table,
):
    count_of_rows = queries.shape[0]
    kv_width = rotated_keys_values.shape[1]
    group_split = QUERY_HEADS // KEY_VALUE_HEADS
    slot_count = paged_cache.shape[0]
    tok_index = lax.axis_index("tok")
    first_row = tok_index * count_of_rows
    grouped_rows = queries.reshape(count_of_rows, KEY_VALUE_HEADS, group_split, HEAD_SIZE)
    own_segment = prompt_window_index[0]
    own_place = first_row + jnp.arange(count_of_rows)
    slot_table = page_table[0]
    score_scale = 1.0 / math.sqrt(HEAD_SIZE)
    initial = (
        jnp.full((count_of_rows, KEY_VALUE_HEADS, group_split), MASK_FILLER, jnp.float32),
        jnp.zeros((count_of_rows, KEY_VALUE_HEADS, group_split), jnp.float32),
        jnp.zeros((count_of_rows, KEY_VALUE_HEADS, group_split, HEAD_SIZE), jnp.float32),
        paged_cache,
    )
    key_value_portion = lax.all_gather(rotated_keys_values, "tok", axis=0, tiled=True)
    seg_piece = lax.all_gather(own_segment, "tok", axis=0, tiled=True)
    count_of_keys = key_value_portion.shape[0]
    rows_of_keys = key_value_portion[:, : KEY_VALUE_HEADS * HEAD_SIZE].reshape(
        count_of_keys, KEY_VALUE_HEADS, HEAD_SIZE
    )
    rows_of_values = key_value_portion[:, KEY_VALUE_HEADS * HEAD_SIZE :].reshape(
        count_of_keys, KEY_VALUE_HEADS, HEAD_SIZE
    )
    key_place = jnp.arange(count_of_keys)
    live_mask = (seg_piece[None, :] == own_segment[:, None]) & (
        key_place[None, :] <= own_place[:, None]
    )
    running = (initial[0], initial[1], initial[2])
    run_max, run_sum, partial_value = running
    scores = (
        jnp.einsum("qgrd,kgd->qgrk", grouped_rows, rows_of_keys, preferred_element_type=jnp.float32)
        * score_scale
    )
    scores = jnp.where(live_mask[:, None, None, :], scores, MASK_FILLER)
    new_max = jnp.maximum(run_max, jnp.max(scores, axis=-1))
    weights = jnp.where(live_mask[:, None, None, :], jnp.exp(scores - new_max[..., None]), 0.0)
    run_sum = jnp.sum(weights, axis=-1)
    partial_value = jnp.einsum(
        "qgrk,kgd->qgrd",
        weights.astype(jnp.bfloat16),
        rows_of_values,
        preferred_element_type=jnp.float32,
    )
    running = (new_max, run_sum, partial_value)
    page_count = count_of_keys // PAGE_TOKENS
    targets = (
        lax.dynamic_slice_in_dim(slot_table, jnp.int32(0) // PAGE_TOKENS, page_count)
        - tok_index * slot_count
    )
    onehot = targets[None, :] == jnp.arange(slot_count)[:, None]
    placed = jnp.dot(
        onehot.astype(jnp.bfloat16),
        key_value_portion.reshape(page_count, PAGE_TOKENS * kv_width),
        preferred_element_type=jnp.float32,
    )
    placed = placed.astype(jnp.bfloat16).reshape(slot_count, PAGE_TOKENS, kv_width)
    written = jnp.where(jnp.any(onehot, axis=1)[:, None, None], placed, initial[3])
    run_sum = running[1]
    partial_value = running[2]
    attention = (
        (partial_value / run_sum[..., None])
        .reshape(count_of_rows, QUERY_HEADS * HEAD_SIZE)
        .astype(jnp.bfloat16)
    )
    attended = (residual.astype(jnp.float32) + attention.astype(jnp.float32)).astype(jnp.bfloat16)
    widened = attended.astype(jnp.float32)
    normed = (
        widened * lax.rsqrt(jnp.mean(widened * widened, axis=-1, keepdims=True) + 1e-06) * ffn_gain
    ).astype(jnp.bfloat16)
    shards = lax.all_gather(normed, "grp", axis=0, tiled=True)
    gate_sum = jnp.dot(shards, gate_weight, preferred_element_type=jnp.float32)
    up_sum = jnp.dot(shards, up_weight, preferred_element_type=jnp.float32)
    produced = (jax.nn.silu(gate_sum) * up_sum).astype(jnp.bfloat16)
    hidden = lax.all_to_all(produced, "grp", split_axis=0, concat_axis=1, tiled=True)
    return (attended, hidden, written)


def solution(mesh):
    in_specs = (
        P(("grp", "tok"), None),
        P(("grp", "tok"), None),
        P("grp", "tok"),
        P(("grp", "tok"), None),
        P(),
        P(None, "grp"),
        P(None, "grp"),
        P(("grp", "tok"), None, None),
        P("grp", None),
    )
    out_specs = (P(("grp", "tok"), None), P(("grp", "tok"), None), P(("grp", "tok"), None, None))
    return jax.shard_map(
        on_device, mesh=mesh, in_specs=in_specs, out_specs=out_specs, check_vma=False
    )
```

```python
import math

import jax
import jax.numpy as jnp
from jax import lax
from jax.experimental import pallas as pl
from jax.experimental.pallas import tpu as pltpu
from jax.sharding import PartitionSpec as P

QUERY_HEADS = 40
KEY_VALUE_HEADS = 8
HEAD_SIZE = 128
PAGE_TOKENS = 16


MASK_FILLER = -1e30


def ring_order(count):
    return list(range(0, 1)) + list(range(1, count, 2)) + list(range((count - 1) // 2 * 2, 0, -2))


def ring_tables(count):
    order = ring_order(count)
    spot = {place: i for i, place in enumerate(order)}
    return [[order[(spot[z] + s) % count] for z in range(count)] for s in range(count)]


def gated_kernel(own_ref, other_ref, gate_ref, up_ref, own_out, other_out, rows_ref):
    half = own_ref.shape[0]

    @pl.when(pl.program_id(0) == 0)
    def _():
        rows_ref[:half] = own_ref[...]
        rows_ref[half:] = other_ref[...]

    rows = rows_ref[...]
    gate_sum = jnp.dot(rows, gate_ref[...], preferred_element_type=jnp.float32)
    up_sum = jnp.dot(rows, up_ref[...], preferred_element_type=jnp.float32)
    made = (gate_sum / (1.0 + jnp.exp(-gate_sum)) * up_sum).astype(jnp.bfloat16)
    own_out[...] = made[:half]
    other_out[...] = made[half:]


def gated(own, other, gate_weight, up_weight):
    rows, width = own.shape
    units = gate_weight.shape[1]
    block = 256
    whole = pl.BlockSpec((rows, width), lambda i: (0, 0))
    columns = pl.BlockSpec((width, block), lambda i: (0, i))
    out = pl.BlockSpec((rows, block), lambda i: (0, i))
    shape = jax.ShapeDtypeStruct((rows, units), jnp.bfloat16)
    return pl.pallas_call(
        gated_kernel,
        grid=(units // block,),
        in_specs=[whole, whole, columns, columns],
        out_specs=[out, out],
        out_shape=[shape, shape],
        scratch_shapes=[pltpu.VMEM((2 * rows, width), jnp.bfloat16)],
        compiler_params=pltpu.CompilerParams(vmem_limit_bytes=48 * 1024 * 1024),
        cost_estimate=pl.CostEstimate(
            flops=8 * rows * width * units,
            bytes_accessed=4 * width * units + 4 * rows * (width + units),
            transcendentals=2 * rows * units,
        ),
    )(own, other, gate_weight, up_weight)


def on_device(
    queries,
    rotated_keys_values,
    prompt_window_index,
    residual,
    ffn_gain,
    gate_weight,
    up_weight,
    paged_cache,
    page_table,
):
    count_of_rows = queries.shape[0]
    kv_width = rotated_keys_values.shape[1]
    group_split = QUERY_HEADS // KEY_VALUE_HEADS
    slot_count = paged_cache.shape[0]
    tok_index = lax.axis_index("tok")
    first_row = tok_index * count_of_rows
    grouped_rows = queries.reshape(count_of_rows, KEY_VALUE_HEADS, group_split, HEAD_SIZE)
    own_segment = prompt_window_index[0]
    own_place = first_row + jnp.arange(count_of_rows)
    slot_table = page_table[0]
    score_scale = 1.0 / math.sqrt(HEAD_SIZE)
    initial = (
        jnp.full((count_of_rows, KEY_VALUE_HEADS, group_split), MASK_FILLER, jnp.float32),
        jnp.zeros((count_of_rows, KEY_VALUE_HEADS, group_split), jnp.float32),
        jnp.zeros((count_of_rows, KEY_VALUE_HEADS, group_split, HEAD_SIZE), jnp.float32),
        paged_cache,
    )
    key_value_portion = lax.all_gather(rotated_keys_values, "tok", axis=0, tiled=True)
    seg_piece = lax.all_gather(own_segment, "tok", axis=0, tiled=True)
    count_of_keys = key_value_portion.shape[0]
    rows_of_keys = key_value_portion[:, : KEY_VALUE_HEADS * HEAD_SIZE].reshape(
        count_of_keys, KEY_VALUE_HEADS, HEAD_SIZE
    )
    rows_of_values = key_value_portion[:, KEY_VALUE_HEADS * HEAD_SIZE :].reshape(
        count_of_keys, KEY_VALUE_HEADS, HEAD_SIZE
    )
    key_place = jnp.arange(count_of_keys)
    live_mask = (seg_piece[None, :] == own_segment[:, None]) & (
        key_place[None, :] <= own_place[:, None]
    )
    running = (initial[0], initial[1], initial[2])
    run_max, run_sum, partial_value = running
    scores = (
        jnp.einsum("qgrd,kgd->qgrk", grouped_rows, rows_of_keys, preferred_element_type=jnp.float32)
        * score_scale
    )
    scores = jnp.where(live_mask[:, None, None, :], scores, MASK_FILLER)
    new_max = jnp.maximum(run_max, jnp.max(scores, axis=-1))
    weights = jnp.where(live_mask[:, None, None, :], jnp.exp(scores - new_max[..., None]), 0.0)
    run_sum = jnp.sum(weights, axis=-1)
    partial_value = jnp.einsum(
        "qgrk,kgd->qgrd",
        weights.astype(jnp.bfloat16),
        rows_of_values,
        preferred_element_type=jnp.float32,
    )
    running = (new_max, run_sum, partial_value)
    page_count = count_of_keys // PAGE_TOKENS
    targets = (
        lax.dynamic_slice_in_dim(slot_table, jnp.int32(0) // PAGE_TOKENS, page_count)
        - tok_index * slot_count
    )
    onehot = targets[None, :] == jnp.arange(slot_count)[:, None]
    placed = jnp.dot(
        onehot.astype(jnp.bfloat16),
        key_value_portion.reshape(page_count, PAGE_TOKENS * kv_width),
        preferred_element_type=jnp.float32,
    )
    placed = placed.astype(jnp.bfloat16).reshape(slot_count, PAGE_TOKENS, kv_width)
    written = jnp.where(jnp.any(onehot, axis=1)[:, None, None], placed, initial[3])
    run_sum = running[1]
    partial_value = running[2]
    attention = (
        (partial_value / run_sum[..., None])
        .reshape(count_of_rows, QUERY_HEADS * HEAD_SIZE)
        .astype(jnp.bfloat16)
    )
    attended = (residual.astype(jnp.float32) + attention.astype(jnp.float32)).astype(jnp.bfloat16)
    widened = attended.astype(jnp.float32)
    normed = (
        widened * lax.rsqrt(jnp.mean(widened * widened, axis=-1, keepdims=True) + 1e-06) * ffn_gain
    ).astype(jnp.bfloat16)
    grp_count = lax.axis_size("grp")
    grp_index = lax.axis_index("grp")
    line, column = grp_index // 2, grp_index % 2
    line_count = grp_count // 2
    ahead = ring_tables(line_count)
    units = gate_weight.shape[1]

    def send(array, steps, flip):
        pairs = []
        for z in range(line_count):
            for y in range(2):
                pairs.append((2 * z + y, 2 * ahead[steps][z] + (1 - y if flip else y)))
        return lax.ppermute(array, "grp", pairs)

    hidden = jnp.zeros((count_of_rows, grp_count * units), jnp.bfloat16)

    def place(hidden, block, steps, flip):
        source = jnp.asarray(ahead[steps], jnp.int32)[line] * 2 + (1 - column if flip else column)
        return lax.dynamic_update_slice_in_dim(hidden, block, source * units, 1)

    held = normed
    for step in range(line_count):
        other = send(held, 0, True)
        following = send(held, 1, False) if step + 1 < line_count else None
        own_block, other_block = gated(held, other, gate_weight, up_weight)
        if step:
            own_block = send(own_block, line_count - step, False)
        other_block = send(other_block, (line_count - step) % line_count, True)
        hidden = place(hidden, own_block, step, False)
        hidden = place(hidden, other_block, step, True)
        held = following
    return (attended, hidden, written)


def solution(mesh):
    in_specs = (
        P(("grp", "tok"), None),
        P(("grp", "tok"), None),
        P("grp", "tok"),
        P(("grp", "tok"), None),
        P(),
        P(None, "grp"),
        P(None, "grp"),
        P(("grp", "tok"), None, None),
        P("grp", None),
    )
    out_specs = (P(("grp", "tok"), None), P(("grp", "tok"), None), P(("grp", "tok"), None, None))
    return jax.shard_map(
        on_device, mesh=mesh, in_specs=in_specs, out_specs=out_specs, check_vma=False
    )
```

```python
import functools
import math

import jax
import jax.numpy as jnp
from jax import lax
from jax.experimental import pallas as pl
from jax.experimental.pallas import tpu as pltpu
from jax.sharding import PartitionSpec as P

QUERY_HEADS = 40
KEY_VALUE_HEADS = 8
HEAD_SIZE = 128
PAGE_TOKENS = 16
GROUP_SPLIT = QUERY_HEADS // KEY_VALUE_HEADS
HEAD_CHUNKS = (2, 2, 2, 2)
SEG_ROWS = 16
SCALE_COLUMNS = 128
MASK_FILLER = -1e30
MIB = 1024 * 1024


def ring_order(count):
    return [0] + list(range(1, count, 2)) + list(range((count - 1) // 2 * 2, 0, -2))


def ring_tables(count):
    order = ring_order(count)
    spot = {place: i for i, place in enumerate(order)}
    return [[order[(spot[z] + s) % count] for z in range(count)] for s in range(count)]


def pack_kernel(kv_ref, seg_ref, *out_refs):
    rows = kv_ref.shape[0]
    key_width = KEY_VALUE_HEADS * HEAD_SIZE
    first = 0
    for out_ref, heads in zip(out_refs, HEAD_CHUNKS):
        width = heads * HEAD_SIZE
        out_ref[:rows, :width] = kv_ref[:, first : first + width]
        out_ref[:rows, width:] = kv_ref[:, key_width + first : key_width + first + width]
        first += width
    ids = jnp.broadcast_to(seg_ref[...], (SEG_ROWS, rows)).astype(jnp.float32)
    tail = jnp.concatenate([ids] * (out_refs[0].shape[1] // rows), axis=1)
    out_refs[0][rows:, :] = tail.astype(jnp.bfloat16)


def pack(kv, seg):
    rows = kv.shape[0]
    shapes = [
        jax.ShapeDtypeStruct(
            (rows + (SEG_ROWS if i == 0 else 0), 2 * heads * HEAD_SIZE), jnp.bfloat16
        )
        for i, heads in enumerate(HEAD_CHUNKS)
    ]
    return pl.pallas_call(
        pack_kernel,
        out_shape=shapes,
        cost_estimate=pl.CostEstimate(flops=0, bytes_accessed=4 * kv.size, transcendentals=0),
    )(kv, seg)


def attend_kernel(chunk, shard_count, width_all, *refs):
    heads = HEAD_CHUNKS[chunk]
    first, last = chunk == 0, chunk == len(HEAD_CHUNKS) - 1
    refs = list(refs)
    q_ref, res_ref, gain_ref = refs[:3]
    kv_refs = refs[3 : 3 + shard_count]
    rest = refs[3 + shard_count :]
    rows = q_ref.shape[0]
    if first:
        place_ref, own_seg_ref = rest[:2]
        attended_ref, scaled_ref, square_ref, bias_ref = rest[2:]
        row = lax.broadcasted_iota(jnp.int32, (rows, rows), 0)
        col = lax.broadcasted_iota(jnp.int32, (rows, rows), 1)
        place = place_ref[0]
        for m in range(shard_count):
            ids = kv_refs[m][rows:, :rows].astype(jnp.float32)[:1]
            apart = ((place ^ m) - place) * rows
            live = (own_seg_ref[...] == ids) & (col + apart <= row)
            bias_ref[:, m * rows : (m + 1) * rows] = jnp.where(live, 0.0, MASK_FILLER)
        total = jnp.zeros((rows, 1), jnp.float32)
    else:
        bias_ref, square_in, _ = rest[:3]
        attended_ref, scaled_ref = rest[3:5]
        square_ref = None if last else rest[5]
        total = square_in[:, :1]
    bias = bias_ref[...]
    bias = jnp.concatenate([bias] * GROUP_SPLIT, axis=0)
    for h in range(heads):
        keys = jnp.concatenate(
            [r[:rows, h * HEAD_SIZE : (h + 1) * HEAD_SIZE] for r in kv_refs], axis=0
        )
        values = jnp.concatenate(
            [r[:rows, (heads + h) * HEAD_SIZE : (heads + h + 1) * HEAD_SIZE] for r in kv_refs],
            axis=0,
        )
        base = h * GROUP_SPLIT * HEAD_SIZE
        query = jnp.concatenate(
            [q_ref[:, base + g * HEAD_SIZE : base + (g + 1) * HEAD_SIZE] for g in range(GROUP_SPLIT)],
            axis=0,
        )
        scores = lax.dot_general(
            query, keys, (((1,), (1,)), ((), ())), preferred_element_type=jnp.float32
        )
        scores = scores * (1.0 / math.sqrt(HEAD_SIZE)) + bias
        weights = jnp.exp(scores - jnp.max(scores, axis=1, keepdims=True))
        denominator = jnp.sum(weights, axis=1, keepdims=True)
        summed = jnp.dot(weights.astype(jnp.bfloat16), values, preferred_element_type=jnp.float32)
        attention = (summed / denominator).astype(jnp.bfloat16).astype(jnp.float32)
        for g in range(GROUP_SPLIT):
            columns = slice(base + g * HEAD_SIZE, base + (g + 1) * HEAD_SIZE)
            attended = res_ref[:, columns].astype(jnp.float32) + attention[g * rows : (g + 1) * rows]
            attended = attended.astype(jnp.bfloat16)
            attended_ref[:, columns] = attended
            widened = attended.astype(jnp.float32)
            scaled_ref[:, columns] = (widened * gain_ref[:, columns]).astype(jnp.bfloat16)
            total = total + jnp.sum(widened * widened, axis=1, keepdims=True)
    if last:
        scale = lax.rsqrt(total * (1.0 / width_all) + 1e-06)
        high = scale.astype(jnp.bfloat16)
        low = (scale - high.astype(jnp.float32)).astype(jnp.bfloat16)
        lane = lax.broadcasted_iota(jnp.int32, (rows, SCALE_COLUMNS), 1)
        both = jnp.where(
            lane < SCALE_COLUMNS // 2, high.astype(jnp.float32), low.astype(jnp.float32)
        )
        scaled_ref[:, heads * GROUP_SPLIT * HEAD_SIZE :] = both.astype(jnp.bfloat16)
    else:
        square_ref[...] = jnp.broadcast_to(total, square_ref.shape)


def attend(chunk, queries, residual, gain, kv_chunks, place, own_seg, carried):
    heads = HEAD_CHUNKS[chunk]
    rows, width_all = queries.shape
    first, last = chunk == 0, chunk == len(HEAD_CHUNKS) - 1
    width = heads * GROUP_SPLIT * HEAD_SIZE
    before = sum(HEAD_CHUNKS[:chunk]) * GROUP_SPLIT * HEAD_SIZE
    assert before % width == 0
    shard_count = len(kv_chunks)

    def whole(shape):
        return pl.BlockSpec(shape, lambda i: (0, 0))

    columns = pl.BlockSpec((rows, width), lambda i: (0, before // width))
    in_specs = [columns, columns, pl.BlockSpec((1, width), lambda i: (0, before // width))]
    in_specs += [whole(a.shape) for a in kv_chunks]
    operands = [queries, residual, gain] + list(kv_chunks)
    sent = width + (SCALE_COLUMNS if last else 0)
    shapes = [
        jax.ShapeDtypeStruct((rows, width_all), jnp.bfloat16),
        jax.ShapeDtypeStruct((rows, sent), jnp.bfloat16),
    ]
    out_specs = [columns, whole((rows, sent))]
    square = jax.ShapeDtypeStruct((rows, 128), jnp.float32)
    bias = jax.ShapeDtypeStruct((rows, rows * shard_count), jnp.float32)
    aliases = {}
    if first:
        operands += [place, own_seg]
        in_specs += [pl.BlockSpec(memory_space=pltpu.SMEM), whole(own_seg.shape)]
        shapes += [square, bias]
        out_specs += [whole(square.shape), whole(bias.shape)]
    else:
        attended_so_far, square_so_far, bias_array = carried
        operands += [bias_array, square_so_far, attended_so_far]
        in_specs += [whole(bias.shape), whole(square.shape), pl.BlockSpec(memory_space=pl.ANY)]
        aliases = {len(operands) - 1: 0}
        if not last:
            shapes += [square]
            out_specs += [whole(square.shape)]
    keys = rows * shard_count
    return pl.pallas_call(
        functools.partial(attend_kernel, chunk, shard_count, width_all),
        grid=(1,),
        in_specs=in_specs,
        out_specs=out_specs,
        out_shape=shapes,
        input_output_aliases=aliases,
        compiler_params=pltpu.CompilerParams(vmem_limit_bytes=32 * MIB),
        cost_estimate=pl.CostEstimate(
            flops=4 * rows * width * keys,
            bytes_accessed=8 * rows * width + 4 * keys * heads * HEAD_SIZE,
            transcendentals=rows * keys * heads * GROUP_SPLIT,
        ),
    )(*operands)


def gated_kernel(shard_count, chunk_count, *refs):
    shards = [refs[i * chunk_count : (i + 1) * chunk_count] for i in range(shard_count)]
    rest = refs[shard_count * chunk_count :]
    gate_ref, up_ref = rest[:2]
    out_refs = rest[2 : 2 + shard_count]
    rows_ref, scale_ref = rest[2 + shard_count :]
    rows = shards[0][0].shape[0]

    @pl.when(pl.program_id(0) == 0)
    def _():
        for i, chunks in enumerate(shards):
            span = slice(i * rows, (i + 1) * rows)
            first = 0
            for j, ref in enumerate(chunks):
                width = ref.shape[1] - (SCALE_COLUMNS if j == chunk_count - 1 else 0)
                rows_ref[span, first : first + width] = ref[:, :width]
                first += width
            both = chunks[-1][:, -SCALE_COLUMNS:].astype(jnp.float32)
            scale = both[:, :1] + both[:, SCALE_COLUMNS // 2 : SCALE_COLUMNS // 2 + 1]
            scale_ref[span, :] = jnp.broadcast_to(scale, (rows, 128))

    tokens = rows_ref[...]
    scale = scale_ref[:, :1]
    gate_sum = jnp.dot(tokens, gate_ref[...], preferred_element_type=jnp.float32) * scale
    up_sum = jnp.dot(tokens, up_ref[...], preferred_element_type=jnp.float32) * scale
    made = (gate_sum / (1.0 + jnp.exp(-gate_sum)) * up_sum).astype(jnp.bfloat16)
    for i in range(shard_count):
        out_refs[i][...] = made[i * rows : (i + 1) * rows]


def gated(shards, gate_weight, up_weight):
    rows = shards[0][0].shape[0]
    width, units = gate_weight.shape
    block = 256
    count = len(shards)
    operands = [a for shard in shards for a in shard]
    columns = pl.BlockSpec((width, block), lambda i: (0, i))
    out = pl.BlockSpec((rows, block), lambda i: (0, i))
    shape = jax.ShapeDtypeStruct((rows, units), jnp.bfloat16)
    return pl.pallas_call(
        functools.partial(gated_kernel, count, len(shards[0])),
        grid=(units // block,),
        in_specs=[pl.BlockSpec(a.shape, lambda i: (0, 0)) for a in operands] + [columns] * 2,
        out_specs=[out] * count,
        out_shape=[shape] * count,
        scratch_shapes=[
            pltpu.VMEM((count * rows, width), jnp.bfloat16),
            pltpu.VMEM((count * rows, 128), jnp.float32),
        ],
        compiler_params=pltpu.CompilerParams(vmem_limit_bytes=40 * MIB),
        cost_estimate=pl.CostEstimate(
            flops=4 * count * rows * width * units,
            bytes_accessed=4 * width * units + 2 * count * rows * (width + units),
            transcendentals=count * rows * units,
        ),
    )(*operands, gate_weight, up_weight)


def cache_kernel(page_ref, kv_ref, cache_ref, out_ref, sems):
    slots = out_ref.shape[0]

    def fresh(i, page):
        rows = pl.ds(pl.multiple_of(page * PAGE_TOKENS, PAGE_TOKENS), PAGE_TOKENS)
        return pltpu.make_async_copy(kv_ref.at[rows], out_ref.at[i], sems.at[i])

    def kept(i):
        return pltpu.make_async_copy(cache_ref.at[i], out_ref.at[i], sems.at[i])

    for i in range(slots):
        page = page_ref[i]

        @pl.when(page >= 0)
        def _():
            fresh(i, page).start()

        @pl.when(page < 0)
        def _():
            kept(i).start()

    for i in range(slots):
        kept(i).wait()


def write_cache(pages, kv, cache):
    return pl.pallas_call(
        cache_kernel,
        in_specs=[
            pl.BlockSpec(memory_space=pltpu.SMEM),
            pl.BlockSpec(memory_space=pl.ANY),
            pl.BlockSpec(memory_space=pl.ANY),
        ],
        out_specs=pl.BlockSpec(memory_space=pl.ANY),
        out_shape=jax.ShapeDtypeStruct(cache.shape, cache.dtype),
        scratch_shapes=[pltpu.SemaphoreType.DMA((cache.shape[0],))],
        cost_estimate=pl.CostEstimate(flops=0, bytes_accessed=4 * cache.size, transcendentals=0),
    )(pages, kv, cache)


def on_device(
    queries,
    rotated_keys_values,
    prompt_window_index,
    residual,
    ffn_gain,
    gate_weight,
    up_weight,
    paged_cache,
    page_table,
):
    rows, width = queries.shape
    tok_index = lax.axis_index("tok")
    tok_count = lax.axis_size("tok")
    grp_index = lax.axis_index("grp")
    grp_count = lax.axis_size("grp")
    line, column = grp_index // 2, grp_index % 2
    line_count = grp_count // 2
    ahead = ring_tables(line_count)
    units = gate_weight.shape[1]
    chunks = range(len(HEAD_CHUNKS))

    def swap(array, mask):
        return lax.ppermute(array, "tok", [(t, t ^ mask) for t in range(tok_count)])

    def send(array, steps, flip):
        pairs = []
        for z in range(line_count):
            for y in range(2):
                pairs.append((2 * z + y, 2 * ahead[steps][z] + (1 - y if flip else y)))
        return lax.ppermute(array, "grp", pairs)

    packed = pack(rotated_keys_values, prompt_window_index)
    group_chunks = []
    for c in chunks:
        held = {0: packed[c]}
        mask = tok_count // 2
        while mask:
            held.update({m ^ mask: swap(a, mask) for m, a in held.items()})
            mask //= 2
        group_chunks.append([held[m] for m in range(tok_count)])

    own_seg = jnp.broadcast_to(prompt_window_index[0].astype(jnp.float32)[:, None], (rows, rows))
    place = tok_index.astype(jnp.int32).reshape(1)
    gain = ffn_gain.reshape(1, width)
    scaled, carried = [], None
    for c in chunks:
        made = attend(c, queries, residual, gain, group_chunks[c], place, own_seg, carried)
        if c == 0:
            bias = made[3]
        if c < len(HEAD_CHUNKS) - 1:
            carried = (made[0], made[2], bias)
        scaled.append(made[1])
    attended = made[0]

    late_kv, _ = lax.optimization_barrier((rotated_keys_values, scaled[-1]))
    group_kv = lax.all_gather(late_kv, "tok", axis=0, tiled=True)
    slot_count = paged_cache.shape[0]
    page_count = group_kv.shape[0] // PAGE_TOKENS
    targets = page_table[0, :page_count] - tok_index * slot_count
    onehot = targets[None, :] == jnp.arange(slot_count)[:, None]
    page = jnp.where(onehot, jnp.arange(page_count, dtype=jnp.int32)[None, :] + 1, 0)
    pages = jnp.max(page, axis=1) - 1
    written = write_cache(pages, group_kv, paged_cache)

    hidden = jnp.zeros((rows, grp_count * units), jnp.bfloat16)

    def put(hidden, block, steps, flip):
        source = jnp.asarray(ahead[steps], jnp.int32)[line] * 2 + (1 - column if flip else column)
        return lax.dynamic_update_slice_in_dim(hidden, block, source * units, 1)

    held = scaled
    for step in range(line_count):
        other, following = [], []
        for c in chunks:
            swapped = send(held[c], 0, True)
            if step + 1 < line_count:
                forwarded = send(held[c], 1, False)
                swapped, forwarded = lax.optimization_barrier((swapped, forwarded))
                following.append(forwarded)
            other.append(swapped)
        own_block, other_block = gated([held, other], gate_weight, up_weight)
        if step:
            own_block = send(own_block, line_count - step, False)
        other_block = send(other_block, (line_count - step) % line_count, True)
        hidden = put(hidden, own_block, step, False)
        hidden = put(hidden, other_block, step, True)
        held = following
    return (attended, hidden, written)


def solution(mesh):
    in_specs = (
        P(("grp", "tok"), None),
        P(("grp", "tok"), None),
        P("grp", "tok"),
        P(("grp", "tok"), None),
        P(),
        P(None, "grp"),
        P(None, "grp"),
        P(("grp", "tok"), None, None),
        P("grp", None),
    )
    out_specs = (P(("grp", "tok"), None), P(("grp", "tok"), None), P(("grp", "tok"), None, None))
    return jax.shard_map(
        on_device, mesh=mesh, in_specs=in_specs, out_specs=out_specs, check_vma=False
    )
```

```python
import functools
import math

import jax
import jax.numpy as jnp
from jax import lax
from jax.experimental import pallas as pl
from jax.experimental.pallas import tpu as pltpu
from jax.sharding import PartitionSpec as P

QUERY_HEADS = 40
KEY_VALUE_HEADS = 8
HEAD_SIZE = 128
PAGE_TOKENS = 16
GROUP_SPLIT = QUERY_HEADS // KEY_VALUE_HEADS
HEAD_CHUNKS = (2, 2, 2, 2)
SEG_ROWS = 16
SCALE_COLUMNS = 128
MASK_FILLER = -1e30
VMEM_LIMIT = 60 * 1024 * 1024


def ring_order(count):
    return [0] + list(range(1, count, 2)) + list(range((count - 1) // 2 * 2, 0, -2))


def ring_tables(count):
    order = ring_order(count)
    spot = {place: i for i, place in enumerate(order)}
    return [[order[(spot[z] + s) % count] for z in range(count)] for s in range(count)]


def pack_kernel(kv_ref, seg_ref, *out_refs):
    rows = kv_ref.shape[0]
    key_width = KEY_VALUE_HEADS * HEAD_SIZE
    first = 0
    for out_ref, heads in zip(out_refs, HEAD_CHUNKS):
        width = heads * HEAD_SIZE
        out_ref[:rows, :width] = kv_ref[:, first : first + width]
        out_ref[:rows, width:] = kv_ref[:, key_width + first : key_width + first + width]
        first += width
    ids = jnp.broadcast_to(seg_ref[...], (SEG_ROWS, rows)).astype(jnp.float32)
    tail = jnp.concatenate([ids] * (out_refs[0].shape[1] // rows), axis=1)
    out_refs[0][rows:, :] = tail.astype(jnp.bfloat16)


def pack(kv, seg):
    rows = kv.shape[0]
    shapes = [
        jax.ShapeDtypeStruct(
            (rows + (SEG_ROWS if i == 0 else 0), 2 * heads * HEAD_SIZE), jnp.bfloat16
        )
        for i, heads in enumerate(HEAD_CHUNKS)
    ]
    return pl.pallas_call(
        pack_kernel,
        out_shape=shapes,
        compiler_params=pltpu.CompilerParams(vmem_limit_bytes=VMEM_LIMIT),
        cost_estimate=pl.CostEstimate(flops=0, bytes_accessed=4 * kv.size, transcendentals=0),
    )(kv, seg)


def attend_kernel(chunk, shard_count, width_all, *refs):
    heads = HEAD_CHUNKS[chunk]
    first, last = chunk == 0, chunk == len(HEAD_CHUNKS) - 1
    refs = list(refs)
    q_ref, res_ref, gain_ref = refs[:3]
    kv_refs = refs[3 : 3 + shard_count]
    rest = refs[3 + shard_count :]
    rows = q_ref.shape[0]
    if first:
        place_ref, own_seg_ref = rest[:2]
        attended_ref, scaled_ref, square_ref, bias_ref = rest[2:]
        row = lax.broadcasted_iota(jnp.int32, (rows, rows), 0)
        col = lax.broadcasted_iota(jnp.int32, (rows, rows), 1)
        place = place_ref[0]
        for m in range(shard_count):
            ids = kv_refs[m][rows:, :rows].astype(jnp.float32)[:1]
            apart = ((place ^ m) - place) * rows
            live = (own_seg_ref[...] == ids) & (col + apart <= row)
            bias_ref[:, m * rows : (m + 1) * rows] = jnp.where(live, 0.0, MASK_FILLER)
        total = jnp.zeros((rows, 1), jnp.float32)
    else:
        bias_ref, square_in, _ = rest[:3]
        attended_ref, scaled_ref = rest[3:5]
        square_ref = None if last else rest[5]
        total = square_in[:, :1]
    bias = bias_ref[...]
    bias = jnp.concatenate([bias] * GROUP_SPLIT, axis=0)
    for h in range(heads):
        keys = jnp.concatenate(
            [r[:rows, h * HEAD_SIZE : (h + 1) * HEAD_SIZE] for r in kv_refs], axis=0
        )
        values = jnp.concatenate(
            [r[:rows, (heads + h) * HEAD_SIZE : (heads + h + 1) * HEAD_SIZE] for r in kv_refs],
            axis=0,
        )
        base = h * GROUP_SPLIT * HEAD_SIZE
        query = jnp.concatenate(
            [q_ref[:, base + g * HEAD_SIZE : base + (g + 1) * HEAD_SIZE] for g in range(GROUP_SPLIT)],
            axis=0,
        )
        scores = lax.dot_general(
            query, keys, (((1,), (1,)), ((), ())), preferred_element_type=jnp.float32
        )
        scores = scores * (1.0 / math.sqrt(HEAD_SIZE)) + bias
        weights = jnp.exp(scores - jnp.max(scores, axis=1, keepdims=True))
        denominator = jnp.sum(weights, axis=1, keepdims=True)
        summed = jnp.dot(weights.astype(jnp.bfloat16), values, preferred_element_type=jnp.float32)
        attention = (summed / denominator).astype(jnp.bfloat16).astype(jnp.float32)
        for g in range(GROUP_SPLIT):
            columns = slice(base + g * HEAD_SIZE, base + (g + 1) * HEAD_SIZE)
            attended = res_ref[:, columns].astype(jnp.float32) + attention[g * rows : (g + 1) * rows]
            attended = attended.astype(jnp.bfloat16)
            attended_ref[:, columns] = attended
            widened = attended.astype(jnp.float32)
            scaled_ref[:, columns] = (widened * gain_ref[:, columns]).astype(jnp.bfloat16)
            total = total + jnp.sum(widened * widened, axis=1, keepdims=True)
    if last:
        scale = lax.rsqrt(total * (1.0 / width_all) + 1e-06)
        high = scale.astype(jnp.bfloat16)
        low = (scale - high.astype(jnp.float32)).astype(jnp.bfloat16)
        lane = lax.broadcasted_iota(jnp.int32, (rows, SCALE_COLUMNS), 1)
        both = jnp.where(
            lane < SCALE_COLUMNS // 2, high.astype(jnp.float32), low.astype(jnp.float32)
        )
        scaled_ref[:, heads * GROUP_SPLIT * HEAD_SIZE :] = both.astype(jnp.bfloat16)
    else:
        square_ref[...] = jnp.broadcast_to(total, square_ref.shape)


def attend(chunk, queries, residual, gain, kv_chunks, place, own_seg, carried):
    heads = HEAD_CHUNKS[chunk]
    rows, width_all = queries.shape
    first, last = chunk == 0, chunk == len(HEAD_CHUNKS) - 1
    width = heads * GROUP_SPLIT * HEAD_SIZE
    before = sum(HEAD_CHUNKS[:chunk]) * GROUP_SPLIT * HEAD_SIZE
    assert before % width == 0
    shard_count = len(kv_chunks)

    def whole(shape):
        return pl.BlockSpec(shape, lambda i: (0, 0))

    columns = pl.BlockSpec((rows, width), lambda i: (0, before // width))
    in_specs = [columns, columns, pl.BlockSpec((1, width), lambda i: (0, before // width))]
    in_specs += [whole(a.shape) for a in kv_chunks]
    operands = [queries, residual, gain] + list(kv_chunks)
    sent = width + (SCALE_COLUMNS if last else 0)
    shapes = [
        jax.ShapeDtypeStruct((rows, width_all), jnp.bfloat16),
        jax.ShapeDtypeStruct((rows, sent), jnp.bfloat16),
    ]
    out_specs = [columns, whole((rows, sent))]
    square = jax.ShapeDtypeStruct((rows, 128), jnp.float32)
    bias = jax.ShapeDtypeStruct((rows, rows * shard_count), jnp.float32)
    aliases = {}
    if first:
        operands += [place, own_seg]
        in_specs += [pl.BlockSpec(memory_space=pltpu.SMEM), whole(own_seg.shape)]
        shapes += [square, bias]
        out_specs += [whole(square.shape), whole(bias.shape)]
    else:
        attended_so_far, square_so_far, bias_array = carried
        operands += [bias_array, square_so_far, attended_so_far]
        in_specs += [whole(bias.shape), whole(square.shape), pl.BlockSpec(memory_space=pl.ANY)]
        aliases = {len(operands) - 1: 0}
        if not last:
            shapes += [square]
            out_specs += [whole(square.shape)]
    keys = rows * shard_count
    return pl.pallas_call(
        functools.partial(attend_kernel, chunk, shard_count, width_all),
        grid=(1,),
        in_specs=in_specs,
        out_specs=out_specs,
        out_shape=shapes,
        input_output_aliases=aliases,
        compiler_params=pltpu.CompilerParams(vmem_limit_bytes=VMEM_LIMIT),
        cost_estimate=pl.CostEstimate(
            flops=4 * rows * width * keys,
            bytes_accessed=8 * rows * width + 4 * keys * heads * HEAD_SIZE,
            transcendentals=rows * keys * heads * GROUP_SPLIT,
        ),
    )(*operands)


def gated_kernel(shard_count, chunk_count, *refs):
    shards = [refs[i * chunk_count : (i + 1) * chunk_count] for i in range(shard_count)]
    rest = refs[shard_count * chunk_count :]
    gate_ref, up_ref = rest[:2]
    out_refs = rest[2 : 2 + shard_count]
    rows_ref, scale_ref = rest[2 + shard_count :]
    rows = shards[0][0].shape[0]

    @pl.when(pl.program_id(0) == 0)
    def _():
        for i, chunks in enumerate(shards):
            span = slice(i * rows, (i + 1) * rows)
            first = 0
            for j, ref in enumerate(chunks):
                width = ref.shape[1] - (SCALE_COLUMNS if j == chunk_count - 1 else 0)
                rows_ref[span, first : first + width] = ref[:, :width]
                first += width
            both = chunks[-1][:, -SCALE_COLUMNS:].astype(jnp.float32)
            scale = both[:, :1] + both[:, SCALE_COLUMNS // 2 : SCALE_COLUMNS // 2 + 1]
            scale_ref[span, :] = jnp.broadcast_to(scale, (rows, 128))

    tokens = rows_ref[...]
    scale = scale_ref[:, :1]
    gate_sum = jnp.dot(tokens, gate_ref[...], preferred_element_type=jnp.float32) * scale
    up_sum = jnp.dot(tokens, up_ref[...], preferred_element_type=jnp.float32) * scale
    made = (gate_sum / (1.0 + jnp.exp(-gate_sum)) * up_sum).astype(jnp.bfloat16)
    for i in range(shard_count):
        out_refs[i][...] = made[i * rows : (i + 1) * rows]


def gated(shards, gate_weight, up_weight):
    rows = shards[0][0].shape[0]
    width, units = gate_weight.shape
    block = 256
    count = len(shards)
    operands = [a for shard in shards for a in shard]
    columns = pl.BlockSpec((width, block), lambda i: (0, i))
    out = pl.BlockSpec((rows, block), lambda i: (0, i))
    shape = jax.ShapeDtypeStruct((rows, units), jnp.bfloat16)
    return pl.pallas_call(
        functools.partial(gated_kernel, count, len(shards[0])),
        grid=(units // block,),
        in_specs=[pl.BlockSpec(a.shape, lambda i: (0, 0)) for a in operands] + [columns] * 2,
        out_specs=[out] * count,
        out_shape=[shape] * count,
        scratch_shapes=[
            pltpu.VMEM((count * rows, width), jnp.bfloat16),
            pltpu.VMEM((count * rows, 128), jnp.float32),
        ],
        compiler_params=pltpu.CompilerParams(vmem_limit_bytes=VMEM_LIMIT),
        cost_estimate=pl.CostEstimate(
            flops=4 * count * rows * width * units,
            bytes_accessed=4 * width * units + 2 * count * rows * (width + units),
            transcendentals=count * rows * units,
        ),
    )(*operands, gate_weight, up_weight)


def cache_kernel(page_ref, kv_ref, cache_ref, out_ref):
    for i in range(out_ref.shape[0]):
        page = page_ref[i]

        @pl.when(page >= 0)
        def _():
            first = pl.multiple_of(jnp.maximum(page, 0) * PAGE_TOKENS, PAGE_TOKENS)
            out_ref[i] = kv_ref[pl.ds(first, PAGE_TOKENS), :]

        @pl.when(page < 0)
        def _():
            out_ref[i] = cache_ref[i]


def write_cache(pages, kv, cache):
    return pl.pallas_call(
        cache_kernel,
        in_specs=[
            pl.BlockSpec(memory_space=pltpu.SMEM),
            pl.BlockSpec(memory_space=pltpu.VMEM),
            pl.BlockSpec(memory_space=pltpu.VMEM),
        ],
        out_specs=pl.BlockSpec(memory_space=pltpu.VMEM),
        out_shape=jax.ShapeDtypeStruct(cache.shape, cache.dtype),
        compiler_params=pltpu.CompilerParams(vmem_limit_bytes=VMEM_LIMIT),
        cost_estimate=pl.CostEstimate(flops=0, bytes_accessed=8 * cache.size, transcendentals=0),
    )(pages, kv, cache)


def on_device(
    queries,
    rotated_keys_values,
    prompt_window_index,
    residual,
    ffn_gain,
    gate_weight,
    up_weight,
    paged_cache,
    page_table,
):
    rows, width = queries.shape
    tok_index = lax.axis_index("tok")
    tok_count = lax.axis_size("tok")
    grp_index = lax.axis_index("grp")
    grp_count = lax.axis_size("grp")
    line, column = grp_index // 2, grp_index % 2
    line_count = grp_count // 2
    ahead = ring_tables(line_count)
    units = gate_weight.shape[1]
    chunks = range(len(HEAD_CHUNKS))

    def swap(array, mask):
        return lax.ppermute(array, "tok", [(t, t ^ mask) for t in range(tok_count)])

    def send(array, steps, flip):
        pairs = []
        for z in range(line_count):
            for y in range(2):
                pairs.append((2 * z + y, 2 * ahead[steps][z] + (1 - y if flip else y)))
        return lax.ppermute(array, "grp", pairs)

    packed = pack(rotated_keys_values, prompt_window_index)
    group_chunks = []
    for c in chunks:
        held = {0: packed[c]}
        mask = tok_count // 2
        while mask:
            held.update({m ^ mask: swap(a, mask) for m, a in held.items()})
            mask //= 2
        group_chunks.append([held[m] for m in range(tok_count)])

    own_seg = jnp.broadcast_to(prompt_window_index[0].astype(jnp.float32)[:, None], (rows, rows))
    place = tok_index.astype(jnp.int32).reshape(1)
    gain = ffn_gain.reshape(1, width)
    scaled, carried = [], None
    for c in chunks:
        made = attend(c, queries, residual, gain, group_chunks[c], place, own_seg, carried)
        if c == 0:
            bias = made[3]
        if c < len(HEAD_CHUNKS) - 1:
            carried = (made[0], made[2], bias)
        scaled.append(made[1])
    attended = made[0]

    late_kv, _ = lax.optimization_barrier((rotated_keys_values, scaled[-1]))
    group_kv = lax.all_gather(late_kv, "tok", axis=0, tiled=True)
    slot_count = paged_cache.shape[0]
    page_count = group_kv.shape[0] // PAGE_TOKENS
    targets = page_table[0, :page_count] - tok_index * slot_count
    onehot = targets[None, :] == jnp.arange(slot_count)[:, None]
    page = jnp.where(onehot, jnp.arange(page_count, dtype=jnp.int32)[None, :] + 1, 0)
    pages = jnp.max(page, axis=1) - 1
    written = write_cache(pages, group_kv, paged_cache)

    hidden = jnp.zeros((rows, grp_count * units), jnp.bfloat16)

    def put(hidden, block, steps, flip):
        source = sum(jnp.where(line == z, ahead[steps][z] * 2, 0) for z in range(line_count))
        source = source + (1 - column if flip else column)
        return lax.dynamic_update_slice_in_dim(hidden, block, source * units, 1)

    held = scaled
    for step in range(line_count):
        other, following = [], []
        for c in chunks:
            swapped = send(held[c], 0, True)
            if step + 1 < line_count:
                forwarded = send(held[c], 1, False)
                swapped, forwarded = lax.optimization_barrier((swapped, forwarded))
                following.append(forwarded)
            other.append(swapped)
        if step + 1 < line_count:
            own_block, other_block = gated([held, other], gate_weight, up_weight)
        else:
            (own_block,) = gated([held], gate_weight, up_weight)
            other[-1], written = lax.optimization_barrier((other[-1], written))
            (other_block,) = gated([other], gate_weight, up_weight)
        if step:
            own_block = send(own_block, line_count - step, False)
        other_block = send(other_block, (line_count - step) % line_count, True)
        hidden = put(hidden, own_block, step, False)
        hidden = put(hidden, other_block, step, True)
        held = following
    return (attended, hidden, written)


def solution(mesh):
    in_specs = (
        P(("grp", "tok"), None),
        P(("grp", "tok"), None),
        P("grp", "tok"),
        P(("grp", "tok"), None),
        P(),
        P(None, "grp"),
        P(None, "grp"),
        P(("grp", "tok"), None, None),
        P("grp", None),
    )
    out_specs = (P(("grp", "tok"), None), P(("grp", "tok"), None), P(("grp", "tok"), None, None))
    return jax.shard_map(
        on_device, mesh=mesh, in_specs=in_specs, out_specs=out_specs, check_vma=False
    )
```

```python
import functools
import math

import jax
import jax.numpy as jnp
from jax import lax
from jax.experimental import pallas as pl
from jax.experimental.pallas import tpu as pltpu
from jax.sharding import PartitionSpec as P

QUERY_HEADS = 40
KEY_VALUE_HEADS = 8
HEAD_SIZE = 128
PAGE_TOKENS = 16
GROUP_SPLIT = QUERY_HEADS // KEY_VALUE_HEADS
HEAD_CHUNKS = (2, 2, 2, 2)
SEG_ROWS = 16
SCALE_COLUMNS = 128
MASK_FILLER = -1e30
VMEM_LIMIT = 28 * 1024 * 1024


def ring_order(count):
    return [0] + list(range(1, count, 2)) + list(range((count - 1) // 2 * 2, 0, -2))


def ring_tables(count):
    order = ring_order(count)
    spot = {place: i for i, place in enumerate(order)}
    return [[order[(spot[z] + s) % count] for z in range(count)] for s in range(count)]


def pack_kernel(kv_ref, seg_ref, *out_refs):
    rows = kv_ref.shape[0]
    key_width = KEY_VALUE_HEADS * HEAD_SIZE
    first = 0
    for out_ref, heads in zip(out_refs, HEAD_CHUNKS):
        width = heads * HEAD_SIZE
        out_ref[:rows, :width] = kv_ref[:, first : first + width]
        out_ref[:rows, width:] = kv_ref[:, key_width + first : key_width + first + width]
        first += width
    ids = jnp.broadcast_to(seg_ref[...], (SEG_ROWS, rows)).astype(jnp.float32)
    tail = jnp.concatenate([ids] * (out_refs[0].shape[1] // rows), axis=1)
    out_refs[0][rows:, :] = tail.astype(jnp.bfloat16)


def pack(kv, seg):
    rows = kv.shape[0]
    shapes = [
        jax.ShapeDtypeStruct(
            (rows + (SEG_ROWS if i == 0 else 0), 2 * heads * HEAD_SIZE), jnp.bfloat16
        )
        for i, heads in enumerate(HEAD_CHUNKS)
    ]
    return pl.pallas_call(
        pack_kernel,
        out_shape=shapes,
        compiler_params=pltpu.CompilerParams(vmem_limit_bytes=VMEM_LIMIT),
        cost_estimate=pl.CostEstimate(flops=0, bytes_accessed=4 * kv.size, transcendentals=0),
    )(kv, seg)


def attend_kernel(chunk, shard_count, width_all, *refs):
    heads = HEAD_CHUNKS[chunk]
    first, last = chunk == 0, chunk == len(HEAD_CHUNKS) - 1
    refs = list(refs)
    q_ref, res_ref, gain_ref = refs[:3]
    kv_refs = refs[3 : 3 + shard_count]
    rest = refs[3 + shard_count :]
    rows = q_ref.shape[0]
    if first:
        place_ref, own_seg_ref = rest[:2]
        attended_ref, scaled_ref, square_ref, bias_ref = rest[2:]
        row = lax.broadcasted_iota(jnp.int32, (rows, rows), 0)
        col = lax.broadcasted_iota(jnp.int32, (rows, rows), 1)
        place = place_ref[0]
        for m in range(shard_count):
            ids = kv_refs[m][rows:, :rows].astype(jnp.float32)[:1]
            apart = ((place ^ m) - place) * rows
            live = (own_seg_ref[...] == ids) & (col + apart <= row)
            bias_ref[:, m * rows : (m + 1) * rows] = jnp.where(live, 0.0, MASK_FILLER)
        total = jnp.zeros((rows, 1), jnp.float32)
    else:
        bias_ref, square_in, _ = rest[:3]
        attended_ref, scaled_ref = rest[3:5]
        square_ref = None if last else rest[5]
        total = square_in[:, :1]
    bias = bias_ref[...]
    bias = jnp.concatenate([bias] * GROUP_SPLIT, axis=0)
    for h in range(heads):
        keys = jnp.concatenate(
            [r[:rows, h * HEAD_SIZE : (h + 1) * HEAD_SIZE] for r in kv_refs], axis=0
        )
        values = jnp.concatenate(
            [r[:rows, (heads + h) * HEAD_SIZE : (heads + h + 1) * HEAD_SIZE] for r in kv_refs],
            axis=0,
        )
        base = h * GROUP_SPLIT * HEAD_SIZE
        query = jnp.concatenate(
            [q_ref[:, base + g * HEAD_SIZE : base + (g + 1) * HEAD_SIZE] for g in range(GROUP_SPLIT)],
            axis=0,
        )
        scores = lax.dot_general(
            query, keys, (((1,), (1,)), ((), ())), preferred_element_type=jnp.float32
        )
        scores = scores * (1.0 / math.sqrt(HEAD_SIZE)) + bias
        weights = jnp.exp(scores - jnp.max(scores, axis=1, keepdims=True))
        denominator = jnp.sum(weights, axis=1, keepdims=True)
        summed = jnp.dot(weights.astype(jnp.bfloat16), values, preferred_element_type=jnp.float32)
        attention = (summed / denominator).astype(jnp.bfloat16).astype(jnp.float32)
        for g in range(GROUP_SPLIT):
            columns = slice(base + g * HEAD_SIZE, base + (g + 1) * HEAD_SIZE)
            attended = res_ref[:, columns].astype(jnp.float32) + attention[g * rows : (g + 1) * rows]
            attended = attended.astype(jnp.bfloat16)
            attended_ref[:, columns] = attended
            widened = attended.astype(jnp.float32)
            scaled_ref[:, columns] = (widened * gain_ref[:, columns]).astype(jnp.bfloat16)
            total = total + jnp.sum(widened * widened, axis=1, keepdims=True)
    if last:
        scale = lax.rsqrt(total * (1.0 / width_all) + 1e-06)
        high = scale.astype(jnp.bfloat16)
        low = (scale - high.astype(jnp.float32)).astype(jnp.bfloat16)
        lane = lax.broadcasted_iota(jnp.int32, (rows, SCALE_COLUMNS), 1)
        both = jnp.where(
            lane < SCALE_COLUMNS // 2, high.astype(jnp.float32), low.astype(jnp.float32)
        )
        scaled_ref[:, heads * GROUP_SPLIT * HEAD_SIZE :] = both.astype(jnp.bfloat16)
    else:
        square_ref[...] = jnp.broadcast_to(total, square_ref.shape)


def attend(chunk, queries, residual, gain, kv_chunks, place, own_seg, carried):
    heads = HEAD_CHUNKS[chunk]
    rows, width_all = queries.shape
    first, last = chunk == 0, chunk == len(HEAD_CHUNKS) - 1
    width = heads * GROUP_SPLIT * HEAD_SIZE
    before = sum(HEAD_CHUNKS[:chunk]) * GROUP_SPLIT * HEAD_SIZE
    assert before % width == 0
    shard_count = len(kv_chunks)

    def whole(shape):
        return pl.BlockSpec(shape, lambda i: (0, 0))

    columns = pl.BlockSpec((rows, width), lambda i: (0, before // width))
    in_specs = [columns, columns, pl.BlockSpec((1, width), lambda i: (0, before // width))]
    in_specs += [whole(a.shape) for a in kv_chunks]
    operands = [queries, residual, gain] + list(kv_chunks)
    sent = width + (SCALE_COLUMNS if last else 0)
    shapes = [
        jax.ShapeDtypeStruct((rows, width_all), jnp.bfloat16),
        jax.ShapeDtypeStruct((rows, sent), jnp.bfloat16),
    ]
    out_specs = [columns, whole((rows, sent))]
    square = jax.ShapeDtypeStruct((rows, 128), jnp.float32)
    bias = jax.ShapeDtypeStruct((rows, rows * shard_count), jnp.float32)
    aliases = {}
    if first:
        operands += [place, own_seg]
        in_specs += [pl.BlockSpec(memory_space=pltpu.SMEM), whole(own_seg.shape)]
        shapes += [square, bias]
        out_specs += [whole(square.shape), whole(bias.shape)]
    else:
        attended_so_far, square_so_far, bias_array = carried
        operands += [bias_array, square_so_far, attended_so_far]
        in_specs += [whole(bias.shape), whole(square.shape), pl.BlockSpec(memory_space=pl.ANY)]
        aliases = {len(operands) - 1: 0}
        if not last:
            shapes += [square]
            out_specs += [whole(square.shape)]
    keys = rows * shard_count
    return pl.pallas_call(
        functools.partial(attend_kernel, chunk, shard_count, width_all),
        grid=(1,),
        in_specs=in_specs,
        out_specs=out_specs,
        out_shape=shapes,
        input_output_aliases=aliases,
        compiler_params=pltpu.CompilerParams(vmem_limit_bytes=VMEM_LIMIT),
        cost_estimate=pl.CostEstimate(
            flops=4 * rows * width * keys,
            bytes_accessed=8 * rows * width + 4 * keys * heads * HEAD_SIZE,
            transcendentals=rows * keys * heads * GROUP_SPLIT,
        ),
    )(*operands)


def gated_kernel(shard_count, chunk_count, *refs):
    shards = [refs[i * chunk_count : (i + 1) * chunk_count] for i in range(shard_count)]
    rest = refs[shard_count * chunk_count :]
    gate_ref, up_ref = rest[:2]
    out_refs = rest[2 : 2 + shard_count]
    rows_ref, scale_ref = rest[2 + shard_count :]
    rows = shards[0][0].shape[0]

    @pl.when(pl.program_id(0) == 0)
    def _():
        for i, chunks in enumerate(shards):
            span = slice(i * rows, (i + 1) * rows)
            first = 0
            for j, ref in enumerate(chunks):
                width = ref.shape[1] - (SCALE_COLUMNS if j == chunk_count - 1 else 0)
                rows_ref[span, first : first + width] = ref[:, :width]
                first += width
            both = chunks[-1][:, -SCALE_COLUMNS:].astype(jnp.float32)
            scale = both[:, :1] + both[:, SCALE_COLUMNS // 2 : SCALE_COLUMNS // 2 + 1]
            scale_ref[span, :] = jnp.broadcast_to(scale, (rows, 128))

    tokens = rows_ref[...]
    scale = scale_ref[:, :1]
    gate_sum = jnp.dot(tokens, gate_ref[...], preferred_element_type=jnp.float32) * scale
    up_sum = jnp.dot(tokens, up_ref[...], preferred_element_type=jnp.float32) * scale
    made = (gate_sum / (1.0 + jnp.exp(-gate_sum)) * up_sum).astype(jnp.bfloat16)
    for i in range(shard_count):
        out_refs[i][...] = made[i * rows : (i + 1) * rows]


def gated(shards, gate_weight, up_weight):
    rows = shards[0][0].shape[0]
    width, units = gate_weight.shape
    block = 256
    count = len(shards)
    operands = [a for shard in shards for a in shard]
    columns = pl.BlockSpec((width, block), lambda i: (0, i))
    out = pl.BlockSpec((rows, block), lambda i: (0, i))
    shape = jax.ShapeDtypeStruct((rows, units), jnp.bfloat16)
    return pl.pallas_call(
        functools.partial(gated_kernel, count, len(shards[0])),
        grid=(units // block,),
        in_specs=[pl.BlockSpec(a.shape, lambda i: (0, 0)) for a in operands] + [columns] * 2,
        out_specs=[out] * count,
        out_shape=[shape] * count,
        scratch_shapes=[
            pltpu.VMEM((count * rows, width), jnp.bfloat16),
            pltpu.VMEM((count * rows, 128), jnp.float32),
        ],
        compiler_params=pltpu.CompilerParams(vmem_limit_bytes=VMEM_LIMIT),
        cost_estimate=pl.CostEstimate(
            flops=4 * count * rows * width * units,
            bytes_accessed=4 * width * units + 2 * count * rows * (width + units),
            transcendentals=count * rows * units,
        ),
    )(*operands, gate_weight, up_weight)


def cache_kernel(page_ref, kv_ref, cache_ref, out_ref):
    for i in range(out_ref.shape[0]):
        page = page_ref[i]

        @pl.when(page >= 0)
        def _():
            first = pl.multiple_of(jnp.maximum(page, 0) * PAGE_TOKENS, PAGE_TOKENS)
            out_ref[i] = kv_ref[pl.ds(first, PAGE_TOKENS), :]

        @pl.when(page < 0)
        def _():
            out_ref[i] = cache_ref[i]


def write_cache(pages, kv, cache):
    return pl.pallas_call(
        cache_kernel,
        grid=(1,),
        in_specs=[
            pl.BlockSpec(memory_space=pltpu.SMEM),
            pl.BlockSpec(kv.shape, lambda i: (0, 0)),
            pl.BlockSpec(cache.shape, lambda i: (0, 0, 0)),
        ],
        out_specs=pl.BlockSpec(cache.shape, lambda i: (0, 0, 0)),
        out_shape=jax.ShapeDtypeStruct(cache.shape, cache.dtype),
        compiler_params=pltpu.CompilerParams(vmem_limit_bytes=VMEM_LIMIT),
        cost_estimate=pl.CostEstimate(flops=0, bytes_accessed=8 * cache.size, transcendentals=0),
    )(pages, kv, cache)


def on_device(
    queries,
    rotated_keys_values,
    prompt_window_index,
    residual,
    ffn_gain,
    gate_weight,
    up_weight,
    paged_cache,
    page_table,
):
    queries, residual, gate_weight, up_weight, paged_cache = [
        pltpu.with_memory_space_constraint(a, pltpu.HBM)
        for a in (queries, residual, gate_weight, up_weight, paged_cache)
    ]
    own_kv = pltpu.with_memory_space_constraint(rotated_keys_values, pltpu.HBM)
    rows, width = queries.shape
    tok_index = lax.axis_index("tok")
    tok_count = lax.axis_size("tok")
    grp_index = lax.axis_index("grp")
    grp_count = lax.axis_size("grp")
    line, column = grp_index // 2, grp_index % 2
    line_count = grp_count // 2
    ahead = ring_tables(line_count)
    units = gate_weight.shape[1]
    chunks = range(len(HEAD_CHUNKS))

    def swap(array, mask):
        return lax.ppermute(array, "tok", [(t, t ^ mask) for t in range(tok_count)])

    def send(array, steps, flip):
        pairs = []
        for z in range(line_count):
            for y in range(2):
                pairs.append((2 * z + y, 2 * ahead[steps][z] + (1 - y if flip else y)))
        return lax.ppermute(array, "grp", pairs)

    packed = pack(own_kv, prompt_window_index)
    group_chunks = []
    for c in chunks:
        held = {0: packed[c]}
        mask = tok_count // 2
        while mask:
            held.update({m ^ mask: swap(a, mask) for m, a in held.items()})
            mask //= 2
        group_chunks.append([held[m] for m in range(tok_count)])

    own_seg = jnp.broadcast_to(prompt_window_index[0].astype(jnp.float32)[:, None], (rows, rows))
    place = tok_index.astype(jnp.int32).reshape(1)
    gain = ffn_gain.reshape(1, width)
    scaled, carried = [], None
    for c in chunks:
        made = attend(c, queries, residual, gain, group_chunks[c], place, own_seg, carried)
        if c == 0:
            bias = made[3]
        if c < len(HEAD_CHUNKS) - 1:
            carried = (made[0], made[2], bias)
        scaled.append(made[1])
    attended = made[0]

    late_kv, _ = lax.optimization_barrier((rotated_keys_values, scaled[-1]))
    group_kv = lax.all_gather(late_kv, "tok", axis=0, tiled=True)
    slot_count = paged_cache.shape[0]
    page_count = group_kv.shape[0] // PAGE_TOKENS
    targets = page_table[0, :page_count] - tok_index * slot_count
    onehot = targets[None, :] == jnp.arange(slot_count)[:, None]
    page = jnp.where(onehot, jnp.arange(page_count, dtype=jnp.int32)[None, :] + 1, 0)
    pages = jnp.max(page, axis=1) - 1
    written = write_cache(pages, group_kv, paged_cache)

    hidden = jnp.zeros((rows, grp_count * units), jnp.bfloat16)

    def put(hidden, block, steps, flip):
        source = sum(jnp.where(line == z, ahead[steps][z] * 2, 0) for z in range(line_count))
        source = source + (1 - column if flip else column)
        return lax.dynamic_update_slice_in_dim(hidden, block, source * units, 1)

    held = scaled
    for step in range(line_count):
        other, following = [], []
        for c in chunks:
            swapped = send(held[c], 0, True)
            if step + 1 < line_count:
                forwarded = send(held[c], 1, False)
                swapped, forwarded = lax.optimization_barrier((swapped, forwarded))
                following.append(forwarded)
            other.append(swapped)
        if step + 1 < line_count:
            own_block, other_block = gated([held, other], gate_weight, up_weight)
        else:
            (own_block,) = gated([held], gate_weight, up_weight)
            other[-1], written = lax.optimization_barrier((other[-1], written))
            (other_block,) = gated([other], gate_weight, up_weight)
        if step:
            own_block = send(own_block, line_count - step, False)
        other_block = send(other_block, (line_count - step) % line_count, True)
        hidden = put(hidden, own_block, step, False)
        hidden = put(hidden, other_block, step, True)
        held = following
    return (attended, hidden, written)


def solution(mesh):
    in_specs = (
        P(("grp", "tok"), None),
        P(("grp", "tok"), None),
        P("grp", "tok"),
        P(("grp", "tok"), None),
        P(),
        P(None, "grp"),
        P(None, "grp"),
        P(("grp", "tok"), None, None),
        P("grp", None),
    )
    out_specs = (P(("grp", "tok"), None), P(("grp", "tok"), None), P(("grp", "tok"), None, None))
    return jax.shard_map(
        on_device, mesh=mesh, in_specs=in_specs, out_specs=out_specs, check_vma=False
    )
```

```python
import functools
import math

import jax
import jax.numpy as jnp
from jax import lax
from jax.experimental import pallas as pl
from jax.experimental.pallas import tpu as pltpu
from jax.sharding import PartitionSpec as P

QUERY_HEADS = 40
KEY_VALUE_HEADS = 8
HEAD_SIZE = 128
PAGE_TOKENS = 16
GROUP_SPLIT = QUERY_HEADS // KEY_VALUE_HEADS
HEAD_CHUNKS = (3, 5)
SEG_ROWS = 16
SCALE_COLUMNS = 128
MASK_FILLER = -1e30
VMEM_LIMIT = 28 * 1024 * 1024


def ring_order(count):
    return [0] + list(range(1, count, 2)) + list(range((count - 1) // 2 * 2, 0, -2))


def ring_tables(count):
    order = ring_order(count)
    spot = {place: i for i, place in enumerate(order)}
    return [[order[(spot[z] + s) % count] for z in range(count)] for s in range(count)]


def pack_kernel(kv_ref, seg_ref, *out_refs):
    rows = kv_ref.shape[0]
    key_width = KEY_VALUE_HEADS * HEAD_SIZE
    first = 0
    for out_ref, heads in zip(out_refs, HEAD_CHUNKS):
        width = heads * HEAD_SIZE
        out_ref[:rows, :width] = kv_ref[:, first : first + width]
        out_ref[:rows, width:] = kv_ref[:, key_width + first : key_width + first + width]
        first += width
    ids = jnp.broadcast_to(seg_ref[...], (SEG_ROWS, rows)).astype(jnp.float32)
    tail = jnp.concatenate([ids] * (out_refs[0].shape[1] // rows), axis=1)
    out_refs[0][rows:, :] = tail.astype(jnp.bfloat16)


def pack(kv, seg):
    rows = kv.shape[0]
    shapes = [
        jax.ShapeDtypeStruct(
            (rows + (SEG_ROWS if i == 0 else 0), 2 * heads * HEAD_SIZE), jnp.bfloat16
        )
        for i, heads in enumerate(HEAD_CHUNKS)
    ]
    return pl.pallas_call(
        pack_kernel,
        out_shape=shapes,
        compiler_params=pltpu.CompilerParams(vmem_limit_bytes=VMEM_LIMIT),
        cost_estimate=pl.CostEstimate(flops=0, bytes_accessed=4 * kv.size, transcendentals=0),
    )(kv, seg)


def attend_kernel(chunk, shard_count, width_all, *refs):
    heads = HEAD_CHUNKS[chunk]
    first, last = chunk == 0, chunk == len(HEAD_CHUNKS) - 1
    refs = list(refs)
    q_ref, res_ref, gain_ref = refs[:3]
    kv_refs = refs[3 : 3 + shard_count]
    rest = refs[3 + shard_count :]
    rows = q_ref.shape[0]
    if first:
        place_ref, own_seg_ref = rest[:2]
        attended_ref, scaled_ref, square_ref, bias_ref = rest[2:]
        row = lax.broadcasted_iota(jnp.int32, (rows, rows), 0)
        col = lax.broadcasted_iota(jnp.int32, (rows, rows), 1)
        place = place_ref[0]
        for m in range(shard_count):
            ids = kv_refs[m][rows:, :rows].astype(jnp.float32)[:1]
            apart = ((place ^ m) - place) * rows
            live = (own_seg_ref[...] == ids) & (col + apart <= row)
            bias_ref[:, m * rows : (m + 1) * rows] = jnp.where(live, 0.0, MASK_FILLER)
        total = jnp.zeros((rows, 1), jnp.float32)
    else:
        bias_ref, square_in = rest[:2]
        attended_ref, scaled_ref = rest[2:4]
        square_ref = None if last else rest[4]
        total = square_in[:, :1]
    bias = bias_ref[...]
    bias = jnp.concatenate([bias] * GROUP_SPLIT, axis=0)
    for h in range(heads):
        keys = jnp.concatenate(
            [r[:rows, h * HEAD_SIZE : (h + 1) * HEAD_SIZE] for r in kv_refs], axis=0
        )
        values = jnp.concatenate(
            [r[:rows, (heads + h) * HEAD_SIZE : (heads + h + 1) * HEAD_SIZE] for r in kv_refs],
            axis=0,
        )
        base = h * GROUP_SPLIT * HEAD_SIZE
        query = jnp.concatenate(
            [q_ref[:, base + g * HEAD_SIZE : base + (g + 1) * HEAD_SIZE] for g in range(GROUP_SPLIT)],
            axis=0,
        )
        scores = lax.dot_general(
            query, keys, (((1,), (1,)), ((), ())), preferred_element_type=jnp.float32
        )
        scores = scores * (1.0 / math.sqrt(HEAD_SIZE)) + bias
        weights = jnp.exp(scores - jnp.max(scores, axis=1, keepdims=True))
        denominator = jnp.sum(weights, axis=1, keepdims=True)
        summed = jnp.dot(weights.astype(jnp.bfloat16), values, preferred_element_type=jnp.float32)
        attention = (summed / denominator).astype(jnp.bfloat16).astype(jnp.float32)
        for g in range(GROUP_SPLIT):
            columns = slice(base + g * HEAD_SIZE, base + (g + 1) * HEAD_SIZE)
            attended = res_ref[:, columns].astype(jnp.float32) + attention[g * rows : (g + 1) * rows]
            attended = attended.astype(jnp.bfloat16)
            attended_ref[:, columns] = attended
            widened = attended.astype(jnp.float32)
            scaled_ref[:, columns] = (widened * gain_ref[:, columns]).astype(jnp.bfloat16)
            total = total + jnp.sum(widened * widened, axis=1, keepdims=True)
    if last:
        scale = lax.rsqrt(total * (1.0 / width_all) + 1e-06)
        high = scale.astype(jnp.bfloat16)
        low = (scale - high.astype(jnp.float32)).astype(jnp.bfloat16)
        lane = lax.broadcasted_iota(jnp.int32, (rows, SCALE_COLUMNS), 1)
        both = jnp.where(
            lane < SCALE_COLUMNS // 2, high.astype(jnp.float32), low.astype(jnp.float32)
        )
        scaled_ref[:, heads * GROUP_SPLIT * HEAD_SIZE :] = both.astype(jnp.bfloat16)
    else:
        square_ref[...] = jnp.broadcast_to(total, square_ref.shape)


def attend(chunk, queries, residual, gain, kv_chunks, place, own_seg, carried):
    heads = HEAD_CHUNKS[chunk]
    rows, width_all = queries.shape
    first, last = chunk == 0, chunk == len(HEAD_CHUNKS) - 1
    width = heads * GROUP_SPLIT * HEAD_SIZE
    before = sum(HEAD_CHUNKS[:chunk]) * GROUP_SPLIT * HEAD_SIZE
    shard_count = len(kv_chunks)

    def whole(shape):
        return pl.BlockSpec(shape, lambda i: (0, 0))

    columns = pl.BlockSpec((pl.Element(rows), pl.Element(width)), lambda i: (0, before))
    gains = pl.BlockSpec((pl.Element(1), pl.Element(width)), lambda i: (0, before))
    in_specs = [columns, columns, gains]
    in_specs += [whole(a.shape) for a in kv_chunks]
    operands = [queries, residual, gain] + list(kv_chunks)
    sent = width + (SCALE_COLUMNS if last else 0)
    shapes = [
        jax.ShapeDtypeStruct((rows, width), jnp.bfloat16),
        jax.ShapeDtypeStruct((rows, sent), jnp.bfloat16),
    ]
    out_specs = [whole((rows, width)), whole((rows, sent))]
    square = jax.ShapeDtypeStruct((rows, 128), jnp.float32)
    bias = jax.ShapeDtypeStruct((rows, rows * shard_count), jnp.float32)
    if first:
        operands += [place, own_seg]
        in_specs += [pl.BlockSpec(memory_space=pltpu.SMEM), whole(own_seg.shape)]
        shapes += [square, bias]
        out_specs += [whole(square.shape), whole(bias.shape)]
    else:
        square_so_far, bias_array = carried
        operands += [bias_array, square_so_far]
        in_specs += [whole(bias.shape), whole(square.shape)]
        if not last:
            shapes += [square]
            out_specs += [whole(square.shape)]
    keys = rows * shard_count
    return pl.pallas_call(
        functools.partial(attend_kernel, chunk, shard_count, width_all),
        grid=(1,),
        in_specs=in_specs,
        out_specs=out_specs,
        out_shape=shapes,
        compiler_params=pltpu.CompilerParams(vmem_limit_bytes=VMEM_LIMIT),
        cost_estimate=pl.CostEstimate(
            flops=4 * rows * width * keys,
            bytes_accessed=8 * rows * width + 4 * keys * heads * HEAD_SIZE,
            transcendentals=rows * keys * heads * GROUP_SPLIT,
        ),
    )(*operands)


def gated_kernel(shard_count, chunk_count, *refs):
    shards = [refs[i * chunk_count : (i + 1) * chunk_count] for i in range(shard_count)]
    rest = refs[shard_count * chunk_count :]
    gate_ref, up_ref = rest[:2]
    out_refs = rest[2 : 2 + shard_count]
    rows_ref, scale_ref = rest[2 + shard_count :]
    rows = shards[0][0].shape[0]

    @pl.when(pl.program_id(0) == 0)
    def _():
        for i, chunks in enumerate(shards):
            span = slice(i * rows, (i + 1) * rows)
            first = 0
            for j, ref in enumerate(chunks):
                width = ref.shape[1] - (SCALE_COLUMNS if j == chunk_count - 1 else 0)
                rows_ref[span, first : first + width] = ref[:, :width]
                first += width
            both = chunks[-1][:, -SCALE_COLUMNS:].astype(jnp.float32)
            scale = both[:, :1] + both[:, SCALE_COLUMNS // 2 : SCALE_COLUMNS // 2 + 1]
            scale_ref[span, :] = jnp.broadcast_to(scale, (rows, 128))

    tokens = rows_ref[...]
    scale = scale_ref[:, :1]
    gate_sum = jnp.dot(tokens, gate_ref[...], preferred_element_type=jnp.float32) * scale
    up_sum = jnp.dot(tokens, up_ref[...], preferred_element_type=jnp.float32) * scale
    made = (gate_sum / (1.0 + jnp.exp(-gate_sum)) * up_sum).astype(jnp.bfloat16)
    for i in range(shard_count):
        out_refs[i][...] = made[i * rows : (i + 1) * rows]


def gated(shards, gate_weight, up_weight):
    rows = shards[0][0].shape[0]
    width, units = gate_weight.shape
    block = 256
    count = len(shards)
    operands = [a for shard in shards for a in shard]
    columns = pl.BlockSpec((width, block), lambda i: (0, i))
    out = pl.BlockSpec((rows, block), lambda i: (0, i))
    shape = jax.ShapeDtypeStruct((rows, units), jnp.bfloat16)
    return pl.pallas_call(
        functools.partial(gated_kernel, count, len(shards[0])),
        grid=(units // block,),
        in_specs=[pl.BlockSpec(a.shape, lambda i: (0, 0)) for a in operands] + [columns] * 2,
        out_specs=[out] * count,
        out_shape=[shape] * count,
        scratch_shapes=[
            pltpu.VMEM((count * rows, width), jnp.bfloat16),
            pltpu.VMEM((count * rows, 128), jnp.float32),
        ],
        compiler_params=pltpu.CompilerParams(vmem_limit_bytes=VMEM_LIMIT),
        cost_estimate=pl.CostEstimate(
            flops=4 * count * rows * width * units,
            bytes_accessed=4 * width * units + 2 * count * rows * (width + units),
            transcendentals=count * rows * units,
        ),
    )(*operands, gate_weight, up_weight)


def cache_kernel(page_ref, kv_ref, cache_ref, out_ref):
    for i in range(out_ref.shape[0]):
        page = page_ref[i]

        @pl.when(page >= 0)
        def _():
            first = pl.multiple_of(jnp.maximum(page, 0) * PAGE_TOKENS, PAGE_TOKENS)
            out_ref[i] = kv_ref[pl.ds(first, PAGE_TOKENS), :]

        @pl.when(page < 0)
        def _():
            out_ref[i] = cache_ref[i]


def write_cache(pages, kv, cache):
    return pl.pallas_call(
        cache_kernel,
        grid=(1,),
        in_specs=[
            pl.BlockSpec(memory_space=pltpu.SMEM),
            pl.BlockSpec(kv.shape, lambda i: (0, 0)),
            pl.BlockSpec(cache.shape, lambda i: (0, 0, 0)),
        ],
        out_specs=pl.BlockSpec(cache.shape, lambda i: (0, 0, 0)),
        out_shape=jax.ShapeDtypeStruct(cache.shape, cache.dtype),
        compiler_params=pltpu.CompilerParams(vmem_limit_bytes=VMEM_LIMIT),
        cost_estimate=pl.CostEstimate(flops=0, bytes_accessed=8 * cache.size, transcendentals=0),
    )(pages, kv, cache)


def on_device(
    queries,
    rotated_keys_values,
    prompt_window_index,
    residual,
    ffn_gain,
    gate_weight,
    up_weight,
    paged_cache,
    page_table,
):
    queries, residual, gate_weight, up_weight, paged_cache = [
        pltpu.with_memory_space_constraint(a, pltpu.HBM)
        for a in (queries, residual, gate_weight, up_weight, paged_cache)
    ]
    own_kv = pltpu.with_memory_space_constraint(rotated_keys_values, pltpu.HBM)
    rows, width = queries.shape
    tok_index = lax.axis_index("tok")
    tok_count = lax.axis_size("tok")
    grp_index = lax.axis_index("grp")
    grp_count = lax.axis_size("grp")
    line, column = grp_index // 2, grp_index % 2
    line_count = grp_count // 2
    ahead = ring_tables(line_count)
    units = gate_weight.shape[1]
    chunks = range(len(HEAD_CHUNKS))

    def after(array, *others):
        return lax.optimization_barrier((array, *others))[0]

    def swap(array, mask):
        return lax.ppermute(array, "tok", [(t, t ^ mask) for t in range(tok_count)])

    def send(array, steps, flip):
        pairs = []
        for z in range(line_count):
            for y in range(2):
                pairs.append((2 * z + y, 2 * ahead[steps][z] + (1 - y if flip else y)))
        return lax.ppermute(array, "grp", pairs)

    own_seg = jnp.broadcast_to(prompt_window_index[0].astype(jnp.float32)[:, None], (rows, rows))
    place = tok_index.astype(jnp.int32).reshape(1)
    gain = ffn_gain.reshape(1, width)
    packed = pack(own_kv, prompt_window_index)
    first_swaps = []
    for c in chunks:
        held = {0: packed[c]}
        mask = tok_count // 2
        while mask > 1:
            held.update({m ^ mask: swap(a, mask) for m, a in held.items()})
            mask //= 2
        first_swaps.append(held)
    scaled, parts, carried = [], [], None
    for c in chunks:
        held = first_swaps[c]
        if c:
            held = {m: after(a, scaled[-1]) if m else a for m, a in held.items()}
        if tok_count > 1:
            held.update({m ^ 1: swap(a, 1) for m, a in held.items()})
        keys_values = [held[m] for m in range(tok_count)]
        made = attend(c, queries, residual, gain, keys_values, place, own_seg, carried)
        if c == 0:
            bias = made[3]
        if c < len(HEAD_CHUNKS) - 1:
            carried = (made[2], bias)
        parts.append(made[0])
        scaled.append(made[1])
    attended = jnp.concatenate(parts, axis=1)

    late_kv, _ = lax.optimization_barrier((rotated_keys_values, scaled[-1]))
    group_kv = lax.all_gather(late_kv, "tok", axis=0, tiled=True)
    slot_count = paged_cache.shape[0]
    page_count = group_kv.shape[0] // PAGE_TOKENS
    targets = page_table[0, :page_count] - tok_index * slot_count
    onehot = targets[None, :] == jnp.arange(slot_count)[:, None]
    page = jnp.where(onehot, jnp.arange(page_count, dtype=jnp.int32)[None, :] + 1, 0)
    pages = jnp.max(page, axis=1) - 1
    written = write_cache(pages, group_kv, paged_cache)

    hidden = jnp.zeros((rows, grp_count * units), jnp.bfloat16)

    def put(hidden, block, steps, flip):
        source = sum(jnp.where(line == z, ahead[steps][z] * 2, 0) for z in range(line_count))
        source = source + (1 - column if flip else column)
        return lax.dynamic_update_slice_in_dim(hidden, block, source * units, 1)

    sent, arrived, waiting = [], [scaled], [(scaled, 0, False)]
    for step in range(line_count):
        other, following = [], []
        for c in chunks:
            ready = arrived[-1][c]
            number = len(sent)
            behind = sent[0] if number == 1 else sent[number - 3] if number > 2 else ()
            if behind:
                ready = after(ready, *behind)
            pair = [send(ready, 0, True)]
            if step + 1 < line_count:
                pair.append(send(ready, 1, False))
                following.append(pair[1])
            other.append(pair[0])
            sent.append(pair)
        arrived.append(following)
        waiting.append((other, step, True))
        if following:
            waiting.append((following, step + 1, False))
        if step == line_count - 2:
            waiting[-1] = ([*following[:-1], after(following[-1], written)], step + 1, False)
        blocks = gated([shard for shard, _, _ in waiting], gate_weight, up_weight)
        for block, (_, steps, flip) in zip(blocks, waiting):
            if steps or flip:
                block = send(block, (line_count - steps) % line_count, flip)
            hidden = put(hidden, block, steps, flip)
        waiting = []
    return (attended, hidden, written)


def solution(mesh):
    in_specs = (
        P(("grp", "tok"), None),
        P(("grp", "tok"), None),
        P("grp", "tok"),
        P(("grp", "tok"), None),
        P(),
        P(None, "grp"),
        P(None, "grp"),
        P(("grp", "tok"), None, None),
        P("grp", None),
    )
    out_specs = (P(("grp", "tok"), None), P(("grp", "tok"), None), P(("grp", "tok"), None, None))
    return jax.shard_map(
        on_device, mesh=mesh, in_specs=in_specs, out_specs=out_specs, check_vma=False
    )
```

```python
import functools
import math

import jax
import jax.numpy as jnp
from jax import lax
from jax.experimental import pallas as pl
from jax.experimental.pallas import tpu as pltpu
from jax.sharding import PartitionSpec as P

QUERY_HEADS = 40
KEY_VALUE_HEADS = 8
HEAD_SIZE = 128
PAGE_TOKENS = 16
GROUP_SPLIT = QUERY_HEADS // KEY_VALUE_HEADS
HEAD_CHUNKS = (3, 5)
SEG_ROWS = 16
SCALE_COLUMNS = 128
MASK_FILLER = -1e30
VMEM_LIMIT = 28 * 1024 * 1024


def ring_order(count):
    return [0] + list(range(1, count, 2)) + list(range((count - 1) // 2 * 2, 0, -2))


def ring_tables(count):
    order = ring_order(count)
    spot = {place: i for i, place in enumerate(order)}
    return [[order[(spot[z] + s) % count] for z in range(count)] for s in range(count)]


def pack_kernel(kv_ref, seg_ref, *out_refs):
    rows = kv_ref.shape[0]
    key_width = KEY_VALUE_HEADS * HEAD_SIZE
    first = 0
    for out_ref, heads in zip(out_refs, HEAD_CHUNKS):
        width = heads * HEAD_SIZE
        out_ref[:rows, :width] = kv_ref[:, first : first + width]
        out_ref[:rows, width:] = kv_ref[:, key_width + first : key_width + first + width]
        first += width
    ids = jnp.broadcast_to(seg_ref[...], (SEG_ROWS, rows)).astype(jnp.float32)
    tail = jnp.concatenate([ids] * (out_refs[0].shape[1] // rows), axis=1)
    out_refs[0][rows:, :] = tail.astype(jnp.bfloat16)


def pack(kv, seg):
    rows = kv.shape[0]
    shapes = [
        jax.ShapeDtypeStruct(
            (rows + (SEG_ROWS if i == 0 else 0), 2 * heads * HEAD_SIZE), jnp.bfloat16
        )
        for i, heads in enumerate(HEAD_CHUNKS)
    ]
    return pl.pallas_call(
        pack_kernel,
        out_shape=shapes,
        compiler_params=pltpu.CompilerParams(vmem_limit_bytes=VMEM_LIMIT),
        cost_estimate=pl.CostEstimate(flops=0, bytes_accessed=4 * kv.size, transcendentals=0),
    )(kv, seg)


def attend_kernel(chunk, shard_count, width_all, *refs):
    heads = HEAD_CHUNKS[chunk]
    first, last = chunk == 0, chunk == len(HEAD_CHUNKS) - 1
    refs = list(refs)
    q_ref, res_ref, gain_ref = refs[:3]
    kv_refs = refs[3 : 3 + shard_count]
    rest = refs[3 + shard_count :]
    rows = q_ref.shape[0]
    if first:
        place_ref, own_seg_ref = rest[:2]
        attended_ref, scaled_ref, square_ref, bias_ref = rest[2:]
        row = lax.broadcasted_iota(jnp.int32, (rows, rows), 0)
        col = lax.broadcasted_iota(jnp.int32, (rows, rows), 1)
        place = place_ref[0]
        for m in range(shard_count):
            ids = kv_refs[m][rows:, :rows].astype(jnp.float32)[:1]
            apart = ((place ^ m) - place) * rows
            live = (own_seg_ref[...] == ids) & (col + apart <= row)
            bias_ref[:, m * rows : (m + 1) * rows] = jnp.where(live, 0.0, MASK_FILLER)
        total = jnp.zeros((rows, 1), jnp.float32)
    else:
        bias_ref, square_in = rest[:2]
        attended_ref, scaled_ref = rest[2:4]
        square_ref = None if last else rest[4]
        total = square_in[:, :1]
    bias = bias_ref[...]
    bias = jnp.concatenate([bias] * GROUP_SPLIT, axis=0)
    for h in range(heads):
        keys = jnp.concatenate(
            [r[:rows, h * HEAD_SIZE : (h + 1) * HEAD_SIZE] for r in kv_refs], axis=0
        )
        values = jnp.concatenate(
            [r[:rows, (heads + h) * HEAD_SIZE : (heads + h + 1) * HEAD_SIZE] for r in kv_refs],
            axis=0,
        )
        base = h * GROUP_SPLIT * HEAD_SIZE
        query = jnp.concatenate(
            [q_ref[:, base + g * HEAD_SIZE : base + (g + 1) * HEAD_SIZE] for g in range(GROUP_SPLIT)],
            axis=0,
        )
        scores = lax.dot_general(
            query, keys, (((1,), (1,)), ((), ())), preferred_element_type=jnp.float32
        )
        scores = scores * (1.0 / math.sqrt(HEAD_SIZE)) + bias
        weights = jnp.exp(scores - jnp.max(scores, axis=1, keepdims=True))
        denominator = jnp.sum(weights, axis=1, keepdims=True)
        summed = jnp.dot(weights.astype(jnp.bfloat16), values, preferred_element_type=jnp.float32)
        attention = (summed / denominator).astype(jnp.bfloat16).astype(jnp.float32)
        for g in range(GROUP_SPLIT):
            columns = slice(base + g * HEAD_SIZE, base + (g + 1) * HEAD_SIZE)
            attended = res_ref[:, columns].astype(jnp.float32) + attention[g * rows : (g + 1) * rows]
            attended = attended.astype(jnp.bfloat16)
            attended_ref[:, columns] = attended
            widened = attended.astype(jnp.float32)
            scaled_ref[:, columns] = (widened * gain_ref[:, columns]).astype(jnp.bfloat16)
            total = total + jnp.sum(widened * widened, axis=1, keepdims=True)
    if last:
        scale = lax.rsqrt(total * (1.0 / width_all) + 1e-06)
        high = scale.astype(jnp.bfloat16)
        low = (scale - high.astype(jnp.float32)).astype(jnp.bfloat16)
        lane = lax.broadcasted_iota(jnp.int32, (rows, SCALE_COLUMNS), 1)
        both = jnp.where(
            lane < SCALE_COLUMNS // 2, high.astype(jnp.float32), low.astype(jnp.float32)
        )
        scaled_ref[:, heads * GROUP_SPLIT * HEAD_SIZE :] = both.astype(jnp.bfloat16)
    else:
        square_ref[...] = jnp.broadcast_to(total, square_ref.shape)


def attend(chunk, queries, residual, gain, kv_chunks, place, own_seg, carried):
    heads = HEAD_CHUNKS[chunk]
    rows, width_all = queries.shape
    first, last = chunk == 0, chunk == len(HEAD_CHUNKS) - 1
    width = heads * GROUP_SPLIT * HEAD_SIZE
    before = sum(HEAD_CHUNKS[:chunk]) * GROUP_SPLIT * HEAD_SIZE
    shard_count = len(kv_chunks)

    def whole(shape):
        return pl.BlockSpec(shape, lambda i: (0, 0))

    columns = pl.BlockSpec((pl.Element(rows), pl.Element(width)), lambda i: (0, before))
    gains = pl.BlockSpec((pl.Element(1), pl.Element(width)), lambda i: (0, before))
    in_specs = [columns, columns, gains]
    in_specs += [whole(a.shape) for a in kv_chunks]
    operands = [queries, residual, gain] + list(kv_chunks)
    sent = width + (SCALE_COLUMNS if last else 0)
    shapes = [
        jax.ShapeDtypeStruct((rows, width), jnp.bfloat16),
        jax.ShapeDtypeStruct((rows, sent), jnp.bfloat16),
    ]
    out_specs = [whole((rows, width)), whole((rows, sent))]
    square = jax.ShapeDtypeStruct((rows, 128), jnp.float32)
    bias = jax.ShapeDtypeStruct((rows, rows * shard_count), jnp.float32)
    if first:
        operands += [place, own_seg]
        in_specs += [pl.BlockSpec(memory_space=pltpu.SMEM), whole(own_seg.shape)]
        shapes += [square, bias]
        out_specs += [whole(square.shape), whole(bias.shape)]
    else:
        square_so_far, bias_array = carried
        operands += [bias_array, square_so_far]
        in_specs += [whole(bias.shape), whole(square.shape)]
        if not last:
            shapes += [square]
            out_specs += [whole(square.shape)]
    keys = rows * shard_count
    return pl.pallas_call(
        functools.partial(attend_kernel, chunk, shard_count, width_all),
        grid=(1,),
        in_specs=in_specs,
        out_specs=out_specs,
        out_shape=shapes,
        compiler_params=pltpu.CompilerParams(vmem_limit_bytes=VMEM_LIMIT),
        cost_estimate=pl.CostEstimate(
            flops=4 * rows * width * keys,
            bytes_accessed=8 * rows * width + 4 * keys * heads * HEAD_SIZE,
            transcendentals=rows * keys * heads * GROUP_SPLIT,
        ),
    )(*operands)


def gated_kernel(shard_count, chunk_count, *refs):
    shards = [refs[i * chunk_count : (i + 1) * chunk_count] for i in range(shard_count)]
    rest = refs[shard_count * chunk_count :]
    gate_ref, up_ref = rest[:2]
    out_refs = rest[2 : 2 + shard_count]
    rows_ref, scale_ref = rest[2 + shard_count :]
    rows = shards[0][0].shape[0]

    @pl.when(pl.program_id(0) == 0)
    def _():
        for i, chunks in enumerate(shards):
            span = slice(i * rows, (i + 1) * rows)
            first = 0
            for j, ref in enumerate(chunks):
                width = ref.shape[1] - (SCALE_COLUMNS if j == chunk_count - 1 else 0)
                rows_ref[span, first : first + width] = ref[:, :width]
                first += width
            both = chunks[-1][:, -SCALE_COLUMNS:].astype(jnp.float32)
            scale = both[:, :1] + both[:, SCALE_COLUMNS // 2 : SCALE_COLUMNS // 2 + 1]
            scale_ref[span, :] = jnp.broadcast_to(scale, (rows, 128))

    tokens = rows_ref[...]
    scale = scale_ref[:, :1]
    gate_sum = jnp.dot(tokens, gate_ref[...], preferred_element_type=jnp.float32) * scale
    up_sum = jnp.dot(tokens, up_ref[...], preferred_element_type=jnp.float32) * scale
    made = (gate_sum / (1.0 + jnp.exp(-gate_sum)) * up_sum).astype(jnp.bfloat16)
    for i in range(shard_count):
        out_refs[i][...] = made[i * rows : (i + 1) * rows]


def gated(shards, gate_weight, up_weight):
    rows = shards[0][0].shape[0]
    width, units = gate_weight.shape
    block = 256
    count = len(shards)
    operands = [a for shard in shards for a in shard]
    columns = pl.BlockSpec((width, block), lambda i: (0, i))
    out = pl.BlockSpec((rows, block), lambda i: (0, i))
    shape = jax.ShapeDtypeStruct((rows, units), jnp.bfloat16)
    return pl.pallas_call(
        functools.partial(gated_kernel, count, len(shards[0])),
        grid=(units // block,),
        in_specs=[pl.BlockSpec(a.shape, lambda i: (0, 0)) for a in operands] + [columns] * 2,
        out_specs=[out] * count,
        out_shape=[shape] * count,
        scratch_shapes=[
            pltpu.VMEM((count * rows, width), jnp.bfloat16),
            pltpu.VMEM((count * rows, 128), jnp.float32),
        ],
        compiler_params=pltpu.CompilerParams(vmem_limit_bytes=VMEM_LIMIT),
        cost_estimate=pl.CostEstimate(
            flops=4 * count * rows * width * units,
            bytes_accessed=4 * width * units + 2 * count * rows * (width + units),
            transcendentals=count * rows * units,
        ),
    )(*operands, gate_weight, up_weight)


def cache_kernel(page_ref, kv_ref, cache_ref, out_ref):
    for i in range(out_ref.shape[0]):
        page = page_ref[i]

        @pl.when(page >= 0)
        def _():
            first = pl.multiple_of(jnp.maximum(page, 0) * PAGE_TOKENS, PAGE_TOKENS)
            out_ref[i] = kv_ref[pl.ds(first, PAGE_TOKENS), :]

        @pl.when(page < 0)
        def _():
            out_ref[i] = cache_ref[i]


def write_cache(pages, kv, cache):
    return pl.pallas_call(
        cache_kernel,
        grid=(1,),
        in_specs=[
            pl.BlockSpec(memory_space=pltpu.SMEM),
            pl.BlockSpec(kv.shape, lambda i: (0, 0)),
            pl.BlockSpec(cache.shape, lambda i: (0, 0, 0)),
        ],
        out_specs=pl.BlockSpec(cache.shape, lambda i: (0, 0, 0)),
        out_shape=jax.ShapeDtypeStruct(cache.shape, cache.dtype),
        compiler_params=pltpu.CompilerParams(vmem_limit_bytes=VMEM_LIMIT),
        cost_estimate=pl.CostEstimate(flops=0, bytes_accessed=8 * cache.size, transcendentals=0),
    )(pages, kv, cache)


def on_device(
    queries,
    rotated_keys_values,
    prompt_window_index,
    residual,
    ffn_gain,
    gate_weight,
    up_weight,
    paged_cache,
    page_table,
):
    queries, residual, gate_weight, up_weight, paged_cache = [
        pltpu.with_memory_space_constraint(a, pltpu.HBM)
        for a in (queries, residual, gate_weight, up_weight, paged_cache)
    ]
    own_kv = pltpu.with_memory_space_constraint(rotated_keys_values, pltpu.HBM)
    rows, width = queries.shape
    tok_index = lax.axis_index("tok")
    tok_count = lax.axis_size("tok")
    grp_index = lax.axis_index("grp")
    grp_count = lax.axis_size("grp")
    line, column = grp_index // 2, grp_index % 2
    line_count = grp_count // 2
    ahead = ring_tables(line_count)
    units = gate_weight.shape[1]
    chunks = range(len(HEAD_CHUNKS))

    def after(array, *others):
        return lax.optimization_barrier((array, *others))[0]

    def swap(array, mask):
        return lax.ppermute(array, "tok", [(t, t ^ mask) for t in range(tok_count)])

    def send(array, steps, flip):
        pairs = []
        for z in range(line_count):
            for y in range(2):
                pairs.append((2 * z + y, 2 * ahead[steps][z] + (1 - y if flip else y)))
        return lax.ppermute(array, "grp", pairs)

    own_seg = jnp.broadcast_to(prompt_window_index[0].astype(jnp.float32)[:, None], (rows, rows))
    place = tok_index.astype(jnp.int32).reshape(1)
    gain = ffn_gain.reshape(1, width)
    packed = pack(own_kv, prompt_window_index)
    first_swaps = []
    for c in chunks:
        held = {0: packed[c]}
        mask = tok_count // 2
        while mask > 1:
            held.update({m ^ mask: swap(a, mask) for m, a in held.items()})
            mask //= 2
        first_swaps.append(held)
    scaled, parts, carried = [], [], None
    for c in chunks:
        held = first_swaps[c]
        if c:
            held = {m: after(a, scaled[-1]) if m else a for m, a in held.items()}
        if tok_count > 1:
            held.update({m ^ 1: swap(a, 1) for m, a in held.items()})
        keys_values = [held[m] for m in range(tok_count)]
        made = attend(c, queries, residual, gain, keys_values, place, own_seg, carried)
        if c == 0:
            bias = made[3]
        if c < len(HEAD_CHUNKS) - 1:
            carried = (made[2], bias)
        parts.append(made[0])
        scaled.append(made[1])
    attended = jnp.concatenate(parts, axis=1)

    late_kv, _ = lax.optimization_barrier((rotated_keys_values, scaled[-1]))
    group_kv = lax.all_gather(late_kv, "tok", axis=0, tiled=True)
    slot_count = paged_cache.shape[0]
    page_count = group_kv.shape[0] // PAGE_TOKENS
    targets = page_table[0, :page_count] - tok_index * slot_count
    onehot = targets[None, :] == jnp.arange(slot_count)[:, None]
    page = jnp.where(onehot, jnp.arange(page_count, dtype=jnp.int32)[None, :] + 1, 0)
    pages = jnp.max(page, axis=1) - 1
    written = write_cache(pages, group_kv, paged_cache)

    hidden = jnp.zeros((rows, grp_count * units), jnp.bfloat16)

    def put(hidden, block, steps, flip):
        source = sum(jnp.where(line == z, ahead[steps][z] * 2, 0) for z in range(line_count))
        source = source + (1 - column if flip else column)
        return lax.dynamic_update_slice_in_dim(hidden, block, source * units, 1)

    sent, arrived, waiting = [], [scaled], [(scaled, 0, False)]
    products, late = [], []
    for step in range(line_count):
        other, following = [], []
        for c in chunks:
            ready = arrived[-1][c]
            number = len(sent)
            behind = sent[0] if number == 1 else sent[number - 2][:1] if number > 1 else []
            if c == 0 and step > 1:
                behind = [*behind, products[step - 2]]
            if behind:
                ready = after(ready, *behind)
            pair = [send(ready, 0, True)]
            if step + 1 < line_count:
                pair.append(send(ready, 1, False))
                following.append(pair[1])
            other.append(pair[0])
            sent.append(pair)
        arrived.append(following)
        waiting.append((other, step, True))
        if following:
            waiting.append((following, step + 1, False))
        if step == line_count - 2:
            waiting[-1] = ([*following[:-1], after(following[-1], written)], step + 1, False)
        blocks = gated([shard for shard, _, _ in waiting], gate_weight, up_weight)
        products.append(blocks[-1])
        late = [(after(block, blocks[-1]), steps, flip) for block, steps, flip in late]
        made = late + [(block, steps, flip) for block, (_, steps, flip) in zip(blocks, waiting)]
        late = []
        if 0 < step < line_count - 2:
            late = [entry for entry in made if entry[2]]
            made = [entry for entry in made if not entry[2]]
        for block, steps, flip in made:
            if steps or flip:
                block = send(block, (line_count - steps) % line_count, flip)
            hidden = put(hidden, block, steps, flip)
        waiting = []
    return (attended, hidden, written)


def solution(mesh):
    in_specs = (
        P(("grp", "tok"), None),
        P(("grp", "tok"), None),
        P("grp", "tok"),
        P(("grp", "tok"), None),
        P(),
        P(None, "grp"),
        P(None, "grp"),
        P(("grp", "tok"), None, None),
        P("grp", None),
    )
    out_specs = (P(("grp", "tok"), None), P(("grp", "tok"), None), P(("grp", "tok"), None, None))
    return jax.shard_map(
        on_device, mesh=mesh, in_specs=in_specs, out_specs=out_specs, check_vma=False
    )
```

```python
import functools
import math

import jax
import jax.numpy as jnp
from jax import lax
from jax.experimental import pallas as pl
from jax.experimental.pallas import tpu as pltpu
from jax.sharding import PartitionSpec as P

QUERY_HEADS = 40
KEY_VALUE_HEADS = 8
HEAD_SIZE = 128
PAGE_TOKENS = 16
GROUP_SPLIT = QUERY_HEADS // KEY_VALUE_HEADS
HEAD_CHUNKS = (3, 5)
SEG_ROWS = 16
SCALE_COLUMNS = 128
MASK_FILLER = -1e30
VMEM_LIMIT = 28 * 1024 * 1024


def ring_order(count):
    return [0] + list(range(1, count, 2)) + list(range((count - 1) // 2 * 2, 0, -2))


def ring_tables(count):
    order = ring_order(count)
    spot = {place: i for i, place in enumerate(order)}
    return [[order[(spot[z] + s) % count] for z in range(count)] for s in range(count)]


def pack_kernel(kv_ref, seg_ref, *out_refs):
    rows = kv_ref.shape[0]
    key_width = KEY_VALUE_HEADS * HEAD_SIZE
    first = 0
    for out_ref, heads in zip(out_refs, HEAD_CHUNKS):
        width = heads * HEAD_SIZE
        out_ref[:rows, :width] = kv_ref[:, first : first + width]
        out_ref[:rows, width:] = kv_ref[:, key_width + first : key_width + first + width]
        first += width
    ids = jnp.broadcast_to(seg_ref[...], (SEG_ROWS, rows)).astype(jnp.float32)
    tail = jnp.concatenate([ids] * (out_refs[0].shape[1] // rows), axis=1)
    out_refs[0][rows:, :] = tail.astype(jnp.bfloat16)


def pack(kv, seg):
    rows = kv.shape[0]
    shapes = [
        jax.ShapeDtypeStruct(
            (rows + (SEG_ROWS if i == 0 else 0), 2 * heads * HEAD_SIZE), jnp.bfloat16
        )
        for i, heads in enumerate(HEAD_CHUNKS)
    ]
    return pl.pallas_call(
        pack_kernel,
        out_shape=shapes,
        compiler_params=pltpu.CompilerParams(vmem_limit_bytes=VMEM_LIMIT),
        cost_estimate=pl.CostEstimate(flops=0, bytes_accessed=4 * kv.size, transcendentals=0),
    )(kv, seg)


def attend_kernel(chunk, shard_count, width_all, *refs):
    heads = HEAD_CHUNKS[chunk]
    first, last = chunk == 0, chunk == len(HEAD_CHUNKS) - 1
    refs = list(refs)
    q_ref, res_ref, gain_ref = refs[:3]
    kv_refs = refs[3 : 3 + shard_count]
    rest = refs[3 + shard_count :]
    rows = q_ref.shape[0]
    if first:
        place_ref, own_seg_ref = rest[:2]
        attended_ref, scaled_ref, square_ref, bias_ref = rest[2:]
        row = lax.broadcasted_iota(jnp.int32, (rows, rows), 0)
        col = lax.broadcasted_iota(jnp.int32, (rows, rows), 1)
        place = place_ref[0]
        for m in range(shard_count):
            ids = kv_refs[m][rows:, :rows].astype(jnp.float32)[:1]
            apart = ((place ^ m) - place) * rows
            live = (own_seg_ref[...] == ids) & (col + apart <= row)
            bias_ref[:, m * rows : (m + 1) * rows] = jnp.where(live, 0.0, MASK_FILLER)
        total = jnp.zeros((rows, 1), jnp.float32)
    else:
        bias_ref, square_in = rest[:2]
        attended_ref, scaled_ref = rest[2:4]
        square_ref = None if last else rest[4]
        total = square_in[:, :1]
    bias = bias_ref[...]
    bias = jnp.concatenate([bias] * GROUP_SPLIT, axis=0)
    for h in range(heads):
        keys = jnp.concatenate(
            [r[:rows, h * HEAD_SIZE : (h + 1) * HEAD_SIZE] for r in kv_refs], axis=0
        )
        values = jnp.concatenate(
            [r[:rows, (heads + h) * HEAD_SIZE : (heads + h + 1) * HEAD_SIZE] for r in kv_refs],
            axis=0,
        )
        base = h * GROUP_SPLIT * HEAD_SIZE
        query = jnp.concatenate(
            [q_ref[:, base + g * HEAD_SIZE : base + (g + 1) * HEAD_SIZE] for g in range(GROUP_SPLIT)],
            axis=0,
        )
        scores = lax.dot_general(
            query, keys, (((1,), (1,)), ((), ())), preferred_element_type=jnp.float32
        )
        scores = scores * (1.0 / math.sqrt(HEAD_SIZE)) + bias
        weights = jnp.exp(scores - jnp.max(scores, axis=1, keepdims=True))
        denominator = jnp.sum(weights, axis=1, keepdims=True)
        summed = jnp.dot(weights.astype(jnp.bfloat16), values, preferred_element_type=jnp.float32)
        attention = (summed / denominator).astype(jnp.bfloat16).astype(jnp.float32)
        for g in range(GROUP_SPLIT):
            columns = slice(base + g * HEAD_SIZE, base + (g + 1) * HEAD_SIZE)
            attended = res_ref[:, columns].astype(jnp.float32) + attention[g * rows : (g + 1) * rows]
            attended = attended.astype(jnp.bfloat16)
            attended_ref[:, columns] = attended
            widened = attended.astype(jnp.float32)
            scaled_ref[:, columns] = (widened * gain_ref[:, columns]).astype(jnp.bfloat16)
            total = total + jnp.sum(widened * widened, axis=1, keepdims=True)
    if last:
        scale = lax.rsqrt(total * (1.0 / width_all) + 1e-06)
        high = scale.astype(jnp.bfloat16)
        low = (scale - high.astype(jnp.float32)).astype(jnp.bfloat16)
        lane = lax.broadcasted_iota(jnp.int32, (rows, SCALE_COLUMNS), 1)
        both = jnp.where(
            lane < SCALE_COLUMNS // 2, high.astype(jnp.float32), low.astype(jnp.float32)
        )
        scaled_ref[:, heads * GROUP_SPLIT * HEAD_SIZE :] = both.astype(jnp.bfloat16)
    else:
        square_ref[...] = jnp.broadcast_to(total, square_ref.shape)


def attend(chunk, queries, residual, gain, kv_chunks, place, own_seg, carried):
    heads = HEAD_CHUNKS[chunk]
    rows, width_all = queries.shape
    first, last = chunk == 0, chunk == len(HEAD_CHUNKS) - 1
    width = heads * GROUP_SPLIT * HEAD_SIZE
    before = sum(HEAD_CHUNKS[:chunk]) * GROUP_SPLIT * HEAD_SIZE
    shard_count = len(kv_chunks)

    def whole(shape):
        return pl.BlockSpec(shape, lambda i: (0, 0))

    columns = pl.BlockSpec((pl.Element(rows), pl.Element(width)), lambda i: (0, before))
    gains = pl.BlockSpec((pl.Element(1), pl.Element(width)), lambda i: (0, before))
    in_specs = [columns, columns, gains]
    in_specs += [whole(a.shape) for a in kv_chunks]
    operands = [queries, residual, gain] + list(kv_chunks)
    sent = width + (SCALE_COLUMNS if last else 0)
    shapes = [
        jax.ShapeDtypeStruct((rows, width), jnp.bfloat16),
        jax.ShapeDtypeStruct((rows, sent), jnp.bfloat16),
    ]
    out_specs = [whole((rows, width)), whole((rows, sent))]
    square = jax.ShapeDtypeStruct((rows, 128), jnp.float32)
    bias = jax.ShapeDtypeStruct((rows, rows * shard_count), jnp.float32)
    if first:
        operands += [place, own_seg]
        in_specs += [pl.BlockSpec(memory_space=pltpu.SMEM), whole(own_seg.shape)]
        shapes += [square, bias]
        out_specs += [whole(square.shape), whole(bias.shape)]
    else:
        square_so_far, bias_array = carried
        operands += [bias_array, square_so_far]
        in_specs += [whole(bias.shape), whole(square.shape)]
        if not last:
            shapes += [square]
            out_specs += [whole(square.shape)]
    keys = rows * shard_count
    return pl.pallas_call(
        functools.partial(attend_kernel, chunk, shard_count, width_all),
        grid=(1,),
        in_specs=in_specs,
        out_specs=out_specs,
        out_shape=shapes,
        compiler_params=pltpu.CompilerParams(vmem_limit_bytes=VMEM_LIMIT),
        cost_estimate=pl.CostEstimate(
            flops=4 * rows * width * keys,
            bytes_accessed=8 * rows * width + 4 * keys * heads * HEAD_SIZE,
            transcendentals=rows * keys * heads * GROUP_SPLIT,
        ),
    )(*operands)


def gated_kernel(shard_count, chunk_count, *refs):
    shards = [refs[i * chunk_count : (i + 1) * chunk_count] for i in range(shard_count)]
    rest = refs[shard_count * chunk_count :]
    gate_ref, up_ref = rest[:2]
    out_refs = rest[2 : 2 + shard_count]
    rows_ref, scale_ref = rest[2 + shard_count :]
    rows = shards[0][0].shape[0]

    @pl.when(pl.program_id(0) == 0)
    def _():
        for i, chunks in enumerate(shards):
            span = slice(i * rows, (i + 1) * rows)
            first = 0
            for j, ref in enumerate(chunks):
                width = ref.shape[1] - (SCALE_COLUMNS if j == chunk_count - 1 else 0)
                rows_ref[span, first : first + width] = ref[:, :width]
                first += width
            both = chunks[-1][:, -SCALE_COLUMNS:].astype(jnp.float32)
            scale = both[:, :1] + both[:, SCALE_COLUMNS // 2 : SCALE_COLUMNS // 2 + 1]
            scale_ref[span, :] = jnp.broadcast_to(scale, (rows, 128))

    tokens = rows_ref[...]
    scale = scale_ref[:, :1]
    gate_sum = jnp.dot(tokens, gate_ref[...], preferred_element_type=jnp.float32) * scale
    up_sum = jnp.dot(tokens, up_ref[...], preferred_element_type=jnp.float32) * scale
    made = (gate_sum / (1.0 + jnp.exp(-gate_sum)) * up_sum).astype(jnp.bfloat16)
    for i in range(shard_count):
        out_refs[i][...] = made[i * rows : (i + 1) * rows]


def gated(shards, gate_weight, up_weight):
    rows = shards[0][0].shape[0]
    width, units = gate_weight.shape
    block = 256
    count = len(shards)
    operands = [a for shard in shards for a in shard]
    columns = pl.BlockSpec((width, block), lambda i: (0, i))
    out = pl.BlockSpec((rows, block), lambda i: (0, i))
    shape = jax.ShapeDtypeStruct((rows, units), jnp.bfloat16)
    return pl.pallas_call(
        functools.partial(gated_kernel, count, len(shards[0])),
        grid=(units // block,),
        in_specs=[pl.BlockSpec(a.shape, lambda i: (0, 0)) for a in operands] + [columns] * 2,
        out_specs=[out] * count,
        out_shape=[shape] * count,
        scratch_shapes=[
            pltpu.VMEM((count * rows, width), jnp.bfloat16),
            pltpu.VMEM((count * rows, 128), jnp.float32),
        ],
        compiler_params=pltpu.CompilerParams(vmem_limit_bytes=VMEM_LIMIT),
        cost_estimate=pl.CostEstimate(
            flops=4 * count * rows * width * units,
            bytes_accessed=4 * width * units + 2 * count * rows * (width + units),
            transcendentals=count * rows * units,
        ),
    )(*operands, gate_weight, up_weight)


def part_kernel(width, final, *refs):
    chunk_ref, gate_ref, up_ref = refs[:3]
    tokens = chunk_ref[:, :width]
    gate_sum = jnp.dot(tokens, gate_ref[...], preferred_element_type=jnp.float32)
    up_sum = jnp.dot(tokens, up_ref[...], preferred_element_type=jnp.float32)
    if final:
        gate_part, up_part, scale_ref, out_ref = refs[3:]
        scale = scale_ref[:, :1]
        gate_sum = (gate_part[...] + gate_sum) * scale
        up_sum = (up_part[...] + up_sum) * scale
        out_ref[...] = (gate_sum / (1.0 + jnp.exp(-gate_sum)) * up_sum).astype(jnp.bfloat16)
    else:
        gate_part, up_part, scale_ref = refs[3:]
        gate_part[...] = gate_sum
        up_part[...] = up_sum
        both = chunk_ref[:, -SCALE_COLUMNS:].astype(jnp.float32)
        scale = both[:, :1] + both[:, SCALE_COLUMNS // 2 : SCALE_COLUMNS // 2 + 1]
        scale_ref[...] = jnp.broadcast_to(scale, scale_ref.shape)


def gated_part(chunk, array, gate_weight, up_weight, so_far):
    rows = array.shape[0]
    units = gate_weight.shape[1]
    block = 256
    before = sum(HEAD_CHUNKS[:chunk]) * GROUP_SPLIT * HEAD_SIZE
    width = HEAD_CHUNKS[chunk] * GROUP_SPLIT * HEAD_SIZE
    weights = pl.BlockSpec((pl.Element(width), pl.Element(block)), lambda i: (before, i * block))
    whole = pl.BlockSpec(array.shape, lambda i: (0, 0))
    part = pl.BlockSpec((rows, block), lambda i: (0, i))
    scale = pl.BlockSpec((rows, 128), lambda i: (0, 0))
    if so_far:
        out_specs, shapes = part, jax.ShapeDtypeStruct((rows, units), jnp.bfloat16)
    else:
        out_specs = [part, part, scale]
        shapes = [jax.ShapeDtypeStruct((rows, units), jnp.float32)] * 2
        shapes.append(jax.ShapeDtypeStruct((rows, 128), jnp.float32))
    return pl.pallas_call(
        functools.partial(part_kernel, width, bool(so_far)),
        grid=(units // block,),
        in_specs=[whole, weights, weights] + ([part, part, scale] if so_far else []),
        out_specs=out_specs,
        out_shape=shapes,
        compiler_params=pltpu.CompilerParams(vmem_limit_bytes=VMEM_LIMIT),
        cost_estimate=pl.CostEstimate(
            flops=4 * rows * width * units,
            bytes_accessed=4 * width * units + 2 * rows * width + 8 * rows * units,
            transcendentals=rows * units if so_far else 0,
        ),
    )(array, gate_weight, up_weight, *so_far)


def cache_kernel(page_ref, kv_ref, cache_ref, out_ref):
    for i in range(out_ref.shape[0]):
        page = page_ref[i]

        @pl.when(page >= 0)
        def _():
            first = pl.multiple_of(jnp.maximum(page, 0) * PAGE_TOKENS, PAGE_TOKENS)
            out_ref[i] = kv_ref[pl.ds(first, PAGE_TOKENS), :]

        @pl.when(page < 0)
        def _():
            out_ref[i] = cache_ref[i]


def write_cache(pages, kv, cache):
    return pl.pallas_call(
        cache_kernel,
        grid=(1,),
        in_specs=[
            pl.BlockSpec(memory_space=pltpu.SMEM),
            pl.BlockSpec(kv.shape, lambda i: (0, 0)),
            pl.BlockSpec(cache.shape, lambda i: (0, 0, 0)),
        ],
        out_specs=pl.BlockSpec(cache.shape, lambda i: (0, 0, 0)),
        out_shape=jax.ShapeDtypeStruct(cache.shape, cache.dtype),
        compiler_params=pltpu.CompilerParams(vmem_limit_bytes=VMEM_LIMIT),
        cost_estimate=pl.CostEstimate(flops=0, bytes_accessed=8 * cache.size, transcendentals=0),
    )(pages, kv, cache)


def on_device(
    queries,
    rotated_keys_values,
    prompt_window_index,
    residual,
    ffn_gain,
    gate_weight,
    up_weight,
    paged_cache,
    page_table,
):
    queries, residual, gate_weight, up_weight, paged_cache = [
        pltpu.with_memory_space_constraint(a, pltpu.HBM)
        for a in (queries, residual, gate_weight, up_weight, paged_cache)
    ]
    own_kv = pltpu.with_memory_space_constraint(rotated_keys_values, pltpu.HBM)
    rows, width = queries.shape
    tok_index = lax.axis_index("tok")
    tok_count = lax.axis_size("tok")
    grp_index = lax.axis_index("grp")
    grp_count = lax.axis_size("grp")
    line, column = grp_index // 2, grp_index % 2
    line_count = grp_count // 2
    ahead = ring_tables(line_count)
    units = gate_weight.shape[1]
    chunks = range(len(HEAD_CHUNKS))

    def after(array, *others):
        return lax.optimization_barrier((array, *others))[0]

    def swap(array, mask):
        return lax.ppermute(array, "tok", [(t, t ^ mask) for t in range(tok_count)])

    def send(array, steps, flip):
        pairs = []
        for z in range(line_count):
            for y in range(2):
                pairs.append((2 * z + y, 2 * ahead[steps][z] + (1 - y if flip else y)))
        return lax.ppermute(array, "grp", pairs)

    own_seg = jnp.broadcast_to(prompt_window_index[0].astype(jnp.float32)[:, None], (rows, rows))
    place = tok_index.astype(jnp.int32).reshape(1)
    gain = ffn_gain.reshape(1, width)
    packed = pack(own_kv, prompt_window_index)
    first_swaps = []
    for c in chunks:
        held = {0: packed[c]}
        mask = tok_count // 2
        while mask > 1:
            if c:
                held = {m: after(a, *first_swaps[0].values()) for m, a in held.items()}
            held.update({m ^ mask: swap(a, mask) for m, a in held.items()})
            mask //= 2
        first_swaps.append(held)
    scaled, parts, carried = [], [], None
    for c in chunks:
        held = first_swaps[c]
        if c:
            held = {m: after(a, scaled[-1]) if m else a for m, a in held.items()}
        if tok_count > 1:
            held.update({m ^ 1: swap(a, 1) for m, a in held.items()})
        keys_values = [held[m] for m in range(tok_count)]
        made = attend(c, queries, residual, gain, keys_values, place, own_seg, carried)
        if c == 0:
            bias = made[3]
        if c < len(HEAD_CHUNKS) - 1:
            carried = (made[2], bias)
        parts.append(made[0])
        scaled.append(made[1])
    attended = jnp.concatenate(parts, axis=1)

    late_kv, _ = lax.optimization_barrier((rotated_keys_values, scaled[-1]))
    group_kv = lax.all_gather(late_kv, "tok", axis=0, tiled=True)
    slot_count = paged_cache.shape[0]
    page_count = group_kv.shape[0] // PAGE_TOKENS
    targets = page_table[0, :page_count] - tok_index * slot_count
    onehot = targets[None, :] == jnp.arange(slot_count)[:, None]
    page = jnp.where(onehot, jnp.arange(page_count, dtype=jnp.int32)[None, :] + 1, 0)
    pages = jnp.max(page, axis=1) - 1
    written = write_cache(pages, group_kv, paged_cache)

    hidden = jnp.zeros((rows, grp_count * units), jnp.bfloat16)

    def put(hidden, block, steps, flip):
        source = sum(jnp.where(line == z, ahead[steps][z] * 2, 0) for z in range(line_count))
        source = source + (1 - column if flip else column)
        return lax.dynamic_update_slice_in_dim(hidden, block, source * units, 1)

    sent, arrived, waiting = [], [scaled], [(scaled, 0, False)]
    products, late = [], []
    for step in range(line_count):
        other, following = [], []
        for c in chunks:
            ready = arrived[-1][c]
            number = len(sent)
            behind = sent[0] if number == 1 else sent[number - 2][:1] if number > 1 else []
            if c == 0 and step > 1:
                behind = [*behind, products[step - 2]]
            if behind:
                ready = after(ready, *behind)
            pair = [send(ready, 0, True)]
            if step + 1 < line_count:
                pair.append(send(ready, 1, False))
                following.append(pair[1])
            other.append(pair[0])
            sent.append(pair)
        arrived.append(following)
        waiting.append((other, step, True))
        if following:
            waiting.append((following, step + 1, False))
        if step == line_count - 2:
            waiting[-1] = ([*following[:-1], after(following[-1], written)], step + 1, False)
        if step + 1 < line_count:
            blocks = gated([shard for shard, _, _ in waiting], gate_weight, up_weight)
        else:
            shares = gated_part(1, other[1], gate_weight, up_weight, ())
            blocks = [gated_part(0, other[0], gate_weight, up_weight, shares)]
        products.append(blocks[-1])
        late = [(after(block, blocks[-1]), steps, flip) for block, steps, flip in late]
        made = late + [(block, steps, flip) for block, (_, steps, flip) in zip(blocks, waiting)]
        late = []
        if 0 < step < line_count - 2:
            late = [entry for entry in made if entry[2]]
            made = [entry for entry in made if not entry[2]]
        for block, steps, flip in made:
            if steps or flip:
                block = send(block, (line_count - steps) % line_count, flip)
            hidden = put(hidden, block, steps, flip)
        waiting = []
    return (attended, hidden, written)


def solution(mesh):
    in_specs = (
        P(("grp", "tok"), None),
        P(("grp", "tok"), None),
        P("grp", "tok"),
        P(("grp", "tok"), None),
        P(),
        P(None, "grp"),
        P(None, "grp"),
        P(("grp", "tok"), None, None),
        P("grp", None),
    )
    out_specs = (P(("grp", "tok"), None), P(("grp", "tok"), None), P(("grp", "tok"), None, None))
    return jax.shard_map(
        on_device, mesh=mesh, in_specs=in_specs, out_specs=out_specs, check_vma=False
    )
```

```python
import functools
import math

import jax
import jax.numpy as jnp
from jax import lax
from jax.experimental import pallas as pl
from jax.experimental.pallas import tpu as pltpu
from jax.sharding import PartitionSpec as P

QUERY_HEADS = 40
KEY_VALUE_HEADS = 8
HEAD_SIZE = 128
PAGE_TOKENS = 16
GROUP_SPLIT = QUERY_HEADS // KEY_VALUE_HEADS
HEAD_CHUNKS = (3, 5)
SEG_ROWS = 16
SCALE_COLUMNS = 128
MASK_FILLER = -1e30
VMEM_LIMIT = 28 * 1024 * 1024


def ring_order(count):
    return [0] + list(range(1, count, 2)) + list(range((count - 1) // 2 * 2, 0, -2))


def ring_tables(count):
    order = ring_order(count)
    spot = {place: i for i, place in enumerate(order)}
    return [[order[(spot[z] + s) % count] for z in range(count)] for s in range(count)]


def pack_kernel(kv_ref, seg_ref, *out_refs):
    rows = kv_ref.shape[0]
    key_width = KEY_VALUE_HEADS * HEAD_SIZE
    first = 0
    for out_ref, heads in zip(out_refs, HEAD_CHUNKS):
        width = heads * HEAD_SIZE
        out_ref[:rows, :width] = kv_ref[:, first : first + width]
        out_ref[:rows, width:] = kv_ref[:, key_width + first : key_width + first + width]
        first += width
    ids = jnp.broadcast_to(seg_ref[...], (SEG_ROWS, rows)).astype(jnp.float32)
    tail = jnp.concatenate([ids] * (out_refs[0].shape[1] // rows), axis=1)
    out_refs[0][rows:, :] = tail.astype(jnp.bfloat16)


def pack(kv, seg):
    rows = kv.shape[0]
    shapes = [
        jax.ShapeDtypeStruct(
            (rows + (SEG_ROWS if i == 0 else 0), 2 * heads * HEAD_SIZE), jnp.bfloat16
        )
        for i, heads in enumerate(HEAD_CHUNKS)
    ]
    return pl.pallas_call(
        pack_kernel,
        out_shape=shapes,
        compiler_params=pltpu.CompilerParams(vmem_limit_bytes=VMEM_LIMIT),
        cost_estimate=pl.CostEstimate(flops=0, bytes_accessed=4 * kv.size, transcendentals=0),
    )(kv, seg)


def attend_kernel(chunk, shard_count, width_all, *refs):
    heads = HEAD_CHUNKS[chunk]
    first, last = chunk == 0, chunk == len(HEAD_CHUNKS) - 1
    refs = list(refs)
    q_ref, res_ref, gain_ref = refs[:3]
    kv_refs = refs[3 : 3 + shard_count]
    rest = refs[3 + shard_count :]
    rows = q_ref.shape[0]
    if first:
        place_ref, own_seg_ref = rest[:2]
        attended_ref, scaled_ref, square_ref, bias_ref = rest[2:]
        row = lax.broadcasted_iota(jnp.int32, (rows, rows), 0)
        col = lax.broadcasted_iota(jnp.int32, (rows, rows), 1)
        place = place_ref[0]
        for m in range(shard_count):
            ids = kv_refs[m][rows:, :rows].astype(jnp.float32)[:1]
            apart = ((place ^ m) - place) * rows
            live = (own_seg_ref[...] == ids) & (col + apart <= row)
            bias_ref[:, m * rows : (m + 1) * rows] = jnp.where(live, 0.0, MASK_FILLER)
        total = jnp.zeros((rows, 1), jnp.float32)
    else:
        bias_ref, square_in = rest[:2]
        attended_ref, scaled_ref = rest[2:4]
        square_ref = None if last else rest[4]
        total = square_in[:, :1]
    bias = bias_ref[...]
    bias = jnp.concatenate([bias] * GROUP_SPLIT, axis=0)
    for h in range(heads):
        keys = jnp.concatenate(
            [r[:rows, h * HEAD_SIZE : (h + 1) * HEAD_SIZE] for r in kv_refs], axis=0
        )
        values = jnp.concatenate(
            [r[:rows, (heads + h) * HEAD_SIZE : (heads + h + 1) * HEAD_SIZE] for r in kv_refs],
            axis=0,
        )
        base = h * GROUP_SPLIT * HEAD_SIZE
        query = jnp.concatenate(
            [q_ref[:, base + g * HEAD_SIZE : base + (g + 1) * HEAD_SIZE] for g in range(GROUP_SPLIT)],
            axis=0,
        )
        scores = lax.dot_general(
            query, keys, (((1,), (1,)), ((), ())), preferred_element_type=jnp.float32
        )
        scores = scores * (1.0 / math.sqrt(HEAD_SIZE)) + bias
        weights = jnp.exp(scores - jnp.max(scores, axis=1, keepdims=True))
        denominator = jnp.sum(weights, axis=1, keepdims=True)
        summed = jnp.dot(weights.astype(jnp.bfloat16), values, preferred_element_type=jnp.float32)
        attention = (summed / denominator).astype(jnp.bfloat16).astype(jnp.float32)
        for g in range(GROUP_SPLIT):
            columns = slice(base + g * HEAD_SIZE, base + (g + 1) * HEAD_SIZE)
            attended = res_ref[:, columns].astype(jnp.float32) + attention[g * rows : (g + 1) * rows]
            attended = attended.astype(jnp.bfloat16)
            attended_ref[:, columns] = attended
            widened = attended.astype(jnp.float32)
            scaled_ref[:, columns] = (widened * gain_ref[:, columns]).astype(jnp.bfloat16)
            total = total + jnp.sum(widened * widened, axis=1, keepdims=True)
    if last:
        scale = lax.rsqrt(total * (1.0 / width_all) + 1e-06)
        high = scale.astype(jnp.bfloat16)
        low = (scale - high.astype(jnp.float32)).astype(jnp.bfloat16)
        lane = lax.broadcasted_iota(jnp.int32, (rows, SCALE_COLUMNS), 1)
        both = jnp.where(
            lane < SCALE_COLUMNS // 2, high.astype(jnp.float32), low.astype(jnp.float32)
        )
        scaled_ref[:, heads * GROUP_SPLIT * HEAD_SIZE :] = both.astype(jnp.bfloat16)
    else:
        square_ref[...] = jnp.broadcast_to(total, square_ref.shape)


def attend(chunk, queries, residual, gain, kv_chunks, place, own_seg, carried):
    heads = HEAD_CHUNKS[chunk]
    rows, width_all = queries.shape
    first, last = chunk == 0, chunk == len(HEAD_CHUNKS) - 1
    width = heads * GROUP_SPLIT * HEAD_SIZE
    before = sum(HEAD_CHUNKS[:chunk]) * GROUP_SPLIT * HEAD_SIZE
    shard_count = len(kv_chunks)

    def whole(shape):
        return pl.BlockSpec(shape, lambda i: (0, 0))

    columns = pl.BlockSpec((pl.Element(rows), pl.Element(width)), lambda i: (0, before))
    gains = pl.BlockSpec((pl.Element(1), pl.Element(width)), lambda i: (0, before))
    in_specs = [columns, columns, gains]
    in_specs += [whole(a.shape) for a in kv_chunks]
    operands = [queries, residual, gain] + list(kv_chunks)
    sent = width + (SCALE_COLUMNS if last else 0)
    shapes = [
        jax.ShapeDtypeStruct((rows, width), jnp.bfloat16),
        jax.ShapeDtypeStruct((rows, sent), jnp.bfloat16),
    ]
    out_specs = [whole((rows, width)), whole((rows, sent))]
    square = jax.ShapeDtypeStruct((rows, 128), jnp.float32)
    bias = jax.ShapeDtypeStruct((rows, rows * shard_count), jnp.float32)
    if first:
        operands += [place, own_seg]
        in_specs += [pl.BlockSpec(memory_space=pltpu.SMEM), whole(own_seg.shape)]
        shapes += [square, bias]
        out_specs += [whole(square.shape), whole(bias.shape)]
    else:
        square_so_far, bias_array = carried
        operands += [bias_array, square_so_far]
        in_specs += [whole(bias.shape), whole(square.shape)]
        if not last:
            shapes += [square]
            out_specs += [whole(square.shape)]
    keys = rows * shard_count
    return pl.pallas_call(
        functools.partial(attend_kernel, chunk, shard_count, width_all),
        grid=(1,),
        in_specs=in_specs,
        out_specs=out_specs,
        out_shape=shapes,
        compiler_params=pltpu.CompilerParams(vmem_limit_bytes=VMEM_LIMIT),
        cost_estimate=pl.CostEstimate(
            flops=4 * rows * width * keys,
            bytes_accessed=8 * rows * width + 4 * keys * heads * HEAD_SIZE,
            transcendentals=rows * keys * heads * GROUP_SPLIT,
        ),
    )(*operands)


def gated_kernel(shard_count, chunk_count, *refs):
    shards = [refs[i * chunk_count : (i + 1) * chunk_count] for i in range(shard_count)]
    rest = refs[shard_count * chunk_count :]
    gate_ref, up_ref = rest[:2]
    out_refs = rest[2 : 2 + shard_count]
    rows_ref, scale_ref = rest[2 + shard_count :]
    rows = shards[0][0].shape[0]

    @pl.when(pl.program_id(0) == 0)
    def _():
        for i, chunks in enumerate(shards):
            span = slice(i * rows, (i + 1) * rows)
            first = 0
            for j, ref in enumerate(chunks):
                width = ref.shape[1] - (SCALE_COLUMNS if j == chunk_count - 1 else 0)
                rows_ref[span, first : first + width] = ref[:, :width]
                first += width
            both = chunks[-1][:, -SCALE_COLUMNS:].astype(jnp.float32)
            scale = both[:, :1] + both[:, SCALE_COLUMNS // 2 : SCALE_COLUMNS // 2 + 1]
            scale_ref[span, :] = jnp.broadcast_to(scale, (rows, 128))

    tokens = rows_ref[...]
    scale = scale_ref[:, :1]
    gate_sum = jnp.dot(tokens, gate_ref[...], preferred_element_type=jnp.float32) * scale
    up_sum = jnp.dot(tokens, up_ref[...], preferred_element_type=jnp.float32) * scale
    made = (gate_sum / (1.0 + jnp.exp(-gate_sum)) * up_sum).astype(jnp.bfloat16)
    for i in range(shard_count):
        out_refs[i][...] = made[i * rows : (i + 1) * rows]


def gated(shards, gate_weight, up_weight):
    rows = shards[0][0].shape[0]
    width, units = gate_weight.shape
    block = 256
    count = len(shards)
    operands = [a for shard in shards for a in shard]
    columns = pl.BlockSpec((width, block), lambda i: (0, i))
    out = pl.BlockSpec((rows, block), lambda i: (0, i))
    shape = jax.ShapeDtypeStruct((rows, units), jnp.bfloat16)
    return pl.pallas_call(
        functools.partial(gated_kernel, count, len(shards[0])),
        grid=(units // block,),
        in_specs=[pl.BlockSpec(a.shape, lambda i: (0, 0)) for a in operands] + [columns] * 2,
        out_specs=[out] * count,
        out_shape=[shape] * count,
        scratch_shapes=[
            pltpu.VMEM((count * rows, width), jnp.bfloat16),
            pltpu.VMEM((count * rows, 128), jnp.float32),
        ],
        compiler_params=pltpu.CompilerParams(vmem_limit_bytes=VMEM_LIMIT),
        cost_estimate=pl.CostEstimate(
            flops=4 * count * rows * width * units,
            bytes_accessed=4 * width * units + 2 * count * rows * (width + units),
            transcendentals=count * rows * units,
        ),
    )(*operands, gate_weight, up_weight)


def part_kernel(width, final, *refs):
    chunk_ref, gate_ref, up_ref = refs[:3]
    tokens = chunk_ref[:, :width]
    gate_sum = jnp.dot(tokens, gate_ref[...], preferred_element_type=jnp.float32)
    up_sum = jnp.dot(tokens, up_ref[...], preferred_element_type=jnp.float32)
    if final:
        gate_part, up_part, scale_ref, out_ref = refs[3:]
        scale = scale_ref[:, :1]
        gate_sum = (gate_part[...] + gate_sum) * scale
        up_sum = (up_part[...] + up_sum) * scale
        out_ref[...] = (gate_sum / (1.0 + jnp.exp(-gate_sum)) * up_sum).astype(jnp.bfloat16)
    else:
        gate_part, up_part, scale_ref = refs[3:]
        gate_part[...] = gate_sum
        up_part[...] = up_sum
        both = chunk_ref[:, -SCALE_COLUMNS:].astype(jnp.float32)
        scale = both[:, :1] + both[:, SCALE_COLUMNS // 2 : SCALE_COLUMNS // 2 + 1]
        scale_ref[...] = jnp.broadcast_to(scale, scale_ref.shape)


def gated_part(chunk, array, gate_weight, up_weight, so_far):
    rows = array.shape[0]
    units = gate_weight.shape[1]
    block = 256
    before = sum(HEAD_CHUNKS[:chunk]) * GROUP_SPLIT * HEAD_SIZE
    width = HEAD_CHUNKS[chunk] * GROUP_SPLIT * HEAD_SIZE
    weights = pl.BlockSpec((pl.Element(width), pl.Element(block)), lambda i: (before, i * block))
    whole = pl.BlockSpec(array.shape, lambda i: (0, 0))
    part = pl.BlockSpec((rows, block), lambda i: (0, i))
    scale = pl.BlockSpec((rows, 128), lambda i: (0, 0))
    if so_far:
        out_specs, shapes = part, jax.ShapeDtypeStruct((rows, units), jnp.bfloat16)
    else:
        out_specs = [part, part, scale]
        shapes = [jax.ShapeDtypeStruct((rows, units), jnp.float32)] * 2
        shapes.append(jax.ShapeDtypeStruct((rows, 128), jnp.float32))
    return pl.pallas_call(
        functools.partial(part_kernel, width, bool(so_far)),
        grid=(units // block,),
        in_specs=[whole, weights, weights] + ([part, part, scale] if so_far else []),
        out_specs=out_specs,
        out_shape=shapes,
        compiler_params=pltpu.CompilerParams(vmem_limit_bytes=VMEM_LIMIT),
        cost_estimate=pl.CostEstimate(
            flops=4 * rows * width * units,
            bytes_accessed=4 * width * units + 2 * rows * width + 8 * rows * units,
            transcendentals=rows * units if so_far else 0,
        ),
    )(array, gate_weight, up_weight, *so_far)


def cache_kernel(page_ref, kv_ref, cache_ref, out_ref):
    for i in range(out_ref.shape[0]):
        page = page_ref[i]

        @pl.when(page >= 0)
        def _():
            first = pl.multiple_of(jnp.maximum(page, 0) * PAGE_TOKENS, PAGE_TOKENS)
            out_ref[i] = kv_ref[pl.ds(first, PAGE_TOKENS), :]

        @pl.when(page < 0)
        def _():
            out_ref[i] = cache_ref[i]


def write_cache(pages, kv, cache):
    return pl.pallas_call(
        cache_kernel,
        grid=(1,),
        in_specs=[
            pl.BlockSpec(memory_space=pltpu.SMEM),
            pl.BlockSpec(kv.shape, lambda i: (0, 0)),
            pl.BlockSpec(cache.shape, lambda i: (0, 0, 0)),
        ],
        out_specs=pl.BlockSpec(cache.shape, lambda i: (0, 0, 0)),
        out_shape=jax.ShapeDtypeStruct(cache.shape, cache.dtype),
        compiler_params=pltpu.CompilerParams(vmem_limit_bytes=VMEM_LIMIT),
        cost_estimate=pl.CostEstimate(flops=0, bytes_accessed=8 * cache.size, transcendentals=0),
    )(pages, kv, cache)


def on_device(
    queries,
    rotated_keys_values,
    prompt_window_index,
    residual,
    ffn_gain,
    gate_weight,
    up_weight,
    paged_cache,
    page_table,
):
    queries, residual, gate_weight, up_weight, paged_cache = [
        pltpu.with_memory_space_constraint(a, pltpu.HBM)
        for a in (queries, residual, gate_weight, up_weight, paged_cache)
    ]
    own_kv = pltpu.with_memory_space_constraint(rotated_keys_values, pltpu.HBM)
    rows, width = queries.shape
    tok_index = lax.axis_index("tok")
    tok_count = lax.axis_size("tok")
    grp_index = lax.axis_index("grp")
    grp_count = lax.axis_size("grp")
    line, column = grp_index // 2, grp_index % 2
    line_count = grp_count // 2
    ahead = ring_tables(line_count)
    units = gate_weight.shape[1]
    chunks = range(len(HEAD_CHUNKS))

    def after(array, *others):
        return lax.optimization_barrier((array, *others))[0]

    def swap(array, mask):
        return lax.ppermute(array, "tok", [(t, t ^ mask) for t in range(tok_count)])

    def send(array, steps, flip):
        pairs = []
        for z in range(line_count):
            for y in range(2):
                pairs.append((2 * z + y, 2 * ahead[steps][z] + (1 - y if flip else y)))
        return lax.ppermute(array, "grp", pairs)

    own_seg = jnp.broadcast_to(prompt_window_index[0].astype(jnp.float32)[:, None], (rows, rows))
    place = tok_index.astype(jnp.int32).reshape(1)
    gain = ffn_gain.reshape(1, width)
    packed = pack(own_kv, prompt_window_index)
    first_swaps = []
    for c in chunks:
        held = {0: packed[c]}
        mask = tok_count // 2
        while mask > 1:
            if c:
                held = {m: after(a, *first_swaps[0].values()) for m, a in held.items()}
            held.update({m ^ mask: swap(a, mask) for m, a in held.items()})
            mask //= 2
        first_swaps.append(held)
    scaled, parts, carried = [], [], None
    for c in chunks:
        held = first_swaps[c]
        if c:
            held = {m: after(a, scaled[-1]) if m else a for m, a in held.items()}
        if tok_count > 1:
            held.update({m ^ 1: swap(a, 1) for m, a in held.items()})
        keys_values = [held[m] for m in range(tok_count)]
        made = attend(c, queries, residual, gain, keys_values, place, own_seg, carried)
        if c == 0:
            bias = made[3]
        if c < len(HEAD_CHUNKS) - 1:
            carried = (made[2], bias)
        parts.append(made[0])
        scaled.append(made[1])
    attended = jnp.concatenate(parts, axis=1)

    late_kv, _ = lax.optimization_barrier((rotated_keys_values, scaled[-1]))
    group_kv = lax.all_gather(late_kv, "tok", axis=0, tiled=True)
    slot_count = paged_cache.shape[0]
    page_count = group_kv.shape[0] // PAGE_TOKENS
    targets = page_table[0, :page_count] - tok_index * slot_count
    onehot = targets[None, :] == jnp.arange(slot_count)[:, None]
    page = jnp.where(onehot, jnp.arange(page_count, dtype=jnp.int32)[None, :] + 1, 0)
    pages = jnp.max(page, axis=1) - 1
    written = write_cache(pages, group_kv, paged_cache)

    hidden = jnp.zeros((rows, grp_count * units), jnp.bfloat16)

    def put(hidden, block, steps, flip):
        source = sum(jnp.where(line == z, ahead[steps][z] * 2, 0) for z in range(line_count))
        source = source + (1 - column if flip else column)
        return lax.dynamic_update_slice_in_dim(hidden, block, source * units, 1)

    sent, arrived, waiting = [], [scaled], [(scaled, 0, False)]
    products, late = [], []
    for step in range(line_count):
        other, following = [], []
        for c in chunks:
            ready = arrived[-1][c]
            number = len(sent)
            behind = sent[0] if number == 1 else sent[number - 2][:1] if number > 1 else []
            if step > 2 or (c == 0 and step > 1):
                behind = [*behind, products[step - 2]]
            if behind:
                ready = after(ready, *behind)
            pair = [send(ready, 0, True)]
            if step + 1 < line_count:
                pair.append(send(ready, 1, False))
                following.append(pair[1])
            other.append(pair[0])
            sent.append(pair)
        arrived.append(following)
        waiting.append((other, step, True))
        if following:
            waiting.append((following, step + 1, False))
        if step == 1:
            waiting[-1] = ([*following[:-1], after(following[-1], written)], step + 1, False)
        if step + 1 < line_count:
            blocks = gated([shard for shard, _, _ in waiting], gate_weight, up_weight)
        else:
            shares = gated_part(1, other[1], gate_weight, up_weight, ())
            blocks = [gated_part(0, other[0], gate_weight, up_weight, shares)]
        products.append(blocks[-1])
        late = [(after(block, blocks[-1]), steps, flip) for block, steps, flip in late]
        made = late + [(block, steps, flip) for block, (_, steps, flip) in zip(blocks, waiting)]
        late = []
        if 0 < step < line_count - 2:
            late = [entry for entry in made if entry[2]]
            made = [entry for entry in made if not entry[2]]
        for block, steps, flip in made:
            if steps or flip:
                block = send(block, (line_count - steps) % line_count, flip)
            hidden = put(hidden, block, steps, flip)
        waiting = []
    return (attended, hidden, written)


def solution(mesh):
    in_specs = (
        P(("grp", "tok"), None),
        P(("grp", "tok"), None),
        P("grp", "tok"),
        P(("grp", "tok"), None),
        P(),
        P(None, "grp"),
        P(None, "grp"),
        P(("grp", "tok"), None, None),
        P("grp", None),
    )
    out_specs = (P(("grp", "tok"), None), P(("grp", "tok"), None), P(("grp", "tok"), None, None))
    return jax.shard_map(
        on_device, mesh=mesh, in_specs=in_specs, out_specs=out_specs, check_vma=False
    )
```

```python
import functools
import math

import jax
import jax.numpy as jnp
from jax import lax
from jax.experimental import pallas as pl
from jax.experimental.pallas import tpu as pltpu
from jax.sharding import PartitionSpec as P

QUERY_HEADS = 40
KEY_VALUE_HEADS = 8
HEAD_SIZE = 128
PAGE_TOKENS = 16
GROUP_SPLIT = QUERY_HEADS // KEY_VALUE_HEADS
HEAD_CHUNKS = (3, 5)
SEG_ROWS = 16
SCALE_COLUMNS = 128
MASK_FILLER = -1e30
VMEM_LIMIT = 28 * 1024 * 1024


def ring_order(count):
    return [0] + list(range(1, count, 2)) + list(range((count - 1) // 2 * 2, 0, -2))


def ring_tables(count):
    order = ring_order(count)
    spot = {place: i for i, place in enumerate(order)}
    return [[order[(spot[z] + s) % count] for z in range(count)] for s in range(count)]


def pack_kernel(kv_ref, seg_ref, *out_refs):
    rows = kv_ref.shape[0]
    key_width = KEY_VALUE_HEADS * HEAD_SIZE
    first = 0
    for out_ref, heads in zip(out_refs, HEAD_CHUNKS):
        width = heads * HEAD_SIZE
        out_ref[:rows, :width] = kv_ref[:, first : first + width]
        out_ref[:rows, width:] = kv_ref[:, key_width + first : key_width + first + width]
        first += width
    ids = jnp.broadcast_to(seg_ref[...], (SEG_ROWS, rows)).astype(jnp.float32)
    tail = jnp.concatenate([ids] * (out_refs[0].shape[1] // rows), axis=1)
    out_refs[0][rows:, :] = tail.astype(jnp.bfloat16)


def pack(kv, seg):
    rows = kv.shape[0]
    shapes = [
        jax.ShapeDtypeStruct(
            (rows + (SEG_ROWS if i == 0 else 0), 2 * heads * HEAD_SIZE), jnp.bfloat16
        )
        for i, heads in enumerate(HEAD_CHUNKS)
    ]
    return pl.pallas_call(
        pack_kernel,
        out_shape=shapes,
        compiler_params=pltpu.CompilerParams(vmem_limit_bytes=VMEM_LIMIT),
        cost_estimate=pl.CostEstimate(flops=0, bytes_accessed=4 * kv.size, transcendentals=0),
    )(kv, seg)


def attend_kernel(chunk, shard_count, width_all, *refs):
    heads = HEAD_CHUNKS[chunk]
    first, last = chunk == 0, chunk == len(HEAD_CHUNKS) - 1
    refs = list(refs)
    q_ref, res_ref, gain_ref = refs[:3]
    kv_refs = refs[3 : 3 + shard_count]
    rest = refs[3 + shard_count :]
    rows = q_ref.shape[0]
    if first:
        place_ref, own_seg_ref = rest[:2]
        attended_ref, scaled_ref, square_ref, bias_ref = rest[2:]
        row = lax.broadcasted_iota(jnp.int32, (rows, rows), 0)
        col = lax.broadcasted_iota(jnp.int32, (rows, rows), 1)
        place = place_ref[0]
        for m in range(shard_count):
            ids = kv_refs[m][rows:, :rows].astype(jnp.float32)[:1]
            apart = ((place ^ m) - place) * rows
            live = (own_seg_ref[...] == ids) & (col + apart <= row)
            bias_ref[:, m * rows : (m + 1) * rows] = jnp.where(live, 0.0, MASK_FILLER)
        total = jnp.zeros((rows, 1), jnp.float32)
    else:
        bias_ref, square_in = rest[:2]
        attended_ref, scaled_ref = rest[2:4]
        square_ref = None if last else rest[4]
        total = square_in[:, :1]
    bias = bias_ref[...]
    bias = jnp.concatenate([bias] * GROUP_SPLIT, axis=0)
    for h in range(heads):
        keys = jnp.concatenate(
            [r[:rows, h * HEAD_SIZE : (h + 1) * HEAD_SIZE] for r in kv_refs], axis=0
        )
        values = jnp.concatenate(
            [r[:rows, (heads + h) * HEAD_SIZE : (heads + h + 1) * HEAD_SIZE] for r in kv_refs],
            axis=0,
        )
        base = h * GROUP_SPLIT * HEAD_SIZE
        query = jnp.concatenate(
            [q_ref[:, base + g * HEAD_SIZE : base + (g + 1) * HEAD_SIZE] for g in range(GROUP_SPLIT)],
            axis=0,
        )
        scores = lax.dot_general(
            query, keys, (((1,), (1,)), ((), ())), preferred_element_type=jnp.float32
        )
        scores = scores * (1.0 / math.sqrt(HEAD_SIZE)) + bias
        weights = jnp.exp(scores - jnp.max(scores, axis=1, keepdims=True))
        denominator = jnp.sum(weights, axis=1, keepdims=True)
        summed = jnp.dot(weights.astype(jnp.bfloat16), values, preferred_element_type=jnp.float32)
        attention = (summed / denominator).astype(jnp.bfloat16).astype(jnp.float32)
        for g in range(GROUP_SPLIT):
            columns = slice(base + g * HEAD_SIZE, base + (g + 1) * HEAD_SIZE)
            attended = res_ref[:, columns].astype(jnp.float32) + attention[g * rows : (g + 1) * rows]
            attended = attended.astype(jnp.bfloat16)
            attended_ref[:, columns] = attended
            widened = attended.astype(jnp.float32)
            scaled_ref[:, columns] = (widened * gain_ref[:, columns]).astype(jnp.bfloat16)
            total = total + jnp.sum(widened * widened, axis=1, keepdims=True)
    if last:
        scale = lax.rsqrt(total * (1.0 / width_all) + 1e-06)
        high = scale.astype(jnp.bfloat16)
        low = (scale - high.astype(jnp.float32)).astype(jnp.bfloat16)
        lane = lax.broadcasted_iota(jnp.int32, (rows, SCALE_COLUMNS), 1)
        both = jnp.where(
            lane < SCALE_COLUMNS // 2, high.astype(jnp.float32), low.astype(jnp.float32)
        )
        scaled_ref[:, heads * GROUP_SPLIT * HEAD_SIZE :] = both.astype(jnp.bfloat16)
    else:
        square_ref[...] = jnp.broadcast_to(total, square_ref.shape)


def attend(chunk, queries, residual, gain, kv_chunks, place, own_seg, carried):
    heads = HEAD_CHUNKS[chunk]
    rows, width_all = queries.shape
    first, last = chunk == 0, chunk == len(HEAD_CHUNKS) - 1
    width = heads * GROUP_SPLIT * HEAD_SIZE
    before = sum(HEAD_CHUNKS[:chunk]) * GROUP_SPLIT * HEAD_SIZE
    shard_count = len(kv_chunks)

    def whole(shape):
        return pl.BlockSpec(shape, lambda i: (0, 0))

    columns = pl.BlockSpec((pl.Element(rows), pl.Element(width)), lambda i: (0, before))
    gains = pl.BlockSpec((pl.Element(1), pl.Element(width)), lambda i: (0, before))
    in_specs = [columns, columns, gains]
    in_specs += [whole(a.shape) for a in kv_chunks]
    operands = [queries, residual, gain] + list(kv_chunks)
    sent = width + (SCALE_COLUMNS if last else 0)
    shapes = [
        jax.ShapeDtypeStruct((rows, width), jnp.bfloat16),
        jax.ShapeDtypeStruct((rows, sent), jnp.bfloat16),
    ]
    out_specs = [whole((rows, width)), whole((rows, sent))]
    square = jax.ShapeDtypeStruct((rows, 128), jnp.float32)
    bias = jax.ShapeDtypeStruct((rows, rows * shard_count), jnp.float32)
    if first:
        operands += [place, own_seg]
        in_specs += [pl.BlockSpec(memory_space=pltpu.SMEM), whole(own_seg.shape)]
        shapes += [square, bias]
        out_specs += [whole(square.shape), whole(bias.shape)]
    else:
        square_so_far, bias_array = carried
        operands += [bias_array, square_so_far]
        in_specs += [whole(bias.shape), whole(square.shape)]
        if not last:
            shapes += [square]
            out_specs += [whole(square.shape)]
    keys = rows * shard_count
    return pl.pallas_call(
        functools.partial(attend_kernel, chunk, shard_count, width_all),
        grid=(1,),
        in_specs=in_specs,
        out_specs=out_specs,
        out_shape=shapes,
        compiler_params=pltpu.CompilerParams(vmem_limit_bytes=VMEM_LIMIT),
        cost_estimate=pl.CostEstimate(
            flops=4 * rows * width * keys,
            bytes_accessed=8 * rows * width + 4 * keys * heads * HEAD_SIZE,
            transcendentals=rows * keys * heads * GROUP_SPLIT,
        ),
    )(*operands)


def gated_kernel(shard_count, chunk_count, *refs):
    shards = [refs[i * chunk_count : (i + 1) * chunk_count] for i in range(shard_count)]
    rest = refs[shard_count * chunk_count :]
    gate_ref, up_ref = rest[:2]
    out_refs = rest[2 : 2 + shard_count]
    rows_ref, scale_ref = rest[2 + shard_count :]
    rows = shards[0][0].shape[0]

    @pl.when(pl.program_id(0) == 0)
    def _():
        for i, chunks in enumerate(shards):
            span = slice(i * rows, (i + 1) * rows)
            first = 0
            for j, ref in enumerate(chunks):
                width = ref.shape[1] - (SCALE_COLUMNS if j == chunk_count - 1 else 0)
                rows_ref[span, first : first + width] = ref[:, :width]
                first += width
            both = chunks[-1][:, -SCALE_COLUMNS:].astype(jnp.float32)
            scale = both[:, :1] + both[:, SCALE_COLUMNS // 2 : SCALE_COLUMNS // 2 + 1]
            scale_ref[span, :] = jnp.broadcast_to(scale, (rows, 128))

    tokens = rows_ref[...]
    scale = scale_ref[:, :1]
    gate_sum = jnp.dot(tokens, gate_ref[...], preferred_element_type=jnp.float32) * scale
    up_sum = jnp.dot(tokens, up_ref[...], preferred_element_type=jnp.float32) * scale
    made = (gate_sum / (1.0 + jnp.exp(-gate_sum)) * up_sum).astype(jnp.bfloat16)
    for i in range(shard_count):
        out_refs[i][...] = made[i * rows : (i + 1) * rows]


def gated(shards, gate_weight, up_weight):
    rows = shards[0][0].shape[0]
    width, units = gate_weight.shape
    block = 256
    count = len(shards)
    operands = [a for shard in shards for a in shard]
    columns = pl.BlockSpec((width, block), lambda i: (0, i))
    out = pl.BlockSpec((rows, block), lambda i: (0, i))
    shape = jax.ShapeDtypeStruct((rows, units), jnp.bfloat16)
    return pl.pallas_call(
        functools.partial(gated_kernel, count, len(shards[0])),
        grid=(units // block,),
        in_specs=[pl.BlockSpec(a.shape, lambda i: (0, 0)) for a in operands] + [columns] * 2,
        out_specs=[out] * count,
        out_shape=[shape] * count,
        scratch_shapes=[
            pltpu.VMEM((count * rows, width), jnp.bfloat16),
            pltpu.VMEM((count * rows, 128), jnp.float32),
        ],
        compiler_params=pltpu.CompilerParams(vmem_limit_bytes=VMEM_LIMIT),
        cost_estimate=pl.CostEstimate(
            flops=4 * count * rows * width * units,
            bytes_accessed=4 * width * units + 2 * count * rows * (width + units),
            transcendentals=count * rows * units,
        ),
    )(*operands, gate_weight, up_weight)


def part_kernel(width, final, *refs):
    chunk_ref, gate_ref, up_ref = refs[:3]
    tokens = chunk_ref[:, :width]
    gate_sum = jnp.dot(tokens, gate_ref[...], preferred_element_type=jnp.float32)
    up_sum = jnp.dot(tokens, up_ref[...], preferred_element_type=jnp.float32)
    if final:
        gate_part, up_part, out_ref = refs[3:]
        both = chunk_ref[:, -SCALE_COLUMNS:].astype(jnp.float32)
        scale = both[:, :1] + both[:, SCALE_COLUMNS // 2 : SCALE_COLUMNS // 2 + 1]
        gate_sum = (gate_part[...] + gate_sum) * scale
        up_sum = (up_part[...] + up_sum) * scale
        out_ref[...] = (gate_sum / (1.0 + jnp.exp(-gate_sum)) * up_sum).astype(jnp.bfloat16)
    else:
        gate_part, up_part = refs[3:]
        gate_part[...] = gate_sum
        up_part[...] = up_sum


def gated_part(chunk, array, gate_weight, up_weight, so_far):
    rows = array.shape[0]
    units = gate_weight.shape[1]
    block = 256
    before = sum(HEAD_CHUNKS[:chunk]) * GROUP_SPLIT * HEAD_SIZE
    width = HEAD_CHUNKS[chunk] * GROUP_SPLIT * HEAD_SIZE
    weights = pl.BlockSpec((pl.Element(width), pl.Element(block)), lambda i: (before, i * block))
    whole = pl.BlockSpec(array.shape, lambda i: (0, 0))
    part = pl.BlockSpec((rows, block), lambda i: (0, i))
    if so_far:
        out_specs, shapes = part, jax.ShapeDtypeStruct((rows, units), jnp.bfloat16)
    else:
        out_specs = [part, part]
        shapes = [jax.ShapeDtypeStruct((rows, units), jnp.float32)] * 2
    return pl.pallas_call(
        functools.partial(part_kernel, width, bool(so_far)),
        grid=(units // block,),
        in_specs=[whole, weights, weights] + ([part, part] if so_far else []),
        out_specs=out_specs,
        out_shape=shapes,
        compiler_params=pltpu.CompilerParams(vmem_limit_bytes=VMEM_LIMIT),
        cost_estimate=pl.CostEstimate(
            flops=4 * rows * width * units,
            bytes_accessed=4 * width * units + 2 * rows * width + 8 * rows * units,
            transcendentals=rows * units if so_far else 0,
        ),
    )(array, gate_weight, up_weight, *so_far)


def cache_kernel(page_ref, kv_ref, cache_ref, out_ref):
    for i in range(out_ref.shape[0]):
        page = page_ref[i]

        @pl.when(page >= 0)
        def _():
            first = pl.multiple_of(jnp.maximum(page, 0) * PAGE_TOKENS, PAGE_TOKENS)
            out_ref[i] = kv_ref[pl.ds(first, PAGE_TOKENS), :]

        @pl.when(page < 0)
        def _():
            out_ref[i] = cache_ref[i]


def write_cache(pages, kv, cache):
    return pl.pallas_call(
        cache_kernel,
        grid=(1,),
        in_specs=[
            pl.BlockSpec(memory_space=pltpu.SMEM),
            pl.BlockSpec(kv.shape, lambda i: (0, 0)),
            pl.BlockSpec(cache.shape, lambda i: (0, 0, 0)),
        ],
        out_specs=pl.BlockSpec(cache.shape, lambda i: (0, 0, 0)),
        out_shape=jax.ShapeDtypeStruct(cache.shape, cache.dtype),
        compiler_params=pltpu.CompilerParams(vmem_limit_bytes=VMEM_LIMIT),
        cost_estimate=pl.CostEstimate(flops=0, bytes_accessed=8 * cache.size, transcendentals=0),
    )(pages, kv, cache)


def on_device(
    queries,
    rotated_keys_values,
    prompt_window_index,
    residual,
    ffn_gain,
    gate_weight,
    up_weight,
    paged_cache,
    page_table,
):
    queries, residual, gate_weight, up_weight, paged_cache = [
        pltpu.with_memory_space_constraint(a, pltpu.HBM)
        for a in (queries, residual, gate_weight, up_weight, paged_cache)
    ]
    own_kv = pltpu.with_memory_space_constraint(rotated_keys_values, pltpu.HBM)
    rows, width = queries.shape
    tok_index = lax.axis_index("tok")
    tok_count = lax.axis_size("tok")
    grp_index = lax.axis_index("grp")
    grp_count = lax.axis_size("grp")
    line, column = grp_index // 2, grp_index % 2
    line_count = grp_count // 2
    ahead = ring_tables(line_count)
    units = gate_weight.shape[1]
    chunks = range(len(HEAD_CHUNKS))

    def after(array, *others):
        return lax.optimization_barrier((array, *others))[0]

    def swap(array, mask):
        return lax.ppermute(array, "tok", [(t, t ^ mask) for t in range(tok_count)])

    def send(array, steps, flip):
        pairs = []
        for z in range(line_count):
            for y in range(2):
                pairs.append((2 * z + y, 2 * ahead[steps][z] + (1 - y if flip else y)))
        return lax.ppermute(array, "grp", pairs)

    own_seg = jnp.broadcast_to(prompt_window_index[0].astype(jnp.float32)[:, None], (rows, rows))
    place = tok_index.astype(jnp.int32).reshape(1)
    gain = ffn_gain.reshape(1, width)
    packed = pack(own_kv, prompt_window_index)
    first_swaps = []
    for c in chunks:
        held = {0: packed[c]}
        mask = tok_count // 2
        while mask > 1:
            if c:
                held = {m: after(a, *first_swaps[0].values()) for m, a in held.items()}
            held.update({m ^ mask: swap(a, mask) for m, a in held.items()})
            mask //= 2
        first_swaps.append(held)
    scaled, parts, carried = [], [], None
    for c in chunks:
        held = first_swaps[c]
        if c:
            held = {m: after(a, scaled[-1]) if m else a for m, a in held.items()}
        if tok_count > 1:
            held.update({m ^ 1: swap(a, 1) for m, a in held.items()})
        keys_values = [held[m] for m in range(tok_count)]
        made = attend(c, queries, residual, gain, keys_values, place, own_seg, carried)
        if c == 0:
            bias = made[3]
        if c < len(HEAD_CHUNKS) - 1:
            carried = (made[2], bias)
        parts.append(made[0])
        scaled.append(made[1])
    attended = jnp.concatenate(parts, axis=1)

    late_kv, _ = lax.optimization_barrier((rotated_keys_values, scaled[-1]))
    group_kv = lax.all_gather(late_kv, "tok", axis=0, tiled=True)
    slot_count = paged_cache.shape[0]
    page_count = group_kv.shape[0] // PAGE_TOKENS
    targets = page_table[0, :page_count] - tok_index * slot_count
    onehot = targets[None, :] == jnp.arange(slot_count)[:, None]
    page = jnp.where(onehot, jnp.arange(page_count, dtype=jnp.int32)[None, :] + 1, 0)
    pages = jnp.max(page, axis=1) - 1
    written = write_cache(pages, group_kv, paged_cache)

    hidden = jnp.zeros((rows, grp_count * units), jnp.bfloat16)

    def put(hidden, block, steps, flip):
        source = sum(jnp.where(line == z, ahead[steps][z] * 2, 0) for z in range(line_count))
        source = source + (1 - column if flip else column)
        return lax.dynamic_update_slice_in_dim(hidden, block, source * units, 1)

    sent, arrived, waiting = [], [scaled], [(scaled, 0, False)]
    products, late = [], []
    for step in range(line_count):
        other, following = [], []
        for c in chunks:
            ready = arrived[-1][c]
            number = len(sent)
            behind = sent[number - 1] if c else sent[number - 2][:1] if step else []
            if c == 0 and step > 1:
                behind = [*behind, products[step - 2]]
            if behind:
                ready = after(ready, *behind)
            pair = [send(ready, 0, True)]
            if step + 1 < line_count:
                pair.append(send(ready, 1, False))
                following.append(pair[1])
            other.append(pair[0])
            sent.append(pair)
        arrived.append(following)
        waiting.append((other, step, True))
        if following:
            waiting.append((following, step + 1, False))
        if step == 1:
            waiting[-1] = ([*following[:-1], after(following[-1], written)], step + 1, False)
        if step + 1 < line_count:
            blocks = gated([shard for shard, _, _ in waiting], gate_weight, up_weight)
        else:
            shares = gated_part(0, other[0], gate_weight, up_weight, ())
            blocks = [gated_part(1, other[1], gate_weight, up_weight, shares)]
        products.append(blocks[-1])
        late = [(after(block, blocks[-1]), steps, flip) for block, steps, flip in late]
        made = late + [(block, steps, flip) for block, (_, steps, flip) in zip(blocks, waiting)]
        late = []
        if 0 < step < line_count - 2:
            late = [entry for entry in made if entry[2]]
            made = [entry for entry in made if not entry[2]]
        for block, steps, flip in made:
            if steps or flip:
                block = send(block, (line_count - steps) % line_count, flip)
            hidden = put(hidden, block, steps, flip)
        waiting = []
    return (attended, hidden, written)


def solution(mesh):
    in_specs = (
        P(("grp", "tok"), None),
        P(("grp", "tok"), None),
        P("grp", "tok"),
        P(("grp", "tok"), None),
        P(),
        P(None, "grp"),
        P(None, "grp"),
        P(("grp", "tok"), None, None),
        P("grp", None),
    )
    out_specs = (P(("grp", "tok"), None), P(("grp", "tok"), None), P(("grp", "tok"), None, None))
    return jax.shard_map(
        on_device, mesh=mesh, in_specs=in_specs, out_specs=out_specs, check_vma=False
    )
```

```python
import functools
import math

import jax
import jax.numpy as jnp
from jax import lax
from jax.experimental import pallas as pl
from jax.experimental.pallas import tpu as pltpu
from jax.sharding import PartitionSpec as P

QUERY_HEADS = 40
KEY_VALUE_HEADS = 8
HEAD_SIZE = 128
PAGE_TOKENS = 16
GROUP_SPLIT = QUERY_HEADS // KEY_VALUE_HEADS
HEAD_CHUNKS = (3, 5)
SEG_ROWS = 16
SCALE_COLUMNS = 128
MASK_FILLER = -1e30
VMEM_LIMIT = 28 * 1024 * 1024


def ring_order(count):
    return [0] + list(range(1, count, 2)) + list(range((count - 1) // 2 * 2, 0, -2))


def ring_tables(count):
    order = ring_order(count)
    spot = {place: i for i, place in enumerate(order)}
    return [[order[(spot[z] + s) % count] for z in range(count)] for s in range(count)]


def pack_kernel(kv_ref, seg_ref, *out_refs):
    rows = kv_ref.shape[0]
    key_width = KEY_VALUE_HEADS * HEAD_SIZE
    first = 0
    for out_ref, heads in zip(out_refs, HEAD_CHUNKS):
        width = heads * HEAD_SIZE
        out_ref[:rows, :width] = kv_ref[:, first : first + width]
        out_ref[:rows, width:] = kv_ref[:, key_width + first : key_width + first + width]
        first += width
    ids = jnp.broadcast_to(seg_ref[...], (SEG_ROWS, rows)).astype(jnp.float32)
    tail = jnp.concatenate([ids] * (out_refs[0].shape[1] // rows), axis=1)
    out_refs[0][rows:, :] = tail.astype(jnp.bfloat16)


def pack(kv, seg):
    rows = kv.shape[0]
    shapes = [
        jax.ShapeDtypeStruct(
            (rows + (SEG_ROWS if i == 0 else 0), 2 * heads * HEAD_SIZE), jnp.bfloat16
        )
        for i, heads in enumerate(HEAD_CHUNKS)
    ]
    return pl.pallas_call(
        pack_kernel,
        out_shape=shapes,
        compiler_params=pltpu.CompilerParams(vmem_limit_bytes=VMEM_LIMIT),
        cost_estimate=pl.CostEstimate(flops=0, bytes_accessed=4 * kv.size, transcendentals=0),
    )(kv, seg)


def attend_kernel(chunk, shard_count, width_all, *refs):
    heads = HEAD_CHUNKS[chunk]
    first, last = chunk == 0, chunk == len(HEAD_CHUNKS) - 1
    refs = list(refs)
    q_ref, res_ref, gain_ref = refs[:3]
    kv_refs = refs[3 : 3 + shard_count]
    rest = refs[3 + shard_count :]
    rows = q_ref.shape[0]
    if first:
        place_ref, own_seg_ref = rest[:2]
        attended_ref, scaled_ref, square_ref, bias_ref = rest[2:]
        row = lax.broadcasted_iota(jnp.int32, (rows, rows), 0)
        col = lax.broadcasted_iota(jnp.int32, (rows, rows), 1)
        place = place_ref[0]
        for m in range(shard_count):
            ids = kv_refs[m][rows:, :rows].astype(jnp.float32)[:1]
            apart = ((place ^ m) - place) * rows
            live = (own_seg_ref[...] == ids) & (col + apart <= row)
            bias_ref[:, m * rows : (m + 1) * rows] = jnp.where(live, 0.0, MASK_FILLER)
        total = jnp.zeros((rows, 1), jnp.float32)
    else:
        bias_ref, square_in = rest[:2]
        attended_ref, scaled_ref = rest[2:4]
        square_ref = None if last else rest[4]
        total = square_in[:, :1]
    bias = bias_ref[...]
    bias = jnp.concatenate([bias] * GROUP_SPLIT, axis=0)
    for h in range(heads):
        keys = jnp.concatenate(
            [r[:rows, h * HEAD_SIZE : (h + 1) * HEAD_SIZE] for r in kv_refs], axis=0
        )
        values = jnp.concatenate(
            [r[:rows, (heads + h) * HEAD_SIZE : (heads + h + 1) * HEAD_SIZE] for r in kv_refs],
            axis=0,
        )
        base = h * GROUP_SPLIT * HEAD_SIZE
        query = jnp.concatenate(
            [q_ref[:, base + g * HEAD_SIZE : base + (g + 1) * HEAD_SIZE] for g in range(GROUP_SPLIT)],
            axis=0,
        )
        scores = lax.dot_general(
            query, keys, (((1,), (1,)), ((), ())), preferred_element_type=jnp.float32
        )
        scores = scores * (1.0 / math.sqrt(HEAD_SIZE)) + bias
        weights = jnp.exp(scores - jnp.max(scores, axis=1, keepdims=True))
        denominator = jnp.sum(weights, axis=1, keepdims=True)
        summed = jnp.dot(weights.astype(jnp.bfloat16), values, preferred_element_type=jnp.float32)
        attention = (summed / denominator).astype(jnp.bfloat16).astype(jnp.float32)
        for g in range(GROUP_SPLIT):
            columns = slice(base + g * HEAD_SIZE, base + (g + 1) * HEAD_SIZE)
            attended = res_ref[:, columns].astype(jnp.float32) + attention[g * rows : (g + 1) * rows]
            attended = attended.astype(jnp.bfloat16)
            attended_ref[:, columns] = attended
            widened = attended.astype(jnp.float32)
            scaled_ref[:, columns] = (widened * gain_ref[:, columns]).astype(jnp.bfloat16)
            total = total + jnp.sum(widened * widened, axis=1, keepdims=True)
    if last:
        scale = lax.rsqrt(total * (1.0 / width_all) + 1e-06)
        high = scale.astype(jnp.bfloat16)
        low = (scale - high.astype(jnp.float32)).astype(jnp.bfloat16)
        lane = lax.broadcasted_iota(jnp.int32, (rows, SCALE_COLUMNS), 1)
        both = jnp.where(
            lane < SCALE_COLUMNS // 2, high.astype(jnp.float32), low.astype(jnp.float32)
        )
        scaled_ref[:, heads * GROUP_SPLIT * HEAD_SIZE :] = both.astype(jnp.bfloat16)
    else:
        square_ref[...] = jnp.broadcast_to(total, square_ref.shape)


def attend(chunk, queries, residual, gain, kv_chunks, place, own_seg, carried):
    heads = HEAD_CHUNKS[chunk]
    rows, width_all = queries.shape
    first, last = chunk == 0, chunk == len(HEAD_CHUNKS) - 1
    width = heads * GROUP_SPLIT * HEAD_SIZE
    before = sum(HEAD_CHUNKS[:chunk]) * GROUP_SPLIT * HEAD_SIZE
    shard_count = len(kv_chunks)

    def whole(shape):
        return pl.BlockSpec(shape, lambda i: (0, 0))

    columns = pl.BlockSpec((pl.Element(rows), pl.Element(width)), lambda i: (0, before))
    gains = pl.BlockSpec((pl.Element(1), pl.Element(width)), lambda i: (0, before))
    in_specs = [columns, columns, gains]
    in_specs += [whole(a.shape) for a in kv_chunks]
    operands = [queries, residual, gain] + list(kv_chunks)
    sent = width + (SCALE_COLUMNS if last else 0)
    shapes = [
        pltpu.HBM((rows, width), jnp.bfloat16),
        jax.ShapeDtypeStruct((rows, sent), jnp.bfloat16),
    ]
    out_specs = [whole((rows, width)), whole((rows, sent))]
    square = jax.ShapeDtypeStruct((rows, 128), jnp.float32)
    bias = jax.ShapeDtypeStruct((rows, rows * shard_count), jnp.float32)
    if first:
        operands += [place, own_seg]
        in_specs += [pl.BlockSpec(memory_space=pltpu.SMEM), whole(own_seg.shape)]
        shapes += [square, bias]
        out_specs += [whole(square.shape), whole(bias.shape)]
    else:
        square_so_far, bias_array = carried
        operands += [bias_array, square_so_far]
        in_specs += [whole(bias.shape), whole(square.shape)]
        if not last:
            shapes += [square]
            out_specs += [whole(square.shape)]
    keys = rows * shard_count
    return pl.pallas_call(
        functools.partial(attend_kernel, chunk, shard_count, width_all),
        grid=(1,),
        in_specs=in_specs,
        out_specs=out_specs,
        out_shape=shapes,
        compiler_params=pltpu.CompilerParams(vmem_limit_bytes=VMEM_LIMIT),
        cost_estimate=pl.CostEstimate(
            flops=4 * rows * width * keys,
            bytes_accessed=8 * rows * width + 4 * keys * heads * HEAD_SIZE,
            transcendentals=rows * keys * heads * GROUP_SPLIT,
        ),
    )(*operands)


def gated_kernel(shard_count, chunk_count, *refs):
    shards = [refs[i * chunk_count : (i + 1) * chunk_count] for i in range(shard_count)]
    rest = refs[shard_count * chunk_count :]
    gate_ref, up_ref = rest[:2]
    out_refs = rest[2 : 2 + shard_count]
    rows_ref, scale_ref = rest[2 + shard_count :]
    rows = shards[0][0].shape[0]

    @pl.when(pl.program_id(0) == 0)
    def _():
        for i, chunks in enumerate(shards):
            span = slice(i * rows, (i + 1) * rows)
            first = 0
            for j, ref in enumerate(chunks):
                width = ref.shape[1] - (SCALE_COLUMNS if j == chunk_count - 1 else 0)
                rows_ref[span, first : first + width] = ref[:, :width]
                first += width
            both = chunks[-1][:, -SCALE_COLUMNS:].astype(jnp.float32)
            scale = both[:, :1] + both[:, SCALE_COLUMNS // 2 : SCALE_COLUMNS // 2 + 1]
            scale_ref[span, :] = jnp.broadcast_to(scale, (rows, 128))

    tokens = rows_ref[...]
    scale = scale_ref[:, :1]
    gate_sum = jnp.dot(tokens, gate_ref[...], preferred_element_type=jnp.float32) * scale
    up_sum = jnp.dot(tokens, up_ref[...], preferred_element_type=jnp.float32) * scale
    made = (gate_sum / (1.0 + jnp.exp(-gate_sum)) * up_sum).astype(jnp.bfloat16)
    for i in range(shard_count):
        out_refs[i][...] = made[i * rows : (i + 1) * rows]


def gated(shards, gate_weight, up_weight):
    rows = shards[0][0].shape[0]
    width, units = gate_weight.shape
    block = 256
    count = len(shards)
    operands = [a for shard in shards for a in shard]
    columns = pl.BlockSpec((width, block), lambda i: (0, i))
    out = pl.BlockSpec((rows, block), lambda i: (0, i))
    shape = jax.ShapeDtypeStruct((rows, units), jnp.bfloat16)
    return pl.pallas_call(
        functools.partial(gated_kernel, count, len(shards[0])),
        grid=(units // block,),
        in_specs=[pl.BlockSpec(a.shape, lambda i: (0, 0)) for a in operands] + [columns] * 2,
        out_specs=[out] * count,
        out_shape=[shape] * count,
        scratch_shapes=[
            pltpu.VMEM((count * rows, width), jnp.bfloat16),
            pltpu.VMEM((count * rows, 128), jnp.float32),
        ],
        compiler_params=pltpu.CompilerParams(vmem_limit_bytes=VMEM_LIMIT),
        cost_estimate=pl.CostEstimate(
            flops=4 * count * rows * width * units,
            bytes_accessed=4 * width * units + 2 * count * rows * (width + units),
            transcendentals=count * rows * units,
        ),
    )(*operands, gate_weight, up_weight)


def part_kernel(width, final, *refs):
    chunk_ref, gate_ref, up_ref = refs[:3]
    tokens = chunk_ref[:, :width]
    gate_sum = jnp.dot(tokens, gate_ref[...], preferred_element_type=jnp.float32)
    up_sum = jnp.dot(tokens, up_ref[...], preferred_element_type=jnp.float32)
    if final:
        gate_part, up_part, scale_ref, out_ref = refs[3:]
        scale = scale_ref[:, :1]
        gate_sum = (gate_part[...] + gate_sum) * scale
        up_sum = (up_part[...] + up_sum) * scale
        out_ref[...] = (gate_sum / (1.0 + jnp.exp(-gate_sum)) * up_sum).astype(jnp.bfloat16)
    else:
        gate_part, up_part, scale_ref = refs[3:]
        gate_part[...] = gate_sum
        up_part[...] = up_sum
        both = chunk_ref[:, -SCALE_COLUMNS:].astype(jnp.float32)
        scale = both[:, :1] + both[:, SCALE_COLUMNS // 2 : SCALE_COLUMNS // 2 + 1]
        scale_ref[...] = jnp.broadcast_to(scale, scale_ref.shape)


def gated_part(chunk, array, gate_weight, up_weight, so_far):
    rows = array.shape[0]
    units = gate_weight.shape[1]
    block = 256
    before = sum(HEAD_CHUNKS[:chunk]) * GROUP_SPLIT * HEAD_SIZE
    width = HEAD_CHUNKS[chunk] * GROUP_SPLIT * HEAD_SIZE
    weights = pl.BlockSpec((pl.Element(width), pl.Element(block)), lambda i: (before, i * block))
    whole = pl.BlockSpec(array.shape, lambda i: (0, 0))
    part = pl.BlockSpec((rows, block), lambda i: (0, i))
    scale = pl.BlockSpec((rows, 128), lambda i: (0, 0))
    if so_far:
        out_specs, shapes = part, jax.ShapeDtypeStruct((rows, units), jnp.bfloat16)
    else:
        out_specs = [part, part, scale]
        shapes = [jax.ShapeDtypeStruct((rows, units), jnp.float32)] * 2
        shapes.append(jax.ShapeDtypeStruct((rows, 128), jnp.float32))
    return pl.pallas_call(
        functools.partial(part_kernel, width, bool(so_far)),
        grid=(units // block,),
        in_specs=[whole, weights, weights] + ([part, part, scale] if so_far else []),
        out_specs=out_specs,
        out_shape=shapes,
        compiler_params=pltpu.CompilerParams(vmem_limit_bytes=VMEM_LIMIT),
        cost_estimate=pl.CostEstimate(
            flops=4 * rows * width * units,
            bytes_accessed=4 * width * units + 2 * rows * width + 8 * rows * units,
            transcendentals=rows * units if so_far else 0,
        ),
    )(array, gate_weight, up_weight, *so_far)


def cache_kernel(page_ref, kv_ref, cache_ref, out_ref):
    for i in range(out_ref.shape[0]):
        page = page_ref[i]

        @pl.when(page >= 0)
        def _():
            first = pl.multiple_of(jnp.maximum(page, 0) * PAGE_TOKENS, PAGE_TOKENS)
            out_ref[i] = kv_ref[pl.ds(first, PAGE_TOKENS), :]

        @pl.when(page < 0)
        def _():
            out_ref[i] = cache_ref[i]


def write_cache(pages, kv, cache):
    return pl.pallas_call(
        cache_kernel,
        grid=(1,),
        in_specs=[
            pl.BlockSpec(memory_space=pltpu.SMEM),
            pl.BlockSpec(kv.shape, lambda i: (0, 0)),
            pl.BlockSpec(cache.shape, lambda i: (0, 0, 0)),
        ],
        out_specs=pl.BlockSpec(cache.shape, lambda i: (0, 0, 0)),
        out_shape=jax.ShapeDtypeStruct(cache.shape, cache.dtype),
        compiler_params=pltpu.CompilerParams(vmem_limit_bytes=VMEM_LIMIT),
        cost_estimate=pl.CostEstimate(flops=0, bytes_accessed=8 * cache.size, transcendentals=0),
    )(pages, kv, cache)


def on_device(
    queries,
    rotated_keys_values,
    prompt_window_index,
    residual,
    ffn_gain,
    gate_weight,
    up_weight,
    paged_cache,
    page_table,
):
    queries, residual, gate_weight, up_weight, paged_cache = [
        pltpu.with_memory_space_constraint(a, pltpu.HBM)
        for a in (queries, residual, gate_weight, up_weight, paged_cache)
    ]
    own_kv = pltpu.with_memory_space_constraint(rotated_keys_values, pltpu.HBM)
    own_ids = pltpu.with_memory_space_constraint(prompt_window_index, pltpu.HBM)
    rows, width = queries.shape
    tok_index = lax.axis_index("tok")
    tok_count = lax.axis_size("tok")
    grp_index = lax.axis_index("grp")
    grp_count = lax.axis_size("grp")
    line, column = grp_index // 2, grp_index % 2
    line_count = grp_count // 2
    ahead = ring_tables(line_count)
    units = gate_weight.shape[1]
    chunks = range(len(HEAD_CHUNKS))

    def after(array, *others):
        return lax.optimization_barrier((array, *others))[0]

    def swap(array, mask):
        return lax.ppermute(array, "tok", [(t, t ^ mask) for t in range(tok_count)])

    def send(array, steps, flip):
        pairs = []
        for z in range(line_count):
            for y in range(2):
                pairs.append((2 * z + y, 2 * ahead[steps][z] + (1 - y if flip else y)))
        return lax.ppermute(array, "grp", pairs)

    own_seg = jnp.broadcast_to(prompt_window_index[0].astype(jnp.float32)[:, None], (rows, rows))
    place = tok_index.astype(jnp.int32).reshape(1)
    gain = pltpu.with_memory_space_constraint(ffn_gain.reshape(1, width), pltpu.HBM)
    packed = pack(own_kv, own_ids)
    first_swaps = []
    for c in chunks:
        held = {0: packed[c]}
        mask = tok_count // 2
        while mask > 1:
            if c:
                held = {m: after(a, *first_swaps[0].values()) for m, a in held.items()}
            held.update({m ^ mask: swap(a, mask) for m, a in held.items()})
            mask //= 2
        first_swaps.append(held)
    scaled, parts, carried = [], [], None
    for c in chunks:
        held = first_swaps[c]
        if c:
            held = {m: after(a, scaled[-1]) if m else a for m, a in held.items()}
        if tok_count > 1:
            held.update({m ^ 1: swap(a, 1) for m, a in held.items()})
        keys_values = [held[m] for m in range(tok_count)]
        made = attend(c, queries, residual, gain, keys_values, place, own_seg, carried)
        if c == 0:
            bias = made[3]
        if c < len(HEAD_CHUNKS) - 1:
            carried = (made[2], bias)
        parts.append(made[0])
        scaled.append(made[1])
    attended = jnp.concatenate(parts, axis=1)

    late_kv, _ = lax.optimization_barrier((rotated_keys_values, scaled[-1]))
    group_kv = lax.all_gather(late_kv, "tok", axis=0, tiled=True)
    slot_count = paged_cache.shape[0]
    page_count = group_kv.shape[0] // PAGE_TOKENS
    targets = page_table[0, :page_count] - tok_index * slot_count
    onehot = targets[None, :] == jnp.arange(slot_count)[:, None]
    page = jnp.where(onehot, jnp.arange(page_count, dtype=jnp.int32)[None, :] + 1, 0)
    pages = jnp.max(page, axis=1) - 1
    written = write_cache(pages, group_kv, paged_cache)

    hidden = jnp.zeros((rows, grp_count * units), jnp.bfloat16)

    def put(hidden, block, steps, flip):
        source = sum(jnp.where(line == z, ahead[steps][z] * 2, 0) for z in range(line_count))
        source = source + (1 - column if flip else column)
        return lax.dynamic_update_slice_in_dim(hidden, block, source * units, 1)

    sent, arrived, waiting = [], [scaled], [(scaled, 0, False)]
    products, late = [], []
    for step in range(line_count):
        other, following = [], []
        for c in chunks:
            ready = arrived[-1][c]
            number = len(sent)
            behind = sent[0] if number == 1 else sent[number - 2][:1] if number > 1 else []
            if c == 0 and step > 1:
                behind = [*behind, products[step - 2]]
            if behind:
                ready = after(ready, *behind)
            pair = [send(ready, 0, True)]
            if step + 1 < line_count:
                pair.append(send(ready, 1, False))
                following.append(pair[1])
            other.append(pair[0])
            sent.append(pair)
        arrived.append(following)
        waiting.append((other, step, True))
        if following:
            waiting.append((following, step + 1, False))
        if step == 1:
            waiting[-1] = ([*following[:-1], after(following[-1], written)], step + 1, False)
        if step + 1 < line_count:
            blocks = gated([shard for shard, _, _ in waiting], gate_weight, up_weight)
        else:
            shares = gated_part(1, other[1], gate_weight, up_weight, ())
            blocks = [gated_part(0, other[0], gate_weight, up_weight, shares)]
        products.append(blocks[-1])
        late = [(after(block, blocks[-1]), steps, flip) for block, steps, flip in late]
        made = late + [(block, steps, flip) for block, (_, steps, flip) in zip(blocks, waiting)]
        late = []
        if 0 < step < line_count - 2:
            late = [entry for entry in made if entry[2]]
            made = [entry for entry in made if not entry[2]]
        for block, steps, flip in made:
            if steps or flip:
                block = send(block, (line_count - steps) % line_count, flip)
            hidden = put(hidden, block, steps, flip)
        waiting = []
    return (attended, hidden, written)


def solution(mesh):
    in_specs = (
        P(("grp", "tok"), None),
        P(("grp", "tok"), None),
        P("grp", "tok"),
        P(("grp", "tok"), None),
        P(),
        P(None, "grp"),
        P(None, "grp"),
        P(("grp", "tok"), None, None),
        P("grp", None),
    )
    out_specs = (P(("grp", "tok"), None), P(("grp", "tok"), None), P(("grp", "tok"), None, None))
    return jax.shard_map(
        on_device, mesh=mesh, in_specs=in_specs, out_specs=out_specs, check_vma=False
    )
```

```python
import functools
import math

import jax
import jax.numpy as jnp
from jax import lax
from jax.experimental import pallas as pl
from jax.experimental.pallas import tpu as pltpu
from jax.sharding import PartitionSpec as P

QUERY_HEADS = 40
KEY_VALUE_HEADS = 8
HEAD_SIZE = 128
PAGE_TOKENS = 16
GROUP_SPLIT = QUERY_HEADS // KEY_VALUE_HEADS
HEAD_CHUNKS = (2, 6)
SEG_ROWS = 16
SCALE_COLUMNS = 128
MASK_FILLER = -1e30
VMEM_LIMIT = 28 * 1024 * 1024


def ring_order(count):
    return [0] + list(range(1, count, 2)) + list(range((count - 1) // 2 * 2, 0, -2))


def ring_tables(count):
    order = ring_order(count)
    spot = {place: i for i, place in enumerate(order)}
    return [[order[(spot[z] + s) % count] for z in range(count)] for s in range(count)]


def pack_kernel(kv_ref, seg_ref, *out_refs):
    rows = kv_ref.shape[0]
    key_width = KEY_VALUE_HEADS * HEAD_SIZE
    first = 0
    for out_ref, heads in zip(out_refs, HEAD_CHUNKS):
        width = heads * HEAD_SIZE
        out_ref[:rows, :width] = kv_ref[:, first : first + width]
        out_ref[:rows, width:] = kv_ref[:, key_width + first : key_width + first + width]
        first += width
    ids = jnp.broadcast_to(seg_ref[...], (SEG_ROWS, rows)).astype(jnp.float32)
    tail = jnp.concatenate([ids] * (out_refs[0].shape[1] // rows), axis=1)
    out_refs[0][rows:, :] = tail.astype(jnp.bfloat16)


def pack(kv, seg):
    rows = kv.shape[0]
    shapes = [
        jax.ShapeDtypeStruct(
            (rows + (SEG_ROWS if i == 0 else 0), 2 * heads * HEAD_SIZE), jnp.bfloat16
        )
        for i, heads in enumerate(HEAD_CHUNKS)
    ]
    return pl.pallas_call(
        pack_kernel,
        out_shape=shapes,
        compiler_params=pltpu.CompilerParams(vmem_limit_bytes=VMEM_LIMIT),
        cost_estimate=pl.CostEstimate(flops=0, bytes_accessed=4 * kv.size, transcendentals=0),
    )(kv, seg)


def attend_kernel(chunk, shard_count, width_all, *refs):
    heads = HEAD_CHUNKS[chunk]
    first, last = chunk == 0, chunk == len(HEAD_CHUNKS) - 1
    refs = list(refs)
    q_ref, res_ref, gain_ref = refs[:3]
    kv_refs = refs[3 : 3 + shard_count]
    rest = refs[3 + shard_count :]
    rows = q_ref.shape[0]
    if first:
        place_ref, own_seg_ref = rest[:2]
        attended_ref, scaled_ref, square_ref, bias_ref = rest[2:]
        row = lax.broadcasted_iota(jnp.int32, (rows, rows), 0)
        col = lax.broadcasted_iota(jnp.int32, (rows, rows), 1)
        place = place_ref[0]
        for m in range(shard_count):
            ids = kv_refs[m][rows:, :rows].astype(jnp.float32)[:1]
            apart = ((place ^ m) - place) * rows
            live = (own_seg_ref[...] == ids) & (col + apart <= row)
            bias_ref[:, m * rows : (m + 1) * rows] = jnp.where(live, 0.0, MASK_FILLER)
        total = jnp.zeros((rows, 1), jnp.float32)
    else:
        bias_ref, square_in = rest[:2]
        attended_ref, scaled_ref = rest[2:4]
        square_ref = None if last else rest[4]
        total = square_in[:, :1]
    bias = bias_ref[...]
    bias = jnp.concatenate([bias] * GROUP_SPLIT, axis=0)
    for h in range(heads):
        keys = jnp.concatenate(
            [r[:rows, h * HEAD_SIZE : (h + 1) * HEAD_SIZE] for r in kv_refs], axis=0
        )
        values = jnp.concatenate(
            [r[:rows, (heads + h) * HEAD_SIZE : (heads + h + 1) * HEAD_SIZE] for r in kv_refs],
            axis=0,
        )
        base = h * GROUP_SPLIT * HEAD_SIZE
        query = jnp.concatenate(
            [q_ref[:, base + g * HEAD_SIZE : base + (g + 1) * HEAD_SIZE] for g in range(GROUP_SPLIT)],
            axis=0,
        )
        scores = lax.dot_general(
            query, keys, (((1,), (1,)), ((), ())), preferred_element_type=jnp.float32
        )
        scores = scores * (1.0 / math.sqrt(HEAD_SIZE)) + bias
        weights = jnp.exp(scores - jnp.max(scores, axis=1, keepdims=True))
        denominator = jnp.sum(weights, axis=1, keepdims=True)
        summed = jnp.dot(weights.astype(jnp.bfloat16), values, preferred_element_type=jnp.float32)
        attention = (summed / denominator).astype(jnp.bfloat16).astype(jnp.float32)
        for g in range(GROUP_SPLIT):
            columns = slice(base + g * HEAD_SIZE, base + (g + 1) * HEAD_SIZE)
            attended = res_ref[:, columns].astype(jnp.float32) + attention[g * rows : (g + 1) * rows]
            attended = attended.astype(jnp.bfloat16)
            attended_ref[:, columns] = attended
            widened = attended.astype(jnp.float32)
            scaled_ref[:, columns] = (widened * gain_ref[:, columns]).astype(jnp.bfloat16)
            total = total + jnp.sum(widened * widened, axis=1, keepdims=True)
    if last:
        scale = lax.rsqrt(total * (1.0 / width_all) + 1e-06)
        high = scale.astype(jnp.bfloat16)
        low = (scale - high.astype(jnp.float32)).astype(jnp.bfloat16)
        lane = lax.broadcasted_iota(jnp.int32, (rows, SCALE_COLUMNS), 1)
        both = jnp.where(
            lane < SCALE_COLUMNS // 2, high.astype(jnp.float32), low.astype(jnp.float32)
        )
        scaled_ref[:, heads * GROUP_SPLIT * HEAD_SIZE :] = both.astype(jnp.bfloat16)
    else:
        square_ref[...] = jnp.broadcast_to(total, square_ref.shape)


def attend(chunk, queries, residual, gain, kv_chunks, place, own_seg, carried):
    heads = HEAD_CHUNKS[chunk]
    rows, width_all = queries.shape
    first, last = chunk == 0, chunk == len(HEAD_CHUNKS) - 1
    width = heads * GROUP_SPLIT * HEAD_SIZE
    before = sum(HEAD_CHUNKS[:chunk]) * GROUP_SPLIT * HEAD_SIZE
    shard_count = len(kv_chunks)

    def whole(shape):
        return pl.BlockSpec(shape, lambda i: (0, 0))

    columns = pl.BlockSpec((pl.Element(rows), pl.Element(width)), lambda i: (0, before))
    gains = pl.BlockSpec((pl.Element(1), pl.Element(width)), lambda i: (0, before))
    in_specs = [columns, columns, gains]
    in_specs += [whole(a.shape) for a in kv_chunks]
    operands = [queries, residual, gain] + list(kv_chunks)
    sent = width + (SCALE_COLUMNS if last else 0)
    shapes = [
        pltpu.HBM((rows, width), jnp.bfloat16),
        jax.ShapeDtypeStruct((rows, sent), jnp.bfloat16),
    ]
    out_specs = [whole((rows, width)), whole((rows, sent))]
    square = jax.ShapeDtypeStruct((rows, 128), jnp.float32)
    bias = jax.ShapeDtypeStruct((rows, rows * shard_count), jnp.float32)
    if first:
        operands += [place, own_seg]
        in_specs += [pl.BlockSpec(memory_space=pltpu.SMEM), whole(own_seg.shape)]
        shapes += [square, bias]
        out_specs += [whole(square.shape), whole(bias.shape)]
    else:
        square_so_far, bias_array = carried
        operands += [bias_array, square_so_far]
        in_specs += [whole(bias.shape), whole(square.shape)]
        if not last:
            shapes += [square]
            out_specs += [whole(square.shape)]
    keys = rows * shard_count
    return pl.pallas_call(
        functools.partial(attend_kernel, chunk, shard_count, width_all),
        grid=(1,),
        in_specs=in_specs,
        out_specs=out_specs,
        out_shape=shapes,
        compiler_params=pltpu.CompilerParams(vmem_limit_bytes=VMEM_LIMIT),
        cost_estimate=pl.CostEstimate(
            flops=4 * rows * width * keys,
            bytes_accessed=8 * rows * width + 4 * keys * heads * HEAD_SIZE,
            transcendentals=rows * keys * heads * GROUP_SPLIT,
        ),
    )(*operands)


def gated_kernel(shard_count, chunk_count, *refs):
    shards = [refs[i * chunk_count : (i + 1) * chunk_count] for i in range(shard_count)]
    rest = refs[shard_count * chunk_count :]
    gate_ref, up_ref = rest[:2]
    out_refs = rest[2 : 2 + shard_count]
    rows_ref, scale_ref = rest[2 + shard_count :]
    rows = shards[0][0].shape[0]

    @pl.when(pl.program_id(0) == 0)
    def _():
        for i, chunks in enumerate(shards):
            span = slice(i * rows, (i + 1) * rows)
            first = 0
            for j, ref in enumerate(chunks):
                width = ref.shape[1] - (SCALE_COLUMNS if j == chunk_count - 1 else 0)
                rows_ref[span, first : first + width] = ref[:, :width]
                first += width
            both = chunks[-1][:, -SCALE_COLUMNS:].astype(jnp.float32)
            scale = both[:, :1] + both[:, SCALE_COLUMNS // 2 : SCALE_COLUMNS // 2 + 1]
            scale_ref[span, :] = jnp.broadcast_to(scale, (rows, 128))

    tokens = rows_ref[...]
    scale = scale_ref[:, :1]
    gate_sum = jnp.dot(tokens, gate_ref[...], preferred_element_type=jnp.float32) * scale
    up_sum = jnp.dot(tokens, up_ref[...], preferred_element_type=jnp.float32) * scale
    made = (gate_sum / (1.0 + jnp.exp(-gate_sum)) * up_sum).astype(jnp.bfloat16)
    for i in range(shard_count):
        out_refs[i][...] = made[i * rows : (i + 1) * rows]


def gated(shards, gate_weight, up_weight):
    rows = shards[0][0].shape[0]
    width, units = gate_weight.shape
    block = 256
    count = len(shards)
    operands = [a for shard in shards for a in shard]
    columns = pl.BlockSpec((width, block), lambda i: (0, i))
    out = pl.BlockSpec((rows, block), lambda i: (0, i))
    shape = jax.ShapeDtypeStruct((rows, units), jnp.bfloat16)
    return pl.pallas_call(
        functools.partial(gated_kernel, count, len(shards[0])),
        grid=(units // block,),
        in_specs=[pl.BlockSpec(a.shape, lambda i: (0, 0)) for a in operands] + [columns] * 2,
        out_specs=[out] * count,
        out_shape=[shape] * count,
        scratch_shapes=[
            pltpu.VMEM((count * rows, width), jnp.bfloat16),
            pltpu.VMEM((count * rows, 128), jnp.float32),
        ],
        compiler_params=pltpu.CompilerParams(vmem_limit_bytes=VMEM_LIMIT),
        cost_estimate=pl.CostEstimate(
            flops=4 * count * rows * width * units,
            bytes_accessed=4 * width * units + 2 * count * rows * (width + units),
            transcendentals=count * rows * units,
        ),
    )(*operands, gate_weight, up_weight)


def part_kernel(width, final, *refs):
    chunk_ref, gate_ref, up_ref = refs[:3]
    tokens = chunk_ref[:, :width]
    gate_sum = jnp.dot(tokens, gate_ref[...], preferred_element_type=jnp.float32)
    up_sum = jnp.dot(tokens, up_ref[...], preferred_element_type=jnp.float32)
    if final:
        gate_part, up_part, scale_ref, out_ref = refs[3:]
        scale = scale_ref[:, :1]
        gate_sum = (gate_part[...] + gate_sum) * scale
        up_sum = (up_part[...] + up_sum) * scale
        out_ref[...] = (gate_sum / (1.0 + jnp.exp(-gate_sum)) * up_sum).astype(jnp.bfloat16)
    else:
        gate_part, up_part, scale_ref = refs[3:]
        gate_part[...] = gate_sum
        up_part[...] = up_sum
        both = chunk_ref[:, -SCALE_COLUMNS:].astype(jnp.float32)
        scale = both[:, :1] + both[:, SCALE_COLUMNS // 2 : SCALE_COLUMNS // 2 + 1]
        scale_ref[...] = jnp.broadcast_to(scale, scale_ref.shape)


def gated_part(chunk, array, gate_weight, up_weight, so_far):
    rows = array.shape[0]
    units = gate_weight.shape[1]
    block = 256
    before = sum(HEAD_CHUNKS[:chunk]) * GROUP_SPLIT * HEAD_SIZE
    width = HEAD_CHUNKS[chunk] * GROUP_SPLIT * HEAD_SIZE
    weights = pl.BlockSpec((pl.Element(width), pl.Element(block)), lambda i: (before, i * block))
    whole = pl.BlockSpec(array.shape, lambda i: (0, 0))
    part = pl.BlockSpec((rows, block), lambda i: (0, i))
    scale = pl.BlockSpec((rows, 128), lambda i: (0, 0))
    if so_far:
        out_specs, shapes = part, jax.ShapeDtypeStruct((rows, units), jnp.bfloat16)
    else:
        out_specs = [part, part, scale]
        shapes = [jax.ShapeDtypeStruct((rows, units), jnp.float32)] * 2
        shapes.append(jax.ShapeDtypeStruct((rows, 128), jnp.float32))
    return pl.pallas_call(
        functools.partial(part_kernel, width, bool(so_far)),
        grid=(units // block,),
        in_specs=[whole, weights, weights] + ([part, part, scale] if so_far else []),
        out_specs=out_specs,
        out_shape=shapes,
        compiler_params=pltpu.CompilerParams(vmem_limit_bytes=VMEM_LIMIT),
        cost_estimate=pl.CostEstimate(
            flops=4 * rows * width * units,
            bytes_accessed=4 * width * units + 2 * rows * width + 8 * rows * units,
            transcendentals=rows * units if so_far else 0,
        ),
    )(array, gate_weight, up_weight, *so_far)


def cache_kernel(page_ref, kv_ref, cache_ref, out_ref):
    for i in range(out_ref.shape[0]):
        page = page_ref[i]

        @pl.when(page >= 0)
        def _():
            first = pl.multiple_of(jnp.maximum(page, 0) * PAGE_TOKENS, PAGE_TOKENS)
            out_ref[i] = kv_ref[pl.ds(first, PAGE_TOKENS), :]

        @pl.when(page < 0)
        def _():
            out_ref[i] = cache_ref[i]


def write_cache(pages, kv, cache):
    return pl.pallas_call(
        cache_kernel,
        grid=(1,),
        in_specs=[
            pl.BlockSpec(memory_space=pltpu.SMEM),
            pl.BlockSpec(kv.shape, lambda i: (0, 0)),
            pl.BlockSpec(cache.shape, lambda i: (0, 0, 0)),
        ],
        out_specs=pl.BlockSpec(cache.shape, lambda i: (0, 0, 0)),
        out_shape=jax.ShapeDtypeStruct(cache.shape, cache.dtype),
        compiler_params=pltpu.CompilerParams(vmem_limit_bytes=VMEM_LIMIT),
        cost_estimate=pl.CostEstimate(flops=0, bytes_accessed=8 * cache.size, transcendentals=0),
    )(pages, kv, cache)


def on_device(
    queries,
    rotated_keys_values,
    prompt_window_index,
    residual,
    ffn_gain,
    gate_weight,
    up_weight,
    paged_cache,
    page_table,
):
    queries, residual, gate_weight, up_weight, paged_cache = [
        pltpu.with_memory_space_constraint(a, pltpu.HBM)
        for a in (queries, residual, gate_weight, up_weight, paged_cache)
    ]
    own_kv = pltpu.with_memory_space_constraint(rotated_keys_values, pltpu.HBM)
    own_ids = pltpu.with_memory_space_constraint(prompt_window_index, pltpu.HBM)
    rows, width = queries.shape
    tok_index = lax.axis_index("tok")
    tok_count = lax.axis_size("tok")
    grp_index = lax.axis_index("grp")
    grp_count = lax.axis_size("grp")
    line, column = grp_index // 2, grp_index % 2
    line_count = grp_count // 2
    ahead = ring_tables(line_count)
    units = gate_weight.shape[1]
    chunks = range(len(HEAD_CHUNKS))

    def after(array, *others):
        return lax.optimization_barrier((array, *others))[0]

    def swap(array, mask):
        return lax.ppermute(array, "tok", [(t, t ^ mask) for t in range(tok_count)])

    def send(array, steps, flip):
        pairs = []
        for z in range(line_count):
            for y in range(2):
                pairs.append((2 * z + y, 2 * ahead[steps][z] + (1 - y if flip else y)))
        return lax.ppermute(array, "grp", pairs)

    own_seg = jnp.broadcast_to(prompt_window_index[0].astype(jnp.float32)[:, None], (rows, rows))
    place = tok_index.astype(jnp.int32).reshape(1)
    gain = pltpu.with_memory_space_constraint(ffn_gain.reshape(1, width), pltpu.HBM)
    packed = pack(own_kv, own_ids)
    first_swaps = []
    for c in chunks:
        held = {0: packed[c]}
        mask = tok_count // 2
        while mask > 1:
            if c:
                held = {m: after(a, *first_swaps[0].values()) for m, a in held.items()}
            held.update({m ^ mask: swap(a, mask) for m, a in held.items()})
            mask //= 2
        first_swaps.append(held)
    scaled, parts, carried = [], [], None
    for c in chunks:
        held = first_swaps[c]
        if c:
            held = {m: after(a, scaled[-1]) if m else a for m, a in held.items()}
        if tok_count > 1:
            held.update({m ^ 1: swap(a, 1) for m, a in held.items()})
        keys_values = [held[m] for m in range(tok_count)]
        made = attend(c, queries, residual, gain, keys_values, place, own_seg, carried)
        if c == 0:
            bias = made[3]
        if c < len(HEAD_CHUNKS) - 1:
            carried = (made[2], bias)
        parts.append(made[0])
        scaled.append(made[1])
    attended = jnp.concatenate(parts, axis=1)

    late_kv, _ = lax.optimization_barrier((rotated_keys_values, scaled[-1]))
    group_kv = lax.all_gather(late_kv, "tok", axis=0, tiled=True)
    slot_count = paged_cache.shape[0]
    page_count = group_kv.shape[0] // PAGE_TOKENS
    targets = page_table[0, :page_count] - tok_index * slot_count
    onehot = targets[None, :] == jnp.arange(slot_count)[:, None]
    page = jnp.where(onehot, jnp.arange(page_count, dtype=jnp.int32)[None, :] + 1, 0)
    pages = jnp.max(page, axis=1) - 1
    written = write_cache(pages, group_kv, paged_cache)

    hidden = jnp.zeros((rows, grp_count * units), jnp.bfloat16)

    def put(hidden, block, steps, flip):
        source = sum(jnp.where(line == z, ahead[steps][z] * 2, 0) for z in range(line_count))
        source = source + (1 - column if flip else column)
        return lax.dynamic_update_slice_in_dim(hidden, block, source * units, 1)

    sent, arrived, waiting = [], [scaled], [(scaled, 0, False)]
    products, late = [], []
    for step in range(line_count):
        other, following = [], []
        for c in chunks:
            ready = arrived[-1][c]
            number = len(sent)
            behind = sent[0] if number == 1 else sent[number - 2][:1] if number > 1 else []
            if c == 0 and step > 1:
                behind = [*behind, products[step - 2]]
            if behind:
                ready = after(ready, *behind)
            pair = [send(ready, 0, True)]
            if step + 1 < line_count:
                pair.append(send(ready, 1, False))
                following.append(pair[1])
            other.append(pair[0])
            sent.append(pair)
        arrived.append(following)
        waiting.append((other, step, True))
        if following:
            waiting.append((following, step + 1, False))
        if step == 1:
            waiting[-1] = ([*following[:-1], after(following[-1], written)], step + 1, False)
        if step + 1 < line_count:
            blocks = gated([shard for shard, _, _ in waiting], gate_weight, up_weight)
        else:
            shares = gated_part(1, other[1], gate_weight, up_weight, ())
            blocks = [gated_part(0, other[0], gate_weight, up_weight, shares)]
        products.append(blocks[-1])
        late = [(after(block, blocks[-1]), steps, flip) for block, steps, flip in late]
        made = late + [(block, steps, flip) for block, (_, steps, flip) in zip(blocks, waiting)]
        late = []
        if 0 < step < line_count - 2:
            late = [entry for entry in made if entry[2]]
            made = [entry for entry in made if not entry[2]]
        for block, steps, flip in made:
            if steps or flip:
                block = send(block, (line_count - steps) % line_count, flip)
            hidden = put(hidden, block, steps, flip)
        waiting = []
    return (attended, hidden, written)


def solution(mesh):
    in_specs = (
        P(("grp", "tok"), None),
        P(("grp", "tok"), None),
        P("grp", "tok"),
        P(("grp", "tok"), None),
        P(),
        P(None, "grp"),
        P(None, "grp"),
        P(("grp", "tok"), None, None),
        P("grp", None),
    )
    out_specs = (P(("grp", "tok"), None), P(("grp", "tok"), None), P(("grp", "tok"), None, None))
    return jax.shard_map(
        on_device, mesh=mesh, in_specs=in_specs, out_specs=out_specs, check_vma=False
    )
```

```python
import functools
import math

import jax
import jax.numpy as jnp
from jax import lax
from jax.experimental import pallas as pl
from jax.experimental.pallas import tpu as pltpu
from jax.sharding import PartitionSpec as P

QUERY_HEADS = 40
KEY_VALUE_HEADS = 8
HEAD_SIZE = 128
PAGE_TOKENS = 16
GROUP_SPLIT = QUERY_HEADS // KEY_VALUE_HEADS
HEAD_CHUNKS = (3, 5)
SEG_ROWS = 16
SCALE_COLUMNS = 128
MASK_FILLER = -1e30
VMEM_LIMIT = 28 * 1024 * 1024


def ring_order(count):
    return [0] + list(range(1, count, 2)) + list(range((count - 1) // 2 * 2, 0, -2))


def ring_tables(count):
    order = ring_order(count)
    spot = {place: i for i, place in enumerate(order)}
    return [[order[(spot[z] + s) % count] for z in range(count)] for s in range(count)]


def pack_kernel(kv_ref, seg_ref, *out_refs):
    rows = kv_ref.shape[0]
    key_width = KEY_VALUE_HEADS * HEAD_SIZE
    first = 0
    for out_ref, heads in zip(out_refs, HEAD_CHUNKS):
        width = heads * HEAD_SIZE
        out_ref[:rows, :width] = kv_ref[:, first : first + width]
        out_ref[:rows, width:] = kv_ref[:, key_width + first : key_width + first + width]
        first += width
    ids = jnp.broadcast_to(seg_ref[...], (SEG_ROWS, rows)).astype(jnp.float32)
    tail = jnp.concatenate([ids] * (out_refs[0].shape[1] // rows), axis=1)
    out_refs[0][rows:, :] = tail.astype(jnp.bfloat16)


def pack(kv, seg):
    rows = kv.shape[0]
    shapes = [
        jax.ShapeDtypeStruct(
            (rows + (SEG_ROWS if i == 0 else 0), 2 * heads * HEAD_SIZE), jnp.bfloat16
        )
        for i, heads in enumerate(HEAD_CHUNKS)
    ]
    return pl.pallas_call(
        pack_kernel,
        out_shape=shapes,
        compiler_params=pltpu.CompilerParams(vmem_limit_bytes=VMEM_LIMIT),
        cost_estimate=pl.CostEstimate(flops=0, bytes_accessed=4 * kv.size, transcendentals=0),
    )(kv, seg)


def attend_kernel(chunk, shard_count, width_all, *refs):
    heads = HEAD_CHUNKS[chunk]
    first, last = chunk == 0, chunk == len(HEAD_CHUNKS) - 1
    refs = list(refs)
    q_ref, res_ref, gain_ref = refs[:3]
    kv_refs = refs[3 : 3 + shard_count]
    rest = refs[3 + shard_count :]
    rows = q_ref.shape[0]
    if first:
        place_ref, own_seg_ref = rest[:2]
        attended_ref, scaled_ref, square_ref, bias_ref = rest[2:]
        row = lax.broadcasted_iota(jnp.int32, (rows, rows), 0)
        col = lax.broadcasted_iota(jnp.int32, (rows, rows), 1)
        place = place_ref[0]
        for m in range(shard_count):
            ids = kv_refs[m][rows:, :rows].astype(jnp.float32)[:1]
            apart = ((place ^ m) - place) * rows
            live = (own_seg_ref[...] == ids) & (col + apart <= row)
            bias_ref[:, m * rows : (m + 1) * rows] = jnp.where(live, 0.0, MASK_FILLER)
        total = jnp.zeros((rows, 1), jnp.float32)
    else:
        bias_ref, square_in = rest[:2]
        attended_ref, scaled_ref = rest[2:4]
        square_ref = None if last else rest[4]
        total = square_in[:, :1]
    bias = bias_ref[...]
    bias = jnp.concatenate([bias] * GROUP_SPLIT, axis=0)
    for h in range(heads):
        keys = jnp.concatenate(
            [r[:rows, h * HEAD_SIZE : (h + 1) * HEAD_SIZE] for r in kv_refs], axis=0
        )
        values = jnp.concatenate(
            [r[:rows, (heads + h) * HEAD_SIZE : (heads + h + 1) * HEAD_SIZE] for r in kv_refs],
            axis=0,
        )
        base = h * GROUP_SPLIT * HEAD_SIZE
        query = jnp.concatenate(
            [q_ref[:, base + g * HEAD_SIZE : base + (g + 1) * HEAD_SIZE] for g in range(GROUP_SPLIT)],
            axis=0,
        )
        scores = lax.dot_general(
            query, keys, (((1,), (1,)), ((), ())), preferred_element_type=jnp.float32
        )
        scores = scores * (1.0 / math.sqrt(HEAD_SIZE)) + bias
        weights = jnp.exp(scores - jnp.max(scores, axis=1, keepdims=True))
        denominator = jnp.sum(weights, axis=1, keepdims=True)
        summed = jnp.dot(weights.astype(jnp.bfloat16), values, preferred_element_type=jnp.float32)
        attention = (summed / denominator).astype(jnp.bfloat16).astype(jnp.float32)
        for g in range(GROUP_SPLIT):
            columns = slice(base + g * HEAD_SIZE, base + (g + 1) * HEAD_SIZE)
            attended = res_ref[:, columns].astype(jnp.float32) + attention[g * rows : (g + 1) * rows]
            attended = attended.astype(jnp.bfloat16)
            attended_ref[:, columns] = attended
            widened = attended.astype(jnp.float32)
            scaled_ref[:, columns] = (widened * gain_ref[:, columns]).astype(jnp.bfloat16)
            total = total + jnp.sum(widened * widened, axis=1, keepdims=True)
    if last:
        scale = lax.rsqrt(total * (1.0 / width_all) + 1e-06)
        high = scale.astype(jnp.bfloat16)
        low = (scale - high.astype(jnp.float32)).astype(jnp.bfloat16)
        lane = lax.broadcasted_iota(jnp.int32, (rows, SCALE_COLUMNS), 1)
        both = jnp.where(
            lane < SCALE_COLUMNS // 2, high.astype(jnp.float32), low.astype(jnp.float32)
        )
        scaled_ref[:, heads * GROUP_SPLIT * HEAD_SIZE :] = both.astype(jnp.bfloat16)
    else:
        square_ref[...] = jnp.broadcast_to(total, square_ref.shape)


def attend(chunk, queries, residual, gain, kv_chunks, place, own_seg, carried):
    heads = HEAD_CHUNKS[chunk]
    rows, width_all = queries.shape
    first, last = chunk == 0, chunk == len(HEAD_CHUNKS) - 1
    width = heads * GROUP_SPLIT * HEAD_SIZE
    before = sum(HEAD_CHUNKS[:chunk]) * GROUP_SPLIT * HEAD_SIZE
    shard_count = len(kv_chunks)

    def whole(shape):
        return pl.BlockSpec(shape, lambda i: (0, 0))

    columns = pl.BlockSpec((pl.Element(rows), pl.Element(width)), lambda i: (0, before))
    gains = pl.BlockSpec((pl.Element(1), pl.Element(width)), lambda i: (0, before))
    in_specs = [columns, columns, gains]
    in_specs += [whole(a.shape) for a in kv_chunks]
    operands = [queries, residual, gain] + list(kv_chunks)
    sent = width + (SCALE_COLUMNS if last else 0)
    shapes = [
        pltpu.HBM((rows, width), jnp.bfloat16),
        jax.ShapeDtypeStruct((rows, sent), jnp.bfloat16),
    ]
    out_specs = [whole((rows, width)), whole((rows, sent))]
    square = jax.ShapeDtypeStruct((rows, 128), jnp.float32)
    bias = jax.ShapeDtypeStruct((rows, rows * shard_count), jnp.float32)
    if first:
        operands += [place, own_seg]
        in_specs += [pl.BlockSpec(memory_space=pltpu.SMEM), whole(own_seg.shape)]
        shapes += [square, bias]
        out_specs += [whole(square.shape), whole(bias.shape)]
    else:
        square_so_far, bias_array = carried
        operands += [bias_array, square_so_far]
        in_specs += [whole(bias.shape), whole(square.shape)]
        if not last:
            shapes += [square]
            out_specs += [whole(square.shape)]
    keys = rows * shard_count
    return pl.pallas_call(
        functools.partial(attend_kernel, chunk, shard_count, width_all),
        grid=(1,),
        in_specs=in_specs,
        out_specs=out_specs,
        out_shape=shapes,
        compiler_params=pltpu.CompilerParams(vmem_limit_bytes=VMEM_LIMIT),
        cost_estimate=pl.CostEstimate(
            flops=4 * rows * width * keys,
            bytes_accessed=8 * rows * width + 4 * keys * heads * HEAD_SIZE,
            transcendentals=rows * keys * heads * GROUP_SPLIT,
        ),
    )(*operands)


def gated_kernel(shard_count, chunk_count, *refs):
    shards = [refs[i * chunk_count : (i + 1) * chunk_count] for i in range(shard_count)]
    rest = refs[shard_count * chunk_count :]
    gate_ref, up_ref = rest[:2]
    out_refs = rest[2 : 2 + shard_count]
    rows_ref, scale_ref = rest[2 + shard_count :]
    rows = shards[0][0].shape[0]

    @pl.when(pl.program_id(0) == 0)
    def _():
        for i, chunks in enumerate(shards):
            span = slice(i * rows, (i + 1) * rows)
            first = 0
            for j, ref in enumerate(chunks):
                width = ref.shape[1] - (SCALE_COLUMNS if j == chunk_count - 1 else 0)
                rows_ref[span, first : first + width] = ref[:, :width]
                first += width
            both = chunks[-1][:, -SCALE_COLUMNS:].astype(jnp.float32)
            scale = both[:, :1] + both[:, SCALE_COLUMNS // 2 : SCALE_COLUMNS // 2 + 1]
            scale_ref[span, :] = jnp.broadcast_to(scale, (rows, 128))

    tokens = rows_ref[...]
    scale = scale_ref[:, :1]
    gate_sum = jnp.dot(tokens, gate_ref[...], preferred_element_type=jnp.float32) * scale
    up_sum = jnp.dot(tokens, up_ref[...], preferred_element_type=jnp.float32) * scale
    made = (gate_sum / (1.0 + jnp.exp(-gate_sum)) * up_sum).astype(jnp.bfloat16)
    for i in range(shard_count):
        out_refs[i][...] = made[i * rows : (i + 1) * rows]


def gated(shards, gate_weight, up_weight):
    rows = shards[0][0].shape[0]
    width, units = gate_weight.shape
    block = 256
    count = len(shards)
    operands = [a for shard in shards for a in shard]
    columns = pl.BlockSpec((width, block), lambda i: (0, i))
    out = pl.BlockSpec((rows, block), lambda i: (0, i))
    shape = jax.ShapeDtypeStruct((rows, units), jnp.bfloat16)
    return pl.pallas_call(
        functools.partial(gated_kernel, count, len(shards[0])),
        grid=(units // block,),
        in_specs=[pl.BlockSpec(a.shape, lambda i: (0, 0)) for a in operands] + [columns] * 2,
        out_specs=[out] * count,
        out_shape=[shape] * count,
        scratch_shapes=[
            pltpu.VMEM((count * rows, width), jnp.bfloat16),
            pltpu.VMEM((count * rows, 128), jnp.float32),
        ],
        compiler_params=pltpu.CompilerParams(vmem_limit_bytes=VMEM_LIMIT),
        cost_estimate=pl.CostEstimate(
            flops=4 * count * rows * width * units,
            bytes_accessed=4 * width * units + 2 * count * rows * (width + units),
            transcendentals=count * rows * units,
        ),
    )(*operands, gate_weight, up_weight)


def part_kernel(width, final, *refs):
    chunk_ref, gate_ref, up_ref = refs[:3]
    tokens = chunk_ref[:, :width]
    gate_sum = jnp.dot(tokens, gate_ref[...], preferred_element_type=jnp.float32)
    up_sum = jnp.dot(tokens, up_ref[...], preferred_element_type=jnp.float32)
    if final:
        gate_part, up_part, scale_ref, out_ref = refs[3:]
        scale = scale_ref[:, :1]
        gate_sum = (gate_part[...] + gate_sum) * scale
        up_sum = (up_part[...] + up_sum) * scale
        out_ref[...] = (gate_sum / (1.0 + jnp.exp(-gate_sum)) * up_sum).astype(jnp.bfloat16)
    else:
        gate_part, up_part, scale_ref = refs[3:]
        gate_part[...] = gate_sum
        up_part[...] = up_sum
        both = chunk_ref[:, -SCALE_COLUMNS:].astype(jnp.float32)
        scale = both[:, :1] + both[:, SCALE_COLUMNS // 2 : SCALE_COLUMNS // 2 + 1]
        scale_ref[...] = jnp.broadcast_to(scale, scale_ref.shape)


def gated_part(chunk, array, gate_weight, up_weight, so_far):
    rows = array.shape[0]
    units = gate_weight.shape[1]
    block = 256
    before = sum(HEAD_CHUNKS[:chunk]) * GROUP_SPLIT * HEAD_SIZE
    width = HEAD_CHUNKS[chunk] * GROUP_SPLIT * HEAD_SIZE
    weights = pl.BlockSpec((pl.Element(width), pl.Element(block)), lambda i: (before, i * block))
    whole = pl.BlockSpec(array.shape, lambda i: (0, 0))
    part = pl.BlockSpec((rows, block), lambda i: (0, i))
    scale = pl.BlockSpec((rows, 128), lambda i: (0, 0))
    if so_far:
        out_specs, shapes = part, jax.ShapeDtypeStruct((rows, units), jnp.bfloat16)
    else:
        out_specs = [part, part, scale]
        shapes = [jax.ShapeDtypeStruct((rows, units), jnp.float32)] * 2
        shapes.append(jax.ShapeDtypeStruct((rows, 128), jnp.float32))
    return pl.pallas_call(
        functools.partial(part_kernel, width, bool(so_far)),
        grid=(units // block,),
        in_specs=[whole, weights, weights] + ([part, part, scale] if so_far else []),
        out_specs=out_specs,
        out_shape=shapes,
        compiler_params=pltpu.CompilerParams(vmem_limit_bytes=VMEM_LIMIT),
        cost_estimate=pl.CostEstimate(
            flops=4 * rows * width * units,
            bytes_accessed=4 * width * units + 2 * rows * width + 8 * rows * units,
            transcendentals=rows * units if so_far else 0,
        ),
    )(array, gate_weight, up_weight, *so_far)


def cache_kernel(page_ref, kv_ref, cache_ref, out_ref):
    for i in range(out_ref.shape[0]):
        page = page_ref[i]

        @pl.when(page >= 0)
        def _():
            first = pl.multiple_of(jnp.maximum(page, 0) * PAGE_TOKENS, PAGE_TOKENS)
            out_ref[i] = kv_ref[pl.ds(first, PAGE_TOKENS), :]

        @pl.when(page < 0)
        def _():
            out_ref[i] = cache_ref[i]


def write_cache(pages, kv, cache):
    return pl.pallas_call(
        cache_kernel,
        grid=(1,),
        in_specs=[
            pl.BlockSpec(memory_space=pltpu.SMEM),
            pl.BlockSpec(kv.shape, lambda i: (0, 0)),
            pl.BlockSpec(cache.shape, lambda i: (0, 0, 0)),
        ],
        out_specs=pl.BlockSpec(cache.shape, lambda i: (0, 0, 0)),
        out_shape=jax.ShapeDtypeStruct(cache.shape, cache.dtype),
        compiler_params=pltpu.CompilerParams(vmem_limit_bytes=VMEM_LIMIT),
        cost_estimate=pl.CostEstimate(flops=0, bytes_accessed=8 * cache.size, transcendentals=0),
    )(pages, kv, cache)


def on_device(
    queries,
    rotated_keys_values,
    prompt_window_index,
    residual,
    ffn_gain,
    gate_weight,
    up_weight,
    paged_cache,
    page_table,
):
    queries, residual, gate_weight, up_weight, paged_cache = [
        pltpu.with_memory_space_constraint(a, pltpu.HBM)
        for a in (queries, residual, gate_weight, up_weight, paged_cache)
    ]
    own_kv = pltpu.with_memory_space_constraint(rotated_keys_values, pltpu.HBM)
    own_ids = pltpu.with_memory_space_constraint(prompt_window_index, pltpu.HBM)
    rows, width = queries.shape
    tok_index = lax.axis_index("tok")
    tok_count = lax.axis_size("tok")
    grp_index = lax.axis_index("grp")
    grp_count = lax.axis_size("grp")
    line, column = grp_index // 2, grp_index % 2
    line_count = grp_count // 2
    ahead = ring_tables(line_count)
    units = gate_weight.shape[1]
    chunks = range(len(HEAD_CHUNKS))

    def after(array, *others):
        return lax.optimization_barrier((array, *others))[0]

    def swap(array, mask):
        return lax.ppermute(array, "tok", [(t, t ^ mask) for t in range(tok_count)])

    def send(array, steps, flip):
        pairs = []
        for z in range(line_count):
            for y in range(2):
                pairs.append((2 * z + y, 2 * ahead[steps][z] + (1 - y if flip else y)))
        return lax.ppermute(array, "grp", pairs)

    own_seg = jnp.broadcast_to(prompt_window_index[0].astype(jnp.float32)[:, None], (rows, rows))
    place = tok_index.astype(jnp.int32).reshape(1)
    gain = pltpu.with_memory_space_constraint(ffn_gain.reshape(1, width), pltpu.HBM)
    packed = pack(own_kv, own_ids)
    first_swaps = []
    for c in chunks:
        held = {0: packed[c]}
        mask = tok_count // 2
        while mask > 1:
            if c:
                held = {m: after(a, *first_swaps[0].values()) for m, a in held.items()}
            held.update({m ^ mask: swap(a, mask) for m, a in held.items()})
            mask //= 2
        first_swaps.append(held)
    scaled, parts, carried = [], [], None
    for c in chunks:
        held = first_swaps[c]
        if c:
            held = {m: after(a, scaled[-1]) if m else a for m, a in held.items()}
        if tok_count > 1:
            held.update({m ^ 1: swap(a, 1) for m, a in held.items()})
        keys_values = [held[m] for m in range(tok_count)]
        made = attend(c, queries, residual, gain, keys_values, place, own_seg, carried)
        if c == 0:
            bias = made[3]
        if c < len(HEAD_CHUNKS) - 1:
            carried = (made[2], bias)
        parts.append(made[0])
        scaled.append(made[1])
    attended = jnp.concatenate(parts, axis=1)

    late_kv, _ = lax.optimization_barrier((rotated_keys_values, scaled[-1]))
    group_kv = lax.all_gather(late_kv, "tok", axis=0, tiled=True)
    slot_count = paged_cache.shape[0]
    page_count = group_kv.shape[0] // PAGE_TOKENS
    targets = page_table[0, :page_count] - tok_index * slot_count
    onehot = targets[None, :] == jnp.arange(slot_count)[:, None]
    page = jnp.where(onehot, jnp.arange(page_count, dtype=jnp.int32)[None, :] + 1, 0)
    pages = jnp.max(page, axis=1) - 1
    written = write_cache(pages, group_kv, paged_cache)

    hidden = jnp.zeros((rows, grp_count * units), jnp.bfloat16)

    def put(hidden, block, steps, flip):
        source = sum(jnp.where(line == z, ahead[steps][z] * 2, 0) for z in range(line_count))
        source = source + (1 - column if flip else column)
        return lax.dynamic_update_slice_in_dim(hidden, block, source * units, 1)

    sent, arrived, waiting = [], [scaled], [(scaled, 0, False)]
    products, late = [], []
    for step in range(line_count):
        other, following = [], []
        for c in chunks:
            ready = arrived[-1][c]
            number = len(sent)
            behind = sent[0] if number == 1 else sent[number - 2][:1] if number > 1 else []
            if step > 1 and (c == 0 or step + 1 < line_count):
                behind = [*behind, products[step - 1 if c == 0 and step + 1 < line_count else step - 2]]
            if behind:
                ready = after(ready, *behind)
            pair = [send(ready, 0, True)]
            if step + 1 < line_count:
                pair.append(send(ready, 1, False))
                following.append(pair[1])
            other.append(pair[0])
            sent.append(pair)
        arrived.append(following)
        waiting.append((other, step, True))
        if following:
            waiting.append((following, step + 1, False))
        if step == 1:
            waiting[-1] = ([*following[:-1], after(following[-1], written)], step + 1, False)
        if step + 1 < line_count:
            blocks = gated([shard for shard, _, _ in waiting], gate_weight, up_weight)
        else:
            shares = gated_part(1, other[1], gate_weight, up_weight, ())
            blocks = [gated_part(0, other[0], gate_weight, up_weight, shares)]
        products.append(blocks[-1])
        late = [(after(block, blocks[-1]), steps, flip) for block, steps, flip in late]
        made = late + [(block, steps, flip) for block, (_, steps, flip) in zip(blocks, waiting)]
        late = []
        if 0 < step < line_count - 2:
            late = [entry for entry in made if entry[2]]
            made = [entry for entry in made if not entry[2]]
        for block, steps, flip in made:
            if steps or flip:
                block = send(block, (line_count - steps) % line_count, flip)
            hidden = put(hidden, block, steps, flip)
        waiting = []
    return (attended, hidden, written)


def solution(mesh):
    in_specs = (
        P(("grp", "tok"), None),
        P(("grp", "tok"), None),
        P("grp", "tok"),
        P(("grp", "tok"), None),
        P(),
        P(None, "grp"),
        P(None, "grp"),
        P(("grp", "tok"), None, None),
        P("grp", None),
    )
    out_specs = (P(("grp", "tok"), None), P(("grp", "tok"), None), P(("grp", "tok"), None, None))
    return jax.shard_map(
        on_device, mesh=mesh, in_specs=in_specs, out_specs=out_specs, check_vma=False
    )
```
